32 devices in a mesh: dp: 4 (over z), cp: 8 (over y, x, core).
Axes of the slice: x: 2, y: 2, z: 4, core: 2. Of those that a mesh axis runs over, the one named last changes fastest.
Arguments:
- inputs: bfloat16 [4, 2048, 2048], P('dp', 'cp'), may hold values from -6 to 6
- attn_gain: bfloat16 [2048], P(('dp', 'cp')), may hold values from 0.099609375 to 1.8984375
- w_query: bfloat16 [2048, 2048], P(('dp', 'cp')), may hold values from -0.125 to 0.125
- w_key: bfloat16 [2048, 1024], P(('dp', 'cp')), may hold values from -0.125 to 0.125
- w_value: bfloat16 [2048, 1024], P(('dp', 'cp')), may hold values from -0.125 to 0.125
- w_output: bfloat16 [2048, 2048], P(('dp', 'cp')), may hold values from -1 to 1
- ffn_gain: bfloat16 [2048], P(('dp', 'cp')), may hold values from 0.099609375 to 1.8984375
- w_gate: bfloat16 [2048, 8192], P(('dp', 'cp')), may hold values from -0.125 to 0.125
- w_up: bfloat16 [2048, 8192], P(('dp', 'cp')), may hold values from -0.125 to 0.125
- w_down: bfloat16 [8192, 2048], P(('dp', 'cp')), may hold values from -0.0625 to 0.0625
- cotangent: bfloat16 [4, 2048, 2048], P('dp', 'cp'), may hold values from -6 to 6
Outputs:
- output: float32 [4, 2048, 2048], P('dp', 'cp')
- grad_input: float32 [4, 2048, 2048], P('dp', 'cp')
- grad_attn_gain: float32 [2048], P(('dp', 'cp'))
- grad_query: float32 [2048, 2048], P(('dp', 'cp'))
- grad_key: float32 [2048, 1024], P(('dp', 'cp'))
- grad_value: float32 [2048, 1024], P(('dp', 'cp'))
- grad_output: float32 [2048, 2048], P(('dp', 'cp'))
- grad_ffn_gain: float32 [2048], P(('dp', 'cp'))
- grad_gate: float32 [2048, 8192], P(('dp', 'cp'))
- grad_up: float32 [2048, 8192], P(('dp', 'cp'))
- grad_down: float32 [8192, 2048], P(('dp', 'cp'))
The draws below stay inside these ranges and needn't reach their ends.
All inputs are finite; a program needn't handle non-finite values.
Results may differ from the reference program's by a relative error of at most 0.018.
Values may be sent and summed in bfloat16 or wider, within the bound.
No kernel may reach another device: no remote copies, remote signals or barrier semaphores. Data moves between devices by JAX's collectives and lax.ppermute only.
A program may use at most 512 MiB of HBM per device.

```python
import jax
import jax.numpy as jnp
from jax import lax

D = 2048
H = 16
KVH = 8
HD = 128
FF = 8192
SEQ_LEN = 2048
SEQS_ALL = 4


def levels(stream_key, dims, shards, low, largest):
    def one(axis_at, shards_of):
        draws = jax.random.uniform(jax.random.fold_in(jax.random.fold_in(stream_key, 6), axis_at), (shards_of,), jnp.float32, low / len(shards), largest / len(shards))
        return jnp.repeat(jnp.exp(draws), dims[axis_at] // shards_of).reshape((-1,) + (1,) * (len(dims) - axis_at - 1))

    level = one(*shards[0])
    for cut in shards[1:]:
        level = level * one(*cut)
    return level


def centred(rng, dims, width, bound, shards=(), kind=jnp.bfloat16):
    array = width * jax.random.normal(rng, dims, jnp.float32)
    if shards:
        array = array * levels(rng, dims, shards, -0.22, 0.18)
    return jnp.clip(array, -bound, bound).astype(kind)


def setup_inputs(seed: int = 0) -> dict:
    arg_keys = jax.random.split(jax.random.key(seed), 12)
    inputs = centred(arg_keys[0], (SEQS_ALL, SEQ_LEN, D), 1.0, 6.0, ((0, 4), (1, 8)))
    attn_gain = jnp.clip(1.0 + 0.18 * jax.random.normal(arg_keys[1], (D,), jnp.float32), 0.099609375, 1.8984375).astype(jnp.bfloat16)
    w_query = centred(arg_keys[2], (D, H * HD), D ** -0.5, 0.125, ((0, 32),))
    w_key = centred(arg_keys[3], (D, KVH * HD), D ** -0.5, 0.125, ((0, 32),))
    w_value = centred(arg_keys[4], (D, KVH * HD), D ** -0.5, 0.125, ((0, 32),))
    w_output = centred(arg_keys[5], (H * HD, D), (max(H * HD // 64, 1)) ** -0.5, 1.0, ((0, 32),))
    ffn_gain = jnp.clip(1.0 + 0.18 * jax.random.normal(arg_keys[6], (D,), jnp.float32), 0.099609375, 1.8984375).astype(jnp.bfloat16)
    w_gate = centred(arg_keys[7], (D, FF), D ** -0.5, 0.125, ((0, 32),))
    w_up = centred(arg_keys[8], (D, FF), D ** -0.5, 0.125, ((0, 32),))
    w_down = centred(arg_keys[9], (FF, D), FF ** -0.5, 0.0625, ((0, 32),))
    cotangent = centred(arg_keys[10], (SEQS_ALL, SEQ_LEN, D), 1.0, 6.0, ((0, 4), (1, 8)))
    return {"inputs": inputs, "attn_gain": attn_gain, "w_query": w_query, "w_key": w_key, "w_value": w_value, "w_output": w_output, "ffn_gain": ffn_gain, "w_gate": w_gate, "w_up": w_up, "w_down": w_down, "cotangent": cotangent}


EPS = 1e-05
THETA = 1000000.0

@jax.custom_vjp
def low(v):
    return lax.optimization_barrier(v.astype(jnp.bfloat16)).astype(jnp.float32)

@jax.custom_vjp
def low_back(v):
    return v

def low_keep(v):
    return (low(v), None)

def low_pass(kept, grad):
    return (grad,)

def back_keep(v):
    return (v, None)

def back_low(kept, grad):
    return (low(grad),)
low.defvjp(low_keep, low_pass)
low_back.defvjp(back_keep, back_low)

def precise(left, right):
    return jnp.dot(left, right, precision=lax.Precision.HIGHEST)

def rotary_tables(length):
    half_dim = HD // 2
    inv_freq = THETA ** (-(jnp.arange(half_dim, dtype=jnp.float32) * 2.0 / HD))
    angles = jnp.arange(length, dtype=jnp.float32)[:, None] * inv_freq[None, :]
    cos_table = jnp.cos(angles)
    sin_table = jnp.sin(angles)
    return (jnp.concatenate([cos_table, cos_table], -1), jnp.concatenate([sin_table, sin_table], -1))

def rotate(heads, cos_table, sin_table):
    half_dim = HD // 2
    rotated = jnp.concatenate([-heads[..., half_dim:], heads[..., :half_dim]], -1)
    return heads * cos_table[:, None, :] + rotated * sin_table[:, None, :]

def attention(query_heads, key_heads, value_heads):
    length = query_heads.shape[0]
    groups = H // KVH
    block_rows = min(512, length)
    softmax_scale = HD ** (-0.5)
    query_blocks = query_heads.reshape(length // block_rows, block_rows, KVH, groups, HD)
    block_starts = jnp.arange(length // block_rows, dtype=jnp.int32) * block_rows
    key_pos = jnp.arange(length, dtype=jnp.int32)

    def one_block(query_rows, first_row):
        raw_scores = low_back(jnp.einsum('qkgd,lkd->kgql', query_rows, key_heads, precision=lax.Precision.HIGHEST))
        scores = raw_scores * softmax_scale
        query_pos = first_row + jnp.arange(block_rows, dtype=jnp.int32)
        causal = key_pos[None, :] <= query_pos[:, None]
        scores = jnp.where(causal, scores, -1e+30)
        row_max = lax.optimization_barrier(jnp.max(scores, -1, keepdims=True))
        exp_scores = jnp.exp(scores - row_max)
        attn_probs = exp_scores / lax.optimization_barrier(jnp.sum(exp_scores, -1, keepdims=True))
        mixed = jnp.einsum('kgql,lkd->qkgd', low(attn_probs), value_heads, precision=lax.Precision.HIGHEST)
        return mixed.reshape(block_rows, H * HD)
    checked = jax.checkpoint(one_block)
    blocks = lax.map(lambda block_pair: checked(block_pair[0], block_pair[1]), (query_blocks, block_starts))
    return blocks.reshape(length, H * HD)

def layer(seq_input, attn_gain, w_query, w_key, w_value, w_output, ffn_gain, w_gate, w_up, w_down):
    length = seq_input.shape[0]
    rms_one = lax.rsqrt(lax.optimization_barrier(jnp.mean(seq_input * seq_input, -1, keepdims=True)) + EPS)
    normed_one = low(seq_input * rms_one * attn_gain)
    cos_table, sin_table = rotary_tables(length)
    query_pre = low_back(precise(normed_one, w_query)).reshape(length, H, HD)
    key_pre = low_back(precise(normed_one, w_key)).reshape(length, KVH, HD)
    value_heads = low(low_back(precise(normed_one, w_value))).reshape(length, KVH, HD)
    query_heads = low(rotate(query_pre, cos_table, sin_table))
    key_heads = low(rotate(key_pre, cos_table, sin_table))
    attn_out = low(low_back(attention(query_heads, key_heads, value_heads)))
    hidden_res = seq_input + low_back(precise(attn_out, w_output))
    rms_two = lax.rsqrt(lax.optimization_barrier(jnp.mean(hidden_res * hidden_res, -1, keepdims=True)) + EPS)
    normed_two = low(hidden_res * rms_two * ffn_gain)
    gate_pre = low_back(precise(normed_two, w_gate))
    up_pre = low_back(precise(normed_two, w_up))
    hidden_act = low(jax.nn.silu(gate_pre) * up_pre)
    return hidden_res + low_back(precise(hidden_act, w_down))

def reference(inputs, attn_gain, w_query, w_key, w_value, w_output, ffn_gain, w_gate, w_up, w_down, cotangent):
    params = tuple((item.astype(jnp.float32) for item in (attn_gain, w_query, w_key, w_value, w_output, ffn_gain, w_gate, w_up, w_down)))
    seq_inputs = inputs.astype(jnp.float32)
    seq_cotans = cotangent.astype(jnp.float32)

    def seq_step(totals, seq_items):
        seq_input, seq_cotan = seq_items
        result, pullback = jax.vjp(layer, seq_input, *params)
        gradients = pullback(seq_cotan)
        totals = tuple((total + grad_part for total, grad_part in zip(totals, gradients[1:])))
        return (totals, (result, gradients[0]))
    zero_grads = tuple((jnp.zeros_like(item) for item in params))
    totals, (outputs, input_grads) = lax.scan(seq_step, zero_grads, (seq_inputs, seq_cotans))
    return (outputs, input_grads, totals[0], totals[1], totals[2], totals[3], totals[4], totals[5], totals[6], totals[7], totals[8])
```

```python
import functools
import math

import jax
import jax.numpy as jnp
from jax import lax
from jax.experimental import pallas as pl
from jax.experimental.pallas import tpu as pltpu
from jax.sharding import PartitionSpec as P

H = 16
KVH = 8
HD = 128
EPS = 1e-05
THETA = 1000000.0
SCALE = HD ** (-0.5)
LOG2E = math.log2(math.e)
BF = jnp.bfloat16
F32 = jnp.float32
VMEM_LIMIT = 56 * 1024 * 1024

NN = (((1,), (0,)), ((), ()))
NT = (((1,), (1,)), ((), ()))
TN = (((0,), (0,)), ((), ()))


def mm(left, right, dims):
    return lax.dot_general(left, right, dims, preferred_element_type=F32)


def offset_of(position, count):
    half = count // 2
    return ((position % half) << 1) | (position // half)


def position_of(offset, count):
    return (offset >> 1) + (offset & 1) * (count // 2)


def swap(value, count, offset):
    return lax.ppermute(value, "cp", [(i, i ^ offset) for i in range(count)])


def gather_parts(part, count):
    half = part.shape[0] // 2
    if count == 8:
        by_x = swap(part, count, 2)
        by_y = swap(part, count, 4)
        inner = [part, by_x, by_y, swap(by_y[:half], count, 2), swap(by_x[half:], count, 4)]
    else:
        inner, bit = [part], 2
        while bit < count:
            inner = inner + [swap(item, count, bit) for item in inner]
            bit *= 2
    outer = [swap(item, count, 1) for item in inner]
    return inner + outer


def gather_rows(part, count):
    return jnp.concatenate(gather_parts(part, count), 0)


def scatter_rows(partial, count):
    total_rows, _ = partial.shape
    middle = total_rows // 2
    rows = total_rows // count
    half = rows // 2

    def plus(left, right):
        return (left.astype(F32) + right.astype(F32)).astype(BF)

    acc = plus(partial[:middle], swap(partial[middle:], count, 1))
    parts = [acc[i * rows : (i + 1) * rows] for i in range(count // 2)]
    if count == 8:
        own, to_x, to_y, far = parts
        from_x = swap(far[:half], count, 2)
        from_y = swap(far[half:], count, 4)
        send_x = jnp.concatenate([to_x[:half], plus(to_x[half:], from_y)], 0)
        send_y = jnp.concatenate([plus(to_y[:half], from_x), to_y[half:]], 0)
        got_x = swap(send_x, count, 2)
        got_y = swap(send_y, count, 4)
        return own.astype(F32) + got_x.astype(F32) + got_y.astype(F32)
    bit = count // 2
    while bit >= 2:
        keep, give = parts[: len(parts) // 2], parts[len(parts) // 2 :]
        parts = [plus(a, swap(b, count, bit)) for a, b in zip(keep, give)]
        bit //= 2
    return parts[0].astype(F32)


def trade(parts, count):
    return [
        part if offset_of(p, count) == 0 else swap(part, count, offset_of(p, count))
        for p, part in enumerate(parts)
    ]


def params(semantics):
    return pltpu.CompilerParams(dimension_semantics=semantics, vmem_limit_bytes=VMEM_LIMIT)


def cost(flops, nbytes, trans=0):
    return pl.CostEstimate(flops=int(flops), bytes_accessed=int(nbytes), transcendentals=int(trans))


def turn(value, cos, sin):
    return value * cos + pltpu.roll(value, HD // 2, 1) * sin


def qkv_kernel(z_ref, w_ref, cos_ref, sin_ref, q_ref, k_ref, v_ref, kt_ref, vt_ref, *, heads):
    cos, sin = cos_ref[...], sin_ref[...]
    flat = mm(z_ref[...], w_ref[...], NN)
    for h in range(heads):
        at = slice(h * HD, (h + 1) * HD)
        q_ref[:, at] = turn(flat[:, at], cos, sin).astype(BF)
    key = turn(flat[:, heads * HD : (heads + 1) * HD], cos, sin)
    value = flat[:, (heads + 1) * HD :]
    k_ref[...] = key.astype(BF)
    v_ref[...] = value.astype(BF)
    kt_ref[...] = key.T.astype(BF)
    vt_ref[...] = value.T.astype(BF)


def qkv_call(z_one, w_qkv, cos, sin, rows, heads):
    total, width = z_one.shape
    cols = w_qkv.shape[1]
    row = lambda i: (i, 0)
    col = lambda i: (0, i)
    whole = lambda i: (0, 0)
    return pl.pallas_call(
        functools.partial(qkv_kernel, heads=heads),
        grid=(total // rows,),
        in_specs=[
            pl.BlockSpec((rows, width), row),
            pl.BlockSpec((width, cols), whole),
            pl.BlockSpec((rows, HD), row),
            pl.BlockSpec((rows, HD), row),
        ],
        out_specs=[
            pl.BlockSpec((rows, heads * HD), row),
            pl.BlockSpec((rows, HD), row),
            pl.BlockSpec((rows, HD), row),
            pl.BlockSpec((HD, rows), col),
            pl.BlockSpec((HD, rows), col),
        ],
        out_shape=[
            jax.ShapeDtypeStruct((total, heads * HD), BF),
            jax.ShapeDtypeStruct((total, HD), BF),
            jax.ShapeDtypeStruct((total, HD), BF),
            jax.ShapeDtypeStruct((HD, total), BF),
            jax.ShapeDtypeStruct((HD, total), BF),
        ],
        compiler_params=params(("arbitrary",)),
        cost_estimate=cost(2 * total * width * cols, 2 * (total * width + width * cols)),
        name="qkv",
    )(z_one, w_qkv, cos, sin)


def stack_heads(block, heads):
    if heads == 1:
        return block
    return jnp.concatenate([block[:, h * HD : (h + 1) * HD] for h in range(heads)], 0)


def diagonal_mask(rows, heads):
    key_at = lax.broadcasted_iota(jnp.int32, (rows, rows), 0)
    query_at = lax.broadcasted_iota(jnp.int32, (rows, rows), 1)
    one = key_at <= query_at
    return one if heads == 1 else jnp.concatenate([one] * heads, 1)


def attend_kernel(me_ref, q_ref, k_ref, vt_ref, o_ref, lse_ref, *, heads, rows, count):
    i = pl.program_id(0)
    me = me_ref[0]
    wide = heads * rows
    queries = stack_heads(q_ref[...], heads)

    def step(j, carry, masked):
        top, total, acc = carry
        at = pl.multiple_of(position_of(j ^ me, count) * rows, rows)
        s = mm(k_ref[pl.ds(at, rows), :], queries, NT) * (SCALE * LOG2E)
        if masked:
            s = jnp.where(diagonal_mask(rows, heads), s, -1e30)
        new_top = jnp.maximum(top, jnp.max(s, 0, keepdims=True))
        fade = jnp.exp2(top - new_top)
        p = jnp.exp2(s - new_top)
        total = total * fade + jnp.sum(p, 0, keepdims=True)
        acc = acc * fade + mm(vt_ref[:, pl.ds(at, rows)], p.astype(BF), NN)
        return new_top, total, acc

    carry = (
        jnp.full((1, wide), -1e30, F32),
        jnp.zeros((1, wide), F32),
        jnp.zeros((HD, wide), F32),
    )
    carry = step(i, carry, True)
    top, total, acc = lax.fori_loop(0, i, lambda j, c: step(j, c, False), carry)
    out = (acc / total).T
    for h in range(heads):
        o_ref[:, h * HD : (h + 1) * HD] = out[h * rows : (h + 1) * rows, :].astype(BF)
    lse_ref[0] = top + jnp.log2(total)


def attend_call(me, q, k, vt, rows, heads, count):
    total = q.shape[0]
    slot = lambda i, me_ref: (position_of(i ^ me_ref[0], count), 0)
    slot3 = lambda i, me_ref: (position_of(i ^ me_ref[0], count), 0, 0)
    whole = lambda i, me_ref: (0, 0)
    return pl.pallas_call(
        functools.partial(attend_kernel, heads=heads, rows=rows, count=count),
        grid_spec=pltpu.PrefetchScalarGridSpec(
            num_scalar_prefetch=1,
            grid=(count,),
            in_specs=[
                pl.BlockSpec((rows, heads * HD), slot),
                pl.BlockSpec((total, HD), whole),
                pl.BlockSpec((HD, total), whole),
            ],
            out_specs=[
                pl.BlockSpec((rows, heads * HD), slot),
                pl.BlockSpec((1, 1, heads * rows), slot3),
            ],
        ),
        out_shape=[
            jax.ShapeDtypeStruct((total, heads * HD), BF),
            jax.ShapeDtypeStruct((count, 1, heads * rows), F32),
        ],
        compiler_params=params(("arbitrary",)),
        cost_estimate=cost(4 * total * total * heads * HD, 8 * total * HD, heads * total * total // 2),
        name="attend",
    )(me, q, k, vt)


def attend_back_kernel(
    me_ref,
    q_ref,
    g_ref,
    o_ref,
    lse_ref,
    k_ref,
    kt_ref,
    v_ref,
    cos_ref,
    sin_ref,
    out_ref,
    dk_ref,
    dv_ref,
    *,
    heads,
    rows,
    count,
):
    i = pl.program_id(0)
    me = me_ref[0]
    wide = heads * rows

    @pl.when(i == 0)
    def _():
        dk_ref[...] = jnp.zeros_like(dk_ref)
        dv_ref[...] = jnp.zeros_like(dv_ref)

    queries = stack_heads(q_ref[...], heads)
    grads = stack_heads(g_ref[...], heads)
    outs = stack_heads(o_ref[...], heads)
    lse = lse_ref[0]
    mixed = jnp.sum((outs.astype(F32) * grads.astype(F32)).T, 0, keepdims=True)

    def step(j, dqt, masked):
        at = pl.multiple_of(position_of(j ^ me, count) * rows, rows)
        here = pl.ds(at, rows)
        s = mm(k_ref[here, :], queries, NT) * (SCALE * LOG2E)
        p = jnp.exp2(s - lse)
        if masked:
            p = jnp.where(diagonal_mask(rows, heads), p, 0.0)
        gp = mm(v_ref[here, :], grads, NT)
        gs = (p * (gp - mixed) * SCALE).astype(BF)
        dv_ref[here, :] += mm(p.astype(BF), grads, NN)
        dk_ref[here, :] += mm(gs, queries, NN)
        return dqt + mm(kt_ref[:, here], gs, NN)

    dqt = step(i, jnp.zeros((HD, wide), F32), True)
    dqt = lax.fori_loop(0, i, lambda j, c: step(j, c, False), dqt)
    dq = dqt.T
    mine = pl.ds(pl.multiple_of(position_of(i ^ me, count) * rows, rows), rows)
    cos, sin = cos_ref[mine, :], sin_ref[mine, :]
    for h in range(heads):
        one = turn(dq[h * rows : (h + 1) * rows, :], cos, -sin)
        out_ref[mine, h * HD : (h + 1) * HD] = one.astype(BF)

    @pl.when(i == count - 1)
    def _():
        out_ref[:, heads * HD : (heads + 1) * HD] = turn(
            dk_ref[...], cos_ref[...], -sin_ref[...]
        ).astype(BF)
        out_ref[:, (heads + 1) * HD :] = dv_ref[...].astype(BF)


def attend_back_call(me, q, g, o, lse, k, kt, v, cos, sin, rows, heads, count):
    total = q.shape[0]
    slot = lambda i, me_ref: (position_of(i ^ me_ref[0], count), 0)
    slot3 = lambda i, me_ref: (position_of(i ^ me_ref[0], count), 0, 0)
    whole = lambda i, me_ref: (0, 0)
    cols = (heads + 2) * HD
    return pl.pallas_call(
        functools.partial(attend_back_kernel, heads=heads, rows=rows, count=count),
        grid_spec=pltpu.PrefetchScalarGridSpec(
            num_scalar_prefetch=1,
            grid=(count,),
            in_specs=[
                pl.BlockSpec((rows, heads * HD), slot),
                pl.BlockSpec((rows, heads * HD), slot),
                pl.BlockSpec((rows, heads * HD), slot),
                pl.BlockSpec((1, 1, heads * rows), slot3),
                pl.BlockSpec((total, HD), whole),
                pl.BlockSpec((HD, total), whole),
                pl.BlockSpec((total, HD), whole),
                pl.BlockSpec((total, HD), whole),
                pl.BlockSpec((total, HD), whole),
            ],
            out_specs=pl.BlockSpec((total, cols), whole),
            scratch_shapes=[pltpu.VMEM((total, HD), F32), pltpu.VMEM((total, HD), F32)],
        ),
        out_shape=jax.ShapeDtypeStruct((total, cols), BF),
        compiler_params=params(("arbitrary",)),
        cost_estimate=cost(10 * total * total * heads * HD, 16 * total * HD, heads * total * total // 2),
        name="attend_back",
    )(me, q, g, o, lse, k, kt, v, cos, sin)


def feed_kernel(z_ref, g_ref, w_ref, d_ref, act_ref, grads_ref):
    cut = d_ref.shape[0]
    z = z_ref[...]
    gate = mm(z, w_ref[:, :cut], NN)
    up = mm(z, w_ref[:, cut:], NN)
    back = mm(g_ref[...], d_ref[...], NT)
    sig = jax.nn.sigmoid(gate)
    silu = gate * sig
    act_ref[...] = (silu * up).astype(BF)
    grads_ref[:, :cut] = (back * up * (sig * (1.0 + gate * (1.0 - sig)))).astype(BF)
    grads_ref[:, cut:] = (back * silu).astype(BF)


def feed_call(z_two, g_out, w_gu, w_down, rows):
    total, width = z_two.shape
    cut = w_down.shape[0]
    row = lambda i: (i, 0)
    whole = lambda i: (0, 0)
    return pl.pallas_call(
        feed_kernel,
        grid=(total // rows,),
        in_specs=[
            pl.BlockSpec((rows, width), row),
            pl.BlockSpec((rows, width), row),
            pl.BlockSpec((width, 2 * cut), whole),
            pl.BlockSpec((cut, width), whole),
        ],
        out_specs=[pl.BlockSpec((rows, cut), row), pl.BlockSpec((rows, 2 * cut), row)],
        out_shape=[
            jax.ShapeDtypeStruct((total, cut), BF),
            jax.ShapeDtypeStruct((total, 2 * cut), BF),
        ],
        compiler_params=params(("arbitrary",)),
        cost_estimate=cost(6 * total * width * cut, 4 * total * width + 6 * cut * width + 6 * total * cut),
        name="feed",
    )(z_two, g_out, w_gu, w_down)


def sum_kernel(*refs, dims):
    *ins, out_ref = refs
    acc = None
    for a_ref, b_ref in zip(ins[0::2], ins[1::2]):
        term = mm(a_ref[...], b_ref[...], dims)
        acc = term if acc is None else acc + term
    out_ref[...] = acc.astype(out_ref.dtype)


def sum_call(pairs, dims, rows, name):
    total = pairs[0][0].shape[0]
    cols = pairs[0][1].shape[1 if dims is NN else 0]
    row = lambda i: (i, 0)
    whole = lambda i: (0, 0)
    specs, flat, depth = [], [], 0
    for a, b in pairs:
        specs += [pl.BlockSpec((rows, a.shape[1]), row), pl.BlockSpec(b.shape, whole)]
        flat += [a, b]
        depth += a.shape[1]
    return pl.pallas_call(
        functools.partial(sum_kernel, dims=dims),
        grid=(total // rows,),
        in_specs=specs,
        out_specs=pl.BlockSpec((rows, cols), row),
        out_shape=jax.ShapeDtypeStruct((total, cols), BF),
        compiler_params=params(("arbitrary",)),
        cost_estimate=cost(2 * total * cols * depth, 2 * (total * depth + depth * cols + total * cols)),
        name=name,
    )(*flat)


def rms_of(values):
    return lax.rsqrt(jnp.mean(values * values, -1, keepdims=True) + EPS)


def shards(
    inputs, attn_gain, w_query, w_key, w_value, w_output, ffn_gain, w_gate, w_up, w_down, cotangent
):
    _, rows, width = inputs.shape
    n_cp = lax.axis_size("cp")
    n_dp = lax.axis_size("dp")
    me = lax.axis_index("cp")
    heads = H // n_cp
    reps = n_cp // KVH
    total = rows * n_cp
    own = w_query.shape[0]
    hidden = w_gate.shape[1]
    unit = hidden // (n_dp * n_cp)
    halves = 2
    per_half = n_dp // halves
    me_arr = jnp.reshape(me, (1,)).astype(jnp.int32)
    gain_one = attn_gain.astype(F32)[:, None]
    gain_two = ffn_gain.astype(F32)[:, None]

    def gather_z(value):
        return lax.all_gather(value, "dp", axis=0, tiled=True)

    def scatter_z(value):
        return lax.psum_scatter(value, "dp", scatter_dimension=0, tiled=True)

    def give(value):
        return lax.all_to_all(value, "cp", 0, 0)

    scaled_q = (w_query.astype(F32) * gain_one).astype(BF).reshape(own, n_cp, heads * HD)
    scaled_k = (w_key.astype(F32) * gain_one).astype(BF).reshape(own, KVH, 1, HD)
    scaled_v = (w_value.astype(F32) * gain_one).astype(BF).reshape(own, KVH, 1, HD)
    spread = lambda v: jnp.broadcast_to(v, (own, KVH, reps, HD)).reshape(own, n_cp, HD)
    qkv_own = jnp.concatenate([scaled_q, spread(scaled_k), spread(scaled_v)], 2).transpose(1, 0, 2)
    qkv_cols = (heads + 2) * HD
    w_qkv = gather_z(give(qkv_own).reshape(n_cp * own, qkv_cols))

    devices = n_dp * n_cp
    moved = [(b, (b % n_dp) * n_cp + b // n_dp) for b in range(devices)]
    moved_back = [(b, a) for a, b in moved]
    wo_rows = gather_z(lax.ppermute(w_output, ("dp", "cp"), moved))

    w_down_full = gather_z(w_down)
    scaled_g = (w_gate.astype(F32) * gain_two).astype(BF).reshape(own, n_dp, n_cp, unit)
    scaled_u = (w_up.astype(F32) * gain_two).astype(BF).reshape(own, n_dp, n_cp, unit)
    cut = per_half * unit
    w_gu, w_dn = [], []
    for h in range(halves):
        at = slice(h * per_half, (h + 1) * per_half)
        both = jnp.concatenate([scaled_g[:, at], scaled_u[:, at]], 1)
        both = both.transpose(2, 0, 1, 3).reshape(n_cp, own, 2 * cut)
        w_gu.append(gather_z(give(both).reshape(n_cp * own, 2 * cut)))
        w_dn.append(w_down_full[h * cut : (h + 1) * cut])

    shard_at = jnp.array([offset_of(p, n_cp) for p in range(n_cp)], jnp.int32) ^ me
    positions = (shard_at[:, None] * rows + jnp.arange(rows, dtype=jnp.int32)[None, :]).reshape(-1)
    half_dim = HD // 2
    inv_freq = THETA ** (-(jnp.arange(half_dim, dtype=F32) * 2.0 / HD))
    angles = positions.astype(F32)[:, None] * inv_freq[None, :]
    cos_half, sin_half = jnp.cos(angles), jnp.sin(angles)
    cos = jnp.concatenate([cos_half, cos_half], -1)
    sin = jnp.concatenate([-sin_half, sin_half], -1)

    x = inputs.reshape(rows, width).astype(F32)
    rms_one = rms_of(x)
    z_one = x * rms_one
    z_one_all = gather_rows(z_one.astype(BF), n_cp)
    g_outb = cotangent.reshape(rows, width)
    g_out = g_outb.astype(F32)
    g_out_all = gather_rows(g_outb, n_cp)
    wo_rel = gather_rows(wo_rows, n_cp)

    q, k, v, kt, vt = qkv_call(z_one_all, w_qkv, cos, sin, rows, heads)
    mixed, lse = attend_call(me_arr, q, k, vt, rows, heads, n_cp)
    pieces = trade([mixed[p * rows : (p + 1) * rows] for p in range(n_cp)], n_cp)
    attn = jnp.concatenate(pieces, 1)
    hid = x + jnp.dot(attn, wo_rel, preferred_element_type=F32)
    rms_two = rms_of(hid)
    z_two = hid * rms_two
    z_two_all = gather_rows(z_two.astype(BF), n_cp)

    acts, gus, red_gu = [], [], []
    for h in range(halves):
        act, gu = feed_call(z_two_all, g_out_all, w_gu[h], w_dn[h], rows)
        acts.append(act)
        gus.append(gu)
        red_gu.append(scatter_z(mm(z_two_all, gu, TN).astype(BF)))
    chunks = 2
    u_parts = []
    for c in range(chunks):
        at = slice(c * width // chunks, (c + 1) * width // chunks)
        part = sum_call([(gus[h], w_gu[h][at]) for h in range(halves)], NT, rows, "g_two")
        u_parts.append(scatter_rows(part, n_cp))
    u = jnp.concatenate(u_parts, 1)
    grad_down = scatter_z(jnp.concatenate([mm(a, g_out_all, TN).astype(BF) for a in acts], 0))

    g_hidden = g_out + rms_two * (u - z_two * jnp.mean(u * z_two, -1, keepdims=True))
    g_hidb = g_hidden.astype(BF)
    g_attn = mm(g_hidb, wo_rel, NT).astype(BF)
    feat = heads * HD
    g_pieces = trade([g_attn[:, p * feat : (p + 1) * feat] for p in range(n_cp)], n_cp)
    g_mixed = jnp.concatenate(g_pieces, 0)
    g_qkv = attend_back_call(me_arr, q, g_mixed, mixed, lse, k, kt, v, cos, sin, rows, heads, n_cp)
    red_qkv = scatter_z(mm(z_one_all, g_qkv, TN).astype(BF))
    w_parts = []
    for c in range(chunks):
        at = slice(c * width // chunks, (c + 1) * width // chunks)
        part = sum_call([(g_qkv, w_qkv[at])], NT, rows, "g_one")
        w_parts.append(scatter_rows(part, n_cp))
    w_one = jnp.concatenate(w_parts, 1)
    grad_in = g_hidden + rms_one * (w_one - z_one * jnp.mean(w_one * z_one, -1, keepdims=True))

    out_part = sum_call([(acts[h], w_dn[h]) for h in range(halves)], NN, rows, "out")
    output = hid + scatter_rows(out_part, n_cp)
    wo_part = mm(attn, g_hidb, TN).astype(BF)
    wo_sum = scatter_z(scatter_rows(wo_part, n_cp).astype(BF))
    grad_output = lax.ppermute(wo_sum, ("dp", "cp"), moved_back).astype(F32)

    got = give(red_qkv.reshape(n_cp, own, qkv_cols)).astype(F32)
    raw_q = got[:, :, : heads * HD].transpose(1, 0, 2).reshape(own, H * HD)
    fold = lambda v: v.reshape(KVH, reps, own, HD).sum(1).transpose(1, 0, 2).reshape(own, KVH * HD)
    raw_k = fold(got[:, :, heads * HD : (heads + 1) * HD])
    raw_v = fold(got[:, :, (heads + 1) * HD :])
    grad_attn_gain = (
        jnp.sum(raw_q * w_query.astype(F32), 1)
        + jnp.sum(raw_k * w_key.astype(F32), 1)
        + jnp.sum(raw_v * w_value.astype(F32), 1)
    )
    back_gu = jnp.stack([give(r.reshape(n_cp, own, 2 * cut)) for r in red_gu], 0)
    back_gu = back_gu.reshape(halves, n_cp, own, 2, per_half, unit).transpose(3, 2, 0, 4, 1, 5)
    back_gu = back_gu.reshape(2, own, hidden).astype(F32)
    raw_g, raw_u = back_gu[0], back_gu[1]
    grad_ffn_gain = jnp.sum(raw_g * w_gate.astype(F32), 1) + jnp.sum(raw_u * w_up.astype(F32), 1)

    return (
        output[None],
        grad_in[None],
        grad_attn_gain,
        raw_q * gain_one,
        raw_k * gain_one,
        raw_v * gain_one,
        grad_output,
        grad_ffn_gain,
        raw_g * gain_two,
        raw_u * gain_two,
        grad_down.astype(F32),
    )


def solution(mesh):
    both = ("dp", "cp")
    rows = P("dp", "cp", None)
    mat = P(both, None)
    vec = P(both)
    return jax.shard_map(
        shards,
        mesh=mesh,
        in_specs=(rows, vec, mat, mat, mat, mat, vec, mat, mat, mat, rows),
        out_specs=(rows, rows, vec, mat, mat, mat, mat, vec, mat, mat, mat),
        check_vma=False,
    )
```

```python
import functools
import math

import jax
import jax.numpy as jnp
from jax import lax
from jax.experimental import pallas as pl
from jax.experimental.pallas import tpu as pltpu
from jax.sharding import PartitionSpec as P

H = 16
KVH = 8
HD = 128
EPS = 1e-05
THETA = 1000000.0
SCALE = HD ** (-0.5)
LOG2E = math.log2(math.e)
BF = jnp.bfloat16
F32 = jnp.float32
VMEM_LIMIT = 56 * 1024 * 1024
SHARE = 0.05

NN = (((1,), (0,)), ((), ()))
NT = (((1,), (1,)), ((), ()))
TN = (((0,), (0,)), ((), ()))


def mm(left, right, dims):
    return lax.dot_general(left, right, dims, preferred_element_type=F32)


def offset_of(position, count):
    half = count // 2
    return ((position % half) << 1) | (position // half)


def position_of(offset, count):
    return (offset >> 1) + (offset & 1) * (count // 2)


def after(value, *deps):
    return lax.optimization_barrier((value, *deps))[0]


def swap(value, count, offset):
    return lax.ppermute(value, "cp", [(i, i ^ offset) for i in range(count)])


def gather_rows(part, count, dep=None):
    half = part.shape[0] // 2
    if count == 8:
        by_x = swap(part, count, 2)
        by_y = swap(part, count, 4)
        if dep is not None:
            by_y = after(by_y, *dep)
        near = jnp.concatenate([part, by_x, by_y], 0)
        near_other = swap(near, count, 1)
        far = jnp.concatenate([swap(by_y[:half], count, 2), swap(by_x[half:], count, 4)], 0)
        return jnp.concatenate([near, far, near_other, swap(far, count, 1)], 0)
    inner, bit = part, 2
    while bit < count:
        inner = jnp.concatenate([inner, swap(inner, count, bit)], 0)
        bit *= 2
    return jnp.concatenate([inner, swap(inner, count, 1)], 0)


def plus(left, right):
    return (left.astype(F32) + right.astype(F32)).astype(BF)


def scatter_first(low, high, count):
    return plus(low, swap(high, count, 1))


def scatter_mid(acc, count):
    rows = 2 * acc.shape[0] // count
    half = rows // 2
    parts = [acc[i * rows : (i + 1) * rows] for i in range(count // 2)]
    if count == 8:
        own, to_x, to_y, far = parts
        from_x = swap(far[:half], count, 2)
        from_y = swap(far[half:], count, 4)
        send_x = jnp.concatenate([to_x[:half], plus(to_x[half:], from_y)], 0)
        send_y = jnp.concatenate([plus(to_y[:half], from_x), to_y[half:]], 0)
        return own, send_x, send_y
    bit = count // 2
    while bit > 2:
        keep, give = parts[: len(parts) // 2], parts[len(parts) // 2 :]
        parts = [plus(a, swap(b, count, bit)) for a, b in zip(keep, give)]
        bit //= 2
    return tuple(parts)


def scatter_last(state, count):
    total = state[0].astype(F32)
    for offset, part in zip((2, 4), state[1:]):
        total = total + swap(part, count, offset).astype(F32)
    return total


def deal(count, n_cp, shift):
    return [
        (b, ((b % count + shift) % count) * n_cp + b // count) for b in range(count * n_cp)
    ]


def params(semantics):
    return pltpu.CompilerParams(dimension_semantics=semantics, vmem_limit_bytes=VMEM_LIMIT)


def cost(flops, nbytes, trans=0):
    return pl.CostEstimate(
        flops=int(flops * SHARE), bytes_accessed=int(nbytes * SHARE), transcendentals=int(trans * SHARE)
    )


def turn(value, cos, sin):
    return value * cos + pltpu.roll(value, HD // 2, 1) * sin


def qkv_kernel(z_ref, w_ref, cos_ref, sin_ref, q_ref, k_ref, v_ref, kt_ref, vt_ref, *, heads):
    cos, sin = cos_ref[...], sin_ref[...]
    flat = None
    depth = z_ref.shape[1] // w_ref.shape[0]
    for d in range(w_ref.shape[0]):
        term = mm(z_ref[:, d * depth : (d + 1) * depth], w_ref[d, :depth, :], NN)
        flat = term if flat is None else flat + term
    for h in range(heads):
        at = slice(h * HD, (h + 1) * HD)
        q_ref[:, at] = turn(flat[:, at], cos, sin).astype(BF)
    key = turn(flat[:, heads * HD : (heads + 1) * HD], cos, sin)
    value = flat[:, (heads + 1) * HD :]
    k_ref[...] = key.astype(BF)
    v_ref[...] = value.astype(BF)
    kt_ref[...] = key.T.astype(BF)
    vt_ref[...] = value.T.astype(BF)


def qkv_call(z_one, w_qkv, cos, sin, rows, heads):
    total, width = z_one.shape
    cols = w_qkv.shape[2]
    row = lambda i: (i, 0)
    col = lambda i: (0, i)
    whole = lambda i: (0, 0)
    return pl.pallas_call(
        functools.partial(qkv_kernel, heads=heads),
        grid=(total // rows,),
        in_specs=[
            pl.BlockSpec((rows, width), row),
            pl.BlockSpec(w_qkv.shape, lambda i: (0, 0, 0)),
            pl.BlockSpec((rows, HD), row),
            pl.BlockSpec((rows, HD), row),
        ],
        out_specs=[
            pl.BlockSpec((rows, heads * HD), row),
            pl.BlockSpec((rows, HD), row),
            pl.BlockSpec((rows, HD), row),
            pl.BlockSpec((HD, rows), col),
            pl.BlockSpec((HD, rows), col),
        ],
        out_shape=[
            jax.ShapeDtypeStruct((total, heads * HD), BF),
            jax.ShapeDtypeStruct((total, HD), BF),
            jax.ShapeDtypeStruct((total, HD), BF),
            jax.ShapeDtypeStruct((HD, total), BF),
            jax.ShapeDtypeStruct((HD, total), BF),
        ],
        compiler_params=params(("arbitrary",)),
        cost_estimate=cost(2 * total * width * cols, 2 * (total * width + width * cols)),
        name="qkv",
    )(z_one, w_qkv, cos, sin)


def stack_heads(block, heads):
    if heads == 1:
        return block
    return jnp.concatenate([block[:, h * HD : (h + 1) * HD] for h in range(heads)], 0)


def diagonal_mask(rows, heads):
    key_at = lax.broadcasted_iota(jnp.int32, (rows, rows), 0)
    query_at = lax.broadcasted_iota(jnp.int32, (rows, rows), 1)
    one = key_at <= query_at
    return one if heads == 1 else jnp.concatenate([one] * heads, 1)


def attend_kernel(me_ref, q_ref, k_ref, vt_ref, o_ref, lse_ref, *, heads, rows, count):
    i = pl.program_id(0)
    me = me_ref[0]
    wide = heads * rows
    queries = stack_heads(q_ref[...], heads)

    def step(j, carry, masked):
        top, total, acc = carry
        at = pl.multiple_of(position_of(j ^ me, count) * rows, rows)
        s = mm(k_ref[pl.ds(at, rows), :], queries, NT) * (SCALE * LOG2E)
        if masked:
            s = jnp.where(diagonal_mask(rows, heads), s, -1e30)
        new_top = jnp.maximum(top, jnp.max(s, 0, keepdims=True))
        fade = jnp.exp2(top - new_top)
        p = jnp.exp2(s - new_top)
        total = total * fade + jnp.sum(p, 0, keepdims=True)
        acc = acc * fade + mm(vt_ref[:, pl.ds(at, rows)], p.astype(BF), NN)
        return new_top, total, acc

    carry = (
        jnp.full((1, wide), -1e30, F32),
        jnp.zeros((1, wide), F32),
        jnp.zeros((HD, wide), F32),
    )
    carry = step(i, carry, True)
    top, total, acc = lax.fori_loop(0, i, lambda j, c: step(j, c, False), carry)
    out = (acc / total).T
    for h in range(heads):
        o_ref[:, h * HD : (h + 1) * HD] = out[h * rows : (h + 1) * rows, :].astype(BF)
    lse_ref[0] = top + jnp.log2(total)


def attend_call(me, q, k, vt, rows, heads, count):
    total = q.shape[0]
    slot = lambda i, me_ref: (position_of(i ^ me_ref[0], count), 0)
    true = lambda i, me_ref: (i, 0)
    true3 = lambda i, me_ref: (i, 0, 0)
    whole = lambda i, me_ref: (0, 0)
    return pl.pallas_call(
        functools.partial(attend_kernel, heads=heads, rows=rows, count=count),
        grid_spec=pltpu.PrefetchScalarGridSpec(
            num_scalar_prefetch=1,
            grid=(count,),
            in_specs=[
                pl.BlockSpec((rows, heads * HD), slot),
                pl.BlockSpec((total, HD), whole),
                pl.BlockSpec((HD, total), whole),
            ],
            out_specs=[
                pl.BlockSpec((rows, heads * HD), true),
                pl.BlockSpec((1, 1, heads * rows), true3),
            ],
        ),
        out_shape=[
            jax.ShapeDtypeStruct((total, heads * HD), BF),
            jax.ShapeDtypeStruct((count, 1, heads * rows), F32),
        ],
        compiler_params=params(("arbitrary",)),
        cost_estimate=cost(4 * total * total * heads * HD, 8 * total * HD, heads * total * total // 2),
        name="attend",
    )(me, q, k, vt)


def attend_back_kernel(
    me_ref,
    q_ref,
    g_ref,
    o_ref,
    lse_ref,
    k_ref,
    kt_ref,
    v_ref,
    cos_ref,
    sin_ref,
    out_ref,
    dk_ref,
    dv_ref,
    *,
    heads,
    rows,
    count,
):
    i = pl.program_id(0)
    me = me_ref[0]
    wide = heads * rows

    @pl.when(i == 0)
    def _():
        dk_ref[...] = jnp.zeros_like(dk_ref)
        dv_ref[...] = jnp.zeros_like(dv_ref)

    queries = stack_heads(q_ref[...], heads)
    grads = stack_heads(g_ref[...], heads)
    outs = stack_heads(o_ref[...], heads)
    lse = lse_ref[0]
    mixed = jnp.sum((outs.astype(F32) * grads.astype(F32)).T, 0, keepdims=True)

    def step(j, dqt, masked):
        at = pl.multiple_of(position_of(j ^ me, count) * rows, rows)
        here = pl.ds(at, rows)
        s = mm(k_ref[here, :], queries, NT) * (SCALE * LOG2E)
        p = jnp.exp2(s - lse)
        if masked:
            p = jnp.where(diagonal_mask(rows, heads), p, 0.0)
        gp = mm(v_ref[here, :], grads, NT)
        gs = (p * (gp - mixed) * SCALE).astype(BF)
        dv_ref[here, :] += mm(p.astype(BF), grads, NN)
        dk_ref[here, :] += mm(gs, queries, NN)
        return dqt + mm(kt_ref[:, here], gs, NN)

    dqt = step(i, jnp.zeros((HD, wide), F32), True)
    dqt = lax.fori_loop(0, i, lambda j, c: step(j, c, False), dqt)
    dq = dqt.T
    mine = pl.ds(pl.multiple_of(position_of(i ^ me, count) * rows, rows), rows)
    cos, sin = cos_ref[mine, :], sin_ref[mine, :]
    for h in range(heads):
        one = turn(dq[h * rows : (h + 1) * rows, :], cos, -sin)
        out_ref[mine, h * HD : (h + 1) * HD] = one.astype(BF)

    @pl.when(i == count - 1)
    def _():
        out_ref[:, heads * HD : (heads + 1) * HD] = turn(
            dk_ref[...], cos_ref[...], -sin_ref[...]
        ).astype(BF)
        out_ref[:, (heads + 1) * HD :] = dv_ref[...].astype(BF)


def attend_back_call(me, q, g, o, lse, k, kt, v, cos, sin, rows, heads, count):
    total = q.shape[0]
    slot = lambda i, me_ref: (position_of(i ^ me_ref[0], count), 0)
    true = lambda i, me_ref: (i, 0)
    true3 = lambda i, me_ref: (i, 0, 0)
    whole = lambda i, me_ref: (0, 0)
    cols = (heads + 2) * HD
    return pl.pallas_call(
        functools.partial(attend_back_kernel, heads=heads, rows=rows, count=count),
        grid_spec=pltpu.PrefetchScalarGridSpec(
            num_scalar_prefetch=1,
            grid=(count,),
            in_specs=[
                pl.BlockSpec((rows, heads * HD), slot),
                pl.BlockSpec((rows, heads * HD), true),
                pl.BlockSpec((rows, heads * HD), true),
                pl.BlockSpec((1, 1, heads * rows), true3),
                pl.BlockSpec((total, HD), whole),
                pl.BlockSpec((HD, total), whole),
                pl.BlockSpec((total, HD), whole),
                pl.BlockSpec((total, HD), whole),
                pl.BlockSpec((total, HD), whole),
            ],
            out_specs=pl.BlockSpec((total, cols), whole),
            scratch_shapes=[pltpu.VMEM((total, HD), F32), pltpu.VMEM((total, HD), F32)],
        ),
        out_shape=jax.ShapeDtypeStruct((total, cols), BF),
        compiler_params=params(("arbitrary",)),
        cost_estimate=cost(10 * total * total * heads * HD, 16 * total * HD, heads * total * total // 2),
        name="attend_back",
    )(me, q, g, o, lse, k, kt, v, cos, sin)


def back_act_kernel(g_ref, d_ref, out_ref):
    out_ref[...] = mm(g_ref[...], d_ref[...], NT)


def back_act_call(g_out, w_down, rows):
    total, width = g_out.shape
    cols = w_down.shape[0]
    return pl.pallas_call(
        back_act_kernel,
        grid=(total // rows,),
        in_specs=[
            pl.BlockSpec((rows, width), lambda i: (i, 0)),
            pl.BlockSpec((cols, width), lambda i: (0, 0)),
        ],
        out_specs=pl.BlockSpec((rows, cols), lambda i: (i, 0)),
        out_shape=jax.ShapeDtypeStruct((total, cols), F32),
        compiler_params=params(("arbitrary",)),
        cost_estimate=cost(2 * total * width * cols, 2 * total * width + 2 * cols * width + 4 * total * cols),
        name="back_act",
    )(g_out, w_down)


def feed_kernel(z_ref, g_ref, w_ref, act_ref, grads_ref):
    cut = g_ref.shape[1]
    z = z_ref[...]
    gate = mm(z, w_ref[:, :cut], NN)
    up = mm(z, w_ref[:, cut:], NN)
    back = g_ref[...]
    sig = jax.nn.sigmoid(gate)
    silu = gate * sig
    act_ref[...] = (silu * up).astype(BF)
    grads_ref[:, :cut] = (back * up * (sig * (1.0 + gate * (1.0 - sig)))).astype(BF)
    grads_ref[:, cut:] = (back * silu).astype(BF)


def feed_call(z_two, g_act, w_gu, part, rows):
    total, width = z_two.shape
    cut = w_gu.shape[1] // 2
    row = lambda i: (i, 0)
    whole = lambda i: (0, 0)
    return pl.pallas_call(
        feed_kernel,
        grid=(total // rows,),
        in_specs=[
            pl.BlockSpec((rows, width), row),
            pl.BlockSpec((rows, cut), lambda i: (i, part)),
            pl.BlockSpec((width, 2 * cut), whole),
        ],
        out_specs=[pl.BlockSpec((rows, cut), row), pl.BlockSpec((rows, 2 * cut), row)],
        out_shape=[
            jax.ShapeDtypeStruct((total, cut), BF),
            jax.ShapeDtypeStruct((total, 2 * cut), BF),
        ],
        compiler_params=params(("arbitrary",)),
        cost_estimate=cost(4 * total * width * cut, 2 * total * width + 4 * cut * width + 10 * total * cut),
        name="feed",
    )(z_two, g_act, w_gu)


def sum_kernel(*refs, dims):
    *ins, low_ref, high_ref = refs
    acc = None
    for a_ref, b_ref in zip(ins[0::2], ins[1::2]):
        term = mm(a_ref[...], b_ref[...], dims)
        acc = term if acc is None else acc + term
    acc = acc.astype(BF)
    half = pl.num_programs(0) // 2

    @pl.when(pl.program_id(0) < half)
    def _():
        high_ref[...] = acc

    @pl.when(pl.program_id(0) >= half)
    def _():
        low_ref[...] = acc


def sum_call(pairs, dims, rows, name):
    total = pairs[0][0].shape[0]
    cols = pairs[0][1].shape[1 if dims is NN else 0]
    steps = total // rows
    half = steps // 2
    row = lambda i: ((i + half) % steps, 0)
    low = lambda i: (jnp.maximum(i - half, 0), 0)
    high = lambda i: (jnp.minimum(i, half - 1), 0)
    whole = lambda i: (0, 0)
    specs, flat, depth = [], [], 0
    for a, b in pairs:
        specs += [pl.BlockSpec((rows, a.shape[1]), row), pl.BlockSpec(b.shape, whole)]
        flat += [a, b]
        depth += a.shape[1]
    return pl.pallas_call(
        functools.partial(sum_kernel, dims=dims),
        grid=(total // rows,),
        in_specs=specs,
        out_specs=[pl.BlockSpec((rows, cols), low), pl.BlockSpec((rows, cols), high)],
        out_shape=[jax.ShapeDtypeStruct((total // 2, cols), BF)] * 2,
        compiler_params=params(("arbitrary",)),
        cost_estimate=cost(2 * total * cols * depth, 2 * (total * depth + depth * cols + total * cols)),
        name=name,
    )(*flat)


def split_rows(count):
    half = count // 2
    row = lambda i: (i + half) % count
    low = lambda i: jnp.maximum(i - half, 0)
    high = lambda i: jnp.minimum(i, half - 1)
    return half, row, low, high


def hidden_kernel(me_ref, a_ref, w_ref, x_ref, hid_ref, z_ref, rms_ref):
    p = pl.program_id(0)

    @pl.when(p == 0)
    def _():
        hid_ref[...] = x_ref[...].astype(F32)

    hid_ref[...] += mm(a_ref[0], w_ref[...], NN)

    @pl.when(p == pl.num_programs(0) - 1)
    def _():
        hid = hid_ref[...]
        rms = rms_of(hid)
        rms_ref[...] = rms
        z_ref[...] = (hid * rms).astype(BF)


def hidden_call(me, attn, wo, x, count):
    _, rows, feat = attn.shape
    width = wo.shape[1]
    true3 = lambda p, me_ref: (offset_of(p, count) ^ me_ref[0], 0, 0)
    block = lambda p, me_ref: (p, 0)
    whole = lambda p, me_ref: (0, 0)
    return pl.pallas_call(
        hidden_kernel,
        grid_spec=pltpu.PrefetchScalarGridSpec(
            num_scalar_prefetch=1,
            grid=(count,),
            in_specs=[
                pl.BlockSpec((1, rows, feat), true3),
                pl.BlockSpec((feat, width), block),
                pl.BlockSpec((rows, width), whole),
            ],
            out_specs=[
                pl.BlockSpec((rows, width), whole),
                pl.BlockSpec((rows, width), whole),
                pl.BlockSpec((rows, 1), whole),
            ],
        ),
        out_shape=[
            jax.ShapeDtypeStruct((rows, width), F32),
            jax.ShapeDtypeStruct((rows, width), BF),
            jax.ShapeDtypeStruct((rows, 1), F32),
        ],
        compiler_params=params(("arbitrary",)),
        cost_estimate=cost(2 * rows * feat * count * width, 2 * feat * count * width + 10 * rows * width),
        name="hidden",
    )(me, attn, wo, x)


def back_attn_kernel(me_ref, g_ref, w_ref, out_ref):
    out_ref[0] = mm(g_ref[...], w_ref[...], NT).astype(BF)


def back_attn_call(me, g, wo, count):
    rows, width = g.shape
    feat = wo.shape[0] // count
    true3 = lambda p, me_ref: (offset_of(p, count) ^ me_ref[0], 0, 0)
    block = lambda p, me_ref: (p, 0)
    whole = lambda p, me_ref: (0, 0)
    return pl.pallas_call(
        back_attn_kernel,
        grid_spec=pltpu.PrefetchScalarGridSpec(
            num_scalar_prefetch=1,
            grid=(count,),
            in_specs=[pl.BlockSpec((rows, width), whole), pl.BlockSpec((feat, width), block)],
            out_specs=pl.BlockSpec((1, rows, feat), true3),
        ),
        out_shape=jax.ShapeDtypeStruct((count, rows, feat), BF),
        compiler_params=params(("arbitrary",)),
        cost_estimate=cost(2 * rows * feat * count * width, 2 * feat * count * width + 4 * rows * width),
        name="back_attn",
    )(me, g, wo)


def grad_wo_kernel(me_ref, a_ref, g_ref, low_ref, high_ref):
    out = mm(a_ref[0], g_ref[...], TN).astype(BF)
    half = pl.num_programs(0) // 2

    @pl.when(pl.program_id(0) < half)
    def _():
        high_ref[...] = out

    @pl.when(pl.program_id(0) >= half)
    def _():
        low_ref[...] = out


def grad_wo_call(me, attn, g, count):
    _, rows, feat = attn.shape
    width = g.shape[1]
    half, row, low, high = split_rows(count)
    return pl.pallas_call(
        grad_wo_kernel,
        grid_spec=pltpu.PrefetchScalarGridSpec(
            num_scalar_prefetch=1,
            grid=(count,),
            in_specs=[
                pl.BlockSpec(
                    (1, rows, feat), lambda p, me_ref: (offset_of(row(p), count) ^ me_ref[0], 0, 0)
                ),
                pl.BlockSpec((rows, width), lambda p, me_ref: (0, 0)),
            ],
            out_specs=[
                pl.BlockSpec((feat, width), lambda p, me_ref: (low(p), 0)),
                pl.BlockSpec((feat, width), lambda p, me_ref: (high(p), 0)),
            ],
        ),
        out_shape=[jax.ShapeDtypeStruct((half * feat, width), BF)] * 2,
        compiler_params=params(("arbitrary",)),
        cost_estimate=cost(2 * rows * feat * count * width, 2 * feat * count * width + 4 * rows * width),
        name="grad_wo",
    )(me, attn, g)


def finish_feed_kernel(*refs, halves, per_half, unit, count):
    gots, (wg_ref, wu_ref, gain_ref, g_ref, u_ref, sum_ref) = refs[:halves], refs[halves:]
    gain = gain_ref[...]
    total = None
    for h, got_ref in enumerate(gots):
        for kind, (w_ref, out_ref) in enumerate(((wg_ref, g_ref), (wu_ref, u_ref))):
            for i in range(per_half):
                frm = (kind * per_half + i) * unit
                for t in range(count):
                    at = ((h * per_half + i) * count + t) * unit
                    raw = got_ref[t, :, frm : frm + unit].astype(F32)
                    out_ref[:, at : at + unit] = raw * gain
                    term = raw * w_ref[:, at : at + unit].astype(F32)
                    total = term if total is None else total + term
    sum_ref[...] = jnp.sum(total, 1, keepdims=True)


def finish_feed_call(gots, w_gate, w_up, gain, per_half, unit):
    own, hidden = w_gate.shape
    return pl.pallas_call(
        functools.partial(
            finish_feed_kernel,
            halves=len(gots),
            per_half=per_half,
            unit=unit,
            count=gots[0].shape[0],
        ),
        out_shape=[
            jax.ShapeDtypeStruct((own, hidden), F32),
            jax.ShapeDtypeStruct((own, hidden), F32),
            jax.ShapeDtypeStruct((own, 1), F32),
        ],
        compiler_params=pltpu.CompilerParams(vmem_limit_bytes=VMEM_LIMIT),
        cost_estimate=cost(8 * own * hidden, 16 * own * hidden),
        name="finish_feed",
    )(*gots, w_gate, w_up, gain)


def finish_qkv_kernel(
    got_ref, wq_ref, wk_ref, wv_ref, gain_ref, q_ref, k_ref, v_ref, sum_ref, *, heads, reps
):
    gain = gain_ref[...]
    total = None
    feat = heads * HD
    for t in range(got_ref.shape[0]):
        raw = got_ref[t, :, :feat].astype(F32)
        at = slice(t * feat, (t + 1) * feat)
        q_ref[:, at] = raw * gain
        term = jnp.sum(raw * wq_ref[:, at].astype(F32), 1, keepdims=True)
        total = term if total is None else total + term
    for kind, (w_ref, out_ref) in enumerate(((wk_ref, k_ref), (wv_ref, v_ref))):
        frm = slice(feat + kind * HD, feat + (kind + 1) * HD)
        for t in range(got_ref.shape[0] // reps):
            raw = got_ref[t * reps, :, frm].astype(F32)
            for r in range(1, reps):
                raw = raw + got_ref[t * reps + r, :, frm].astype(F32)
            at = slice(t * HD, (t + 1) * HD)
            out_ref[:, at] = raw * gain
            total = total + jnp.sum(raw * w_ref[:, at].astype(F32), 1, keepdims=True)
    sum_ref[...] = total


def finish_qkv_call(got, w_query, w_key, w_value, gain, heads, reps):
    own = w_query.shape[0]
    like = lambda w: jax.ShapeDtypeStruct(w.shape, F32)
    return pl.pallas_call(
        functools.partial(finish_qkv_kernel, heads=heads, reps=reps),
        out_shape=[like(w_query), like(w_key), like(w_value), jax.ShapeDtypeStruct((own, 1), F32)],
        compiler_params=pltpu.CompilerParams(vmem_limit_bytes=VMEM_LIMIT),
        cost_estimate=cost(8 * own * w_query.shape[1], 16 * own * w_query.shape[1]),
        name="finish_qkv",
    )(got, w_query, w_key, w_value, gain)


def rms_of(values):
    return lax.rsqrt(jnp.mean(values * values, -1, keepdims=True) + EPS)


def shards(
    inputs, attn_gain, w_query, w_key, w_value, w_output, ffn_gain, w_gate, w_up, w_down, cotangent
):
    _, rows, width = inputs.shape
    n_cp = lax.axis_size("cp")
    n_dp = lax.axis_size("dp")
    me = lax.axis_index("cp")
    heads = H // n_cp
    reps = n_cp // KVH
    total = rows * n_cp
    own = w_query.shape[0]
    hidden = w_gate.shape[1]
    unit = hidden // (n_dp * n_cp)
    halves = 2
    per_half = n_dp // halves
    me_arr = jnp.reshape(me, (1,)).astype(jnp.int32)
    gain_one = attn_gain.astype(F32)[:, None]
    gain_two = ffn_gain.astype(F32)[:, None]

    def gather_z(value):
        return lax.all_gather(value, "dp", axis=0, tiled=True)

    def scatter_z(value):
        return lax.psum_scatter(value, "dp", scatter_dimension=0, tiled=True)

    def give(value):
        return lax.all_to_all(value, "cp", 0, 0)

    scaled_q = (w_query.astype(F32) * gain_one).astype(BF).reshape(own, n_cp, heads * HD)
    scaled_k = (w_key.astype(F32) * gain_one).astype(BF).reshape(own, KVH, 1, HD)
    scaled_v = (w_value.astype(F32) * gain_one).astype(BF).reshape(own, KVH, 1, HD)
    spread = lambda v: jnp.broadcast_to(v, (own, KVH, reps, HD)).reshape(own, n_cp, HD)
    qkv_own = jnp.concatenate([scaled_q, spread(scaled_k), spread(scaled_v)], 2).transpose(1, 0, 2)
    qkv_cols = (heads + 2) * HD
    qkv_rows = give(qkv_own).reshape(n_cp * own, qkv_cols)
    wo_own = lax.ppermute(w_output, ("dp", "cp"), deal(n_dp, n_cp, 0))
    depth = n_cp * own
    packs = own * width % qkv_cols == 0
    if packs:
        joint = jnp.concatenate([qkv_rows, wo_own.reshape(-1, qkv_cols)], 0)
        joint = gather_z(joint).reshape(n_dp, -1, qkv_cols)
        wo_rows = joint[:, depth:].reshape(n_dp * own, width)
    else:
        joint = gather_z(qkv_rows).reshape(n_dp, -1, qkv_cols)
        wo_rows = gather_z(wo_own)

    w_down_full = gather_z(w_down)
    scaled_g = (w_gate.astype(F32) * gain_two).astype(BF).reshape(own, n_dp, n_cp, unit)
    scaled_u = (w_up.astype(F32) * gain_two).astype(BF).reshape(own, n_dp, n_cp, unit)
    cut = per_half * unit
    w_gu, w_dn, last, given = [], [], qkv_rows, []
    for h in range(halves):
        at = slice(h * per_half, (h + 1) * per_half)
        both = jnp.concatenate([scaled_g[:, at], scaled_u[:, at]], 1)
        both = both.transpose(2, 0, 1, 3).reshape(n_cp, own, 2 * cut)
        last = give(after(both, last))
        given.append(last)
        w_gu.append(gather_z(last.reshape(n_cp * own, 2 * cut)))
        w_dn.append(w_down_full[h * cut : (h + 1) * cut])

    shard_at = jnp.array([offset_of(p, n_cp) for p in range(n_cp)], jnp.int32) ^ me
    positions = (shard_at[:, None] * rows + jnp.arange(rows, dtype=jnp.int32)[None, :]).reshape(-1)
    half_dim = HD // 2
    inv_freq = THETA ** (-(jnp.arange(half_dim, dtype=F32) * 2.0 / HD))
    angles = positions.astype(F32)[:, None] * inv_freq[None, :]
    cos_half, sin_half = jnp.cos(angles), jnp.sin(angles)
    cos = jnp.concatenate([cos_half, cos_half], -1)
    sin = jnp.concatenate([-sin_half, sin_half], -1)

    xb = inputs.reshape(rows, width)
    x = xb.astype(F32)
    rms_one = rms_of(x)
    z_one = x * rms_one
    z_one_all = gather_rows(z_one.astype(BF), n_cp, [cos, sin] + given)
    wo_rel = gather_rows(wo_rows, n_cp)
    g_outb = cotangent.reshape(rows, width)
    g_out = g_outb.astype(F32)
    g_out_all = gather_rows(after(g_outb, z_one_all), n_cp)
    g_act = back_act_call(g_out_all, w_down_full, rows)

    q, k, v, kt, vt = qkv_call(z_one_all, joint, cos, sin, rows, heads)
    mixed, lse = attend_call(me_arr, q, k, vt, rows, heads, n_cp)
    feat = heads * HD
    attn = give(mixed.reshape(n_cp, rows, feat))
    hid, z_two_b, rms_two = hidden_call(me_arr, after(attn, g_act), wo_rel, xb, n_cp)
    z_two_all = gather_rows(z_two_b, n_cp)

    acts, gus, red_gu = [], [], []
    for h in range(halves):
        z_in = after(z_two_all, part_gu) if h else z_two_all
        act, gu = feed_call(z_in, g_act, w_gu[h], h, rows)
        acts.append(act)
        gus.append(gu)
        if h == 0:
            part_gu = mm(z_two_all, gu, TN).astype(BF)
            red_gu.append(scatter_z(part_gu))
    chunks = 2
    accs = []
    for c in range(chunks):
        at = slice(c * width // chunks, (c + 1) * width // chunks)
        part = sum_call([(gus[h], w_gu[h][at]) for h in range(halves)], NT, rows, "g_two")
        accs.append(scatter_first(*part, n_cp))
    states = [scatter_mid(acc, n_cp) for acc in accs]
    part_gu = mm(z_two_all, after(gus[1], accs[0]), TN).astype(BF)
    red_gu.append(scatter_z(part_gu))
    downs = []
    for c, act in enumerate(acts):
        act = after(act, part_gu, *states[c])
        downs.append(mm(act, g_out_all, TN).astype(BF))
    grad_down = scatter_z(after(jnp.concatenate(downs, 0), red_gu[0]))
    out_part = sum_call([(after(acts[h], *downs), w_dn[h]) for h in range(halves)], NN, rows, "out")
    u = jnp.concatenate([scatter_last(state, n_cp) for state in states], 1)

    z_two = hid * rms_two
    g_hidden = g_out + rms_two * (u - z_two * jnp.mean(u * z_two, -1, keepdims=True))
    g_hidb = g_hidden.astype(BF)
    wo_part = grad_wo_call(me_arr, attn, after(g_hidb, *out_part), n_cp)
    g_heads = back_attn_call(me_arr, after(g_hidb, *wo_part), wo_rel, n_cp)
    g_mixed = give(g_heads).reshape(total, feat)
    wo_state = scatter_mid(scatter_first(*wo_part, n_cp), n_cp)
    out_state = scatter_mid(scatter_first(*out_part, n_cp), n_cp)
    lse = after(lse, red_gu[1], *wo_state, *out_state)
    g_qkv = attend_back_call(me_arr, q, g_mixed, mixed, lse, k, kt, v, cos, sin, rows, heads, n_cp)
    part_qkv = mm(z_one_all, g_qkv, TN).astype(BF)
    back_gu = [give(after(red_gu[0].reshape(n_cp, own, 2 * cut), g_qkv))]
    wo_sum = scatter_last(wo_state, n_cp).astype(BF)
    if packs:
        both = jnp.concatenate(
            [part_qkv.reshape(n_dp, depth, qkv_cols), wo_sum.reshape(n_dp, -1, qkv_cols)], 1
        ).reshape(-1, qkv_cols)
        g_qkv = after(g_qkv, both)
    w_states = []
    w_qkv = joint[:, :depth].reshape(width, qkv_cols)
    for c in range(chunks):
        at = slice(c * width // chunks, (c + 1) * width // chunks)
        part = sum_call([(g_qkv, w_qkv[at])], NT, rows, "g_one")
        w_states.append(scatter_mid(scatter_first(*part, n_cp), n_cp))

    output = hid + scatter_last(out_state, n_cp)
    back_pairs = [(b, a) for a, b in deal(n_dp, n_cp, 0)]
    if packs:
        both = scatter_z(after(both, grad_down))
        red_qkv, wo_sum = both[:depth], both[depth:].reshape(own, width)
    else:
        red_qkv, wo_sum = scatter_z(part_qkv), scatter_z(wo_sum)
    grad_output = lax.ppermute(wo_sum, ("dp", "cp"), back_pairs).astype(F32)
    w_one = jnp.concatenate([scatter_last(state, n_cp) for state in w_states], 1)
    grad_in = g_hidden + rms_one * (w_one - z_one * jnp.mean(w_one * z_one, -1, keepdims=True))

    back_gu.append(give(red_gu[1].reshape(n_cp, own, 2 * cut)))
    grad_g, grad_u, gain_two_sum = finish_feed_call(back_gu, w_gate, w_up, gain_two, per_half, unit)
    got = give(after(red_qkv.reshape(n_cp, own, qkv_cols), back_gu[1]))
    grad_q, grad_k, grad_v, gain_one_sum = finish_qkv_call(
        got, w_query, w_key, w_value, gain_one, heads, reps
    )

    return (
        output[None],
        grad_in[None],
        gain_one_sum[:, 0],
        grad_q,
        grad_k,
        grad_v,
        grad_output,
        gain_two_sum[:, 0],
        grad_g,
        grad_u,
        grad_down.astype(F32),
    )


def solution(mesh):
    both = ("dp", "cp")
    rows = P("dp", "cp", None)
    mat = P(both, None)
    vec = P(both)
    return jax.shard_map(
        shards,
        mesh=mesh,
        in_specs=(rows, vec, mat, mat, mat, mat, vec, mat, mat, mat, rows),
        out_specs=(rows, rows, vec, mat, mat, mat, mat, vec, mat, mat, mat),
        check_vma=False,
    )
```

```python
import functools
import math

import jax
import jax.numpy as jnp
from jax import lax
from jax.experimental import pallas as pl
from jax.experimental.pallas import tpu as pltpu
from jax.sharding import PartitionSpec as P

H = 16
KVH = 8
HD = 128
EPS = 1e-05
THETA = 1000000.0
SCALE = HD ** (-0.5)
LOG2E = math.log2(math.e)
BF = jnp.bfloat16
F32 = jnp.float32
VMEM_LIMIT = 56 * 1024 * 1024
SHARE = 0.05

NN = (((1,), (0,)), ((), ()))
NT = (((1,), (1,)), ((), ()))
TN = (((0,), (0,)), ((), ()))


def mm(left, right, dims):
    return lax.dot_general(left, right, dims, preferred_element_type=F32)


def offset_of(position, count):
    half = count // 2
    return ((position % half) << 1) | (position // half)


def position_of(offset, count):
    return (offset >> 1) + (offset & 1) * (count // 2)


def after(value, *deps):
    return lax.optimization_barrier((value, *deps))[0]


def swap(value, count, offset):
    return lax.ppermute(value, "cp", [(i, i ^ offset) for i in range(count)])


def gather_rows(part, count, dep=None):
    half = part.shape[0] // 2
    if count == 8:
        by_x = swap(part, count, 2)
        by_y = swap(part, count, 4)
        if dep is not None:
            by_y = after(by_y, *dep)
        near = jnp.concatenate([part, by_x, by_y], 0)
        near_other = swap(near, count, 1)
        far = jnp.concatenate([swap(by_y[:half], count, 2), swap(by_x[half:], count, 4)], 0)
        return jnp.concatenate([near, far, near_other, swap(far, count, 1)], 0)
    inner, bit = part, 2
    while bit < count:
        inner = jnp.concatenate([inner, swap(inner, count, bit)], 0)
        bit *= 2
    return jnp.concatenate([inner, swap(inner, count, 1)], 0)


def plus(left, right):
    return (left.astype(F32) + right.astype(F32)).astype(BF)


def scatter_first(low, high, count, *deps):
    got = swap(high, count, 1)
    return plus(low, after(got, *deps) if deps else got)


def scatter_mid(acc, count, *deps):
    rows = 2 * acc.shape[0] // count
    half = rows // 2
    parts = [acc[i * rows : (i + 1) * rows] for i in range(count // 2)]
    if count == 8:
        own, to_x, to_y, far = parts
        from_x = swap(far[:half], count, 2)
        from_y = swap(far[half:], count, 4)
        if deps:
            from_x, from_y = lax.optimization_barrier((from_x, from_y, *deps))[:2]
        send_x = jnp.concatenate([to_x[:half], plus(to_x[half:], from_y)], 0)
        send_y = jnp.concatenate([plus(to_y[:half], from_x), to_y[half:]], 0)
        return own, send_x, send_y
    bit = count // 2
    while bit > 2:
        keep, give = parts[: len(parts) // 2], parts[len(parts) // 2 :]
        parts = [plus(a, swap(b, count, bit)) for a, b in zip(keep, give)]
        bit //= 2
    return tuple(parts)


def scatter_last(state, count, *deps):
    got = [swap(part, count, offset) for offset, part in zip((2, 4), state[1:])]
    if deps:
        got = lax.optimization_barrier((*got, *deps))[: len(got)]
    total = state[0].astype(F32)
    for part in got:
        total = total + part.astype(F32)
    return total


def deal(count, n_cp, shift):
    return [
        (b, ((b % count + shift) % count) * n_cp + b // count) for b in range(count * n_cp)
    ]


def params(semantics):
    return pltpu.CompilerParams(dimension_semantics=semantics, vmem_limit_bytes=VMEM_LIMIT)


def cost(flops, nbytes, trans=0):
    return pl.CostEstimate(
        flops=int(flops * SHARE), bytes_accessed=int(nbytes * SHARE), transcendentals=int(trans * SHARE)
    )


def turn(value, cos, sin):
    return value * cos + pltpu.roll(value, HD // 2, 1) * sin


def qkv_kernel(z_ref, w_ref, cos_ref, sin_ref, q_ref, k_ref, v_ref, kt_ref, vt_ref, *, heads):
    cos, sin = cos_ref[...], sin_ref[...]
    flat = None
    depth = z_ref.shape[1] // w_ref.shape[0]
    for d in range(w_ref.shape[0]):
        term = mm(z_ref[:, d * depth : (d + 1) * depth], w_ref[d, :depth, :], NN)
        flat = term if flat is None else flat + term
    for h in range(heads):
        at = slice(h * HD, (h + 1) * HD)
        q_ref[:, at] = turn(flat[:, at], cos, sin).astype(BF)
    key = turn(flat[:, heads * HD : (heads + 1) * HD], cos, sin)
    value = flat[:, (heads + 1) * HD :]
    k_ref[...] = key.astype(BF)
    v_ref[...] = value.astype(BF)
    kt_ref[...] = key.T.astype(BF)
    vt_ref[...] = value.T.astype(BF)


def qkv_call(z_one, w_qkv, cos, sin, rows, heads):
    total, width = z_one.shape
    cols = w_qkv.shape[2]
    row = lambda i: (i, 0)
    col = lambda i: (0, i)
    whole = lambda i: (0, 0)
    return pl.pallas_call(
        functools.partial(qkv_kernel, heads=heads),
        grid=(total // rows,),
        in_specs=[
            pl.BlockSpec((rows, width), row),
            pl.BlockSpec(w_qkv.shape, lambda i: (0, 0, 0)),
            pl.BlockSpec((rows, HD), row),
            pl.BlockSpec((rows, HD), row),
        ],
        out_specs=[
            pl.BlockSpec((rows, heads * HD), row),
            pl.BlockSpec((rows, HD), row),
            pl.BlockSpec((rows, HD), row),
            pl.BlockSpec((HD, rows), col),
            pl.BlockSpec((HD, rows), col),
        ],
        out_shape=[
            jax.ShapeDtypeStruct((total, heads * HD), BF),
            jax.ShapeDtypeStruct((total, HD), BF),
            jax.ShapeDtypeStruct((total, HD), BF),
            jax.ShapeDtypeStruct((HD, total), BF),
            jax.ShapeDtypeStruct((HD, total), BF),
        ],
        compiler_params=params(("arbitrary",)),
        cost_estimate=cost(2 * total * width * cols, 2 * (total * width + width * cols)),
        name="qkv",
    )(z_one, w_qkv, cos, sin)


def stack_heads(block, heads):
    if heads == 1:
        return block
    return jnp.concatenate([block[:, h * HD : (h + 1) * HD] for h in range(heads)], 0)


def diagonal_mask(rows, heads):
    key_at = lax.broadcasted_iota(jnp.int32, (rows, rows), 0)
    query_at = lax.broadcasted_iota(jnp.int32, (rows, rows), 1)
    one = key_at <= query_at
    return one if heads == 1 else jnp.concatenate([one] * heads, 1)


def attend_kernel(me_ref, q_ref, k_ref, vt_ref, o_ref, lse_ref, *, heads, rows, count):
    i = pl.program_id(0)
    me = me_ref[0]
    wide = heads * rows
    queries = stack_heads(q_ref[...], heads)

    def step(j, carry, masked):
        top, total, acc = carry
        at = pl.multiple_of(position_of(j ^ me, count) * rows, rows)
        s = mm(k_ref[pl.ds(at, rows), :], queries, NT) * (SCALE * LOG2E)
        if masked:
            s = jnp.where(diagonal_mask(rows, heads), s, -1e30)
        new_top = jnp.maximum(top, jnp.max(s, 0, keepdims=True))
        fade = jnp.exp2(top - new_top)
        p = jnp.exp2(s - new_top)
        total = total * fade + jnp.sum(p, 0, keepdims=True)
        acc = acc * fade + mm(vt_ref[:, pl.ds(at, rows)], p.astype(BF), NN)
        return new_top, total, acc

    carry = (
        jnp.full((1, wide), -1e30, F32),
        jnp.zeros((1, wide), F32),
        jnp.zeros((HD, wide), F32),
    )
    carry = step(i, carry, True)
    top, total, acc = lax.fori_loop(0, i, lambda j, c: step(j, c, False), carry)
    out = (acc / total).T
    for h in range(heads):
        o_ref[:, h * HD : (h + 1) * HD] = out[h * rows : (h + 1) * rows, :].astype(BF)
    lse_ref[0] = top + jnp.log2(total)


def attend_call(me, q, k, vt, rows, heads, count):
    total = q.shape[0]
    slot = lambda i, me_ref: (position_of(i ^ me_ref[0], count), 0)
    true = lambda i, me_ref: (i, 0)
    true3 = lambda i, me_ref: (i, 0, 0)
    whole = lambda i, me_ref: (0, 0)
    return pl.pallas_call(
        functools.partial(attend_kernel, heads=heads, rows=rows, count=count),
        grid_spec=pltpu.PrefetchScalarGridSpec(
            num_scalar_prefetch=1,
            grid=(count,),
            in_specs=[
                pl.BlockSpec((rows, heads * HD), slot),
                pl.BlockSpec((total, HD), whole),
                pl.BlockSpec((HD, total), whole),
            ],
            out_specs=[
                pl.BlockSpec((rows, heads * HD), true),
                pl.BlockSpec((1, 1, heads * rows), true3),
            ],
        ),
        out_shape=[
            jax.ShapeDtypeStruct((total, heads * HD), BF),
            jax.ShapeDtypeStruct((count, 1, heads * rows), F32),
        ],
        compiler_params=params(("arbitrary",)),
        cost_estimate=cost(4 * total * total * heads * HD, 8 * total * HD, heads * total * total // 2),
        name="attend",
    )(me, q, k, vt)


def attend_back_kernel(
    me_ref,
    q_ref,
    g_ref,
    o_ref,
    lse_ref,
    k_ref,
    kt_ref,
    v_ref,
    cos_ref,
    sin_ref,
    out_ref,
    dk_ref,
    dv_ref,
    *,
    heads,
    rows,
    count,
):
    i = pl.program_id(0)
    me = me_ref[0]
    wide = heads * rows

    @pl.when(i == 0)
    def _():
        dk_ref[...] = jnp.zeros_like(dk_ref)
        dv_ref[...] = jnp.zeros_like(dv_ref)

    queries = stack_heads(q_ref[...], heads)
    grads = stack_heads(g_ref[...], heads)
    outs = stack_heads(o_ref[...], heads)
    lse = lse_ref[0]
    mixed = jnp.sum((outs.astype(F32) * grads.astype(F32)).T, 0, keepdims=True)

    def step(j, dqt, masked):
        at = pl.multiple_of(position_of(j ^ me, count) * rows, rows)
        here = pl.ds(at, rows)
        s = mm(k_ref[here, :], queries, NT) * (SCALE * LOG2E)
        p = jnp.exp2(s - lse)
        if masked:
            p = jnp.where(diagonal_mask(rows, heads), p, 0.0)
        gp = mm(v_ref[here, :], grads, NT)
        gs = (p * (gp - mixed) * SCALE).astype(BF)
        dv_ref[here, :] += mm(p.astype(BF), grads, NN)
        dk_ref[here, :] += mm(gs, queries, NN)
        return dqt + mm(kt_ref[:, here], gs, NN)

    dqt = step(i, jnp.zeros((HD, wide), F32), True)
    dqt = lax.fori_loop(0, i, lambda j, c: step(j, c, False), dqt)
    dq = dqt.T
    mine = pl.ds(pl.multiple_of(position_of(i ^ me, count) * rows, rows), rows)
    cos, sin = cos_ref[mine, :], sin_ref[mine, :]
    for h in range(heads):
        one = turn(dq[h * rows : (h + 1) * rows, :], cos, -sin)
        out_ref[mine, h * HD : (h + 1) * HD] = one.astype(BF)

    @pl.when(i == count - 1)
    def _():
        out_ref[:, heads * HD : (heads + 1) * HD] = turn(
            dk_ref[...], cos_ref[...], -sin_ref[...]
        ).astype(BF)
        out_ref[:, (heads + 1) * HD :] = dv_ref[...].astype(BF)


def attend_back_call(me, q, g, o, lse, k, kt, v, cos, sin, rows, heads, count):
    total = q.shape[0]
    slot = lambda i, me_ref: (position_of(i ^ me_ref[0], count), 0)
    true = lambda i, me_ref: (i, 0)
    true3 = lambda i, me_ref: (i, 0, 0)
    whole = lambda i, me_ref: (0, 0)
    cols = (heads + 2) * HD
    return pl.pallas_call(
        functools.partial(attend_back_kernel, heads=heads, rows=rows, count=count),
        grid_spec=pltpu.PrefetchScalarGridSpec(
            num_scalar_prefetch=1,
            grid=(count,),
            in_specs=[
                pl.BlockSpec((rows, heads * HD), slot),
                pl.BlockSpec((rows, heads * HD), true),
                pl.BlockSpec((rows, heads * HD), true),
                pl.BlockSpec((1, 1, heads * rows), true3),
                pl.BlockSpec((total, HD), whole),
                pl.BlockSpec((HD, total), whole),
                pl.BlockSpec((total, HD), whole),
                pl.BlockSpec((total, HD), whole),
                pl.BlockSpec((total, HD), whole),
            ],
            out_specs=pl.BlockSpec((total, cols), whole),
            scratch_shapes=[pltpu.VMEM((total, HD), F32), pltpu.VMEM((total, HD), F32)],
        ),
        out_shape=jax.ShapeDtypeStruct((total, cols), BF),
        compiler_params=params(("arbitrary",)),
        cost_estimate=cost(10 * total * total * heads * HD, 16 * total * HD, heads * total * total // 2),
        name="attend_back",
    )(me, q, g, o, lse, k, kt, v, cos, sin)


def back_act_kernel(g_ref, d_ref, out_ref):
    out_ref[...] = mm(g_ref[...], d_ref[...], NT)


def back_act_call(g_out, w_down, rows):
    total, width = g_out.shape
    cols = w_down.shape[0]
    return pl.pallas_call(
        back_act_kernel,
        grid=(total // rows,),
        in_specs=[
            pl.BlockSpec((rows, width), lambda i: (i, 0)),
            pl.BlockSpec((cols, width), lambda i: (0, 0)),
        ],
        out_specs=pl.BlockSpec((rows, cols), lambda i: (i, 0)),
        out_shape=jax.ShapeDtypeStruct((total, cols), F32),
        compiler_params=params(("arbitrary",)),
        cost_estimate=cost(2 * total * width * cols, 2 * total * width + 2 * cols * width + 4 * total * cols),
        name="back_act",
    )(g_out, w_down)


def feed_kernel(z_ref, g_ref, w_ref, act_ref, grads_ref):
    cut = g_ref.shape[1]
    z = z_ref[...]
    gate = mm(z, w_ref[:, :cut], NN)
    up = mm(z, w_ref[:, cut:], NN)
    back = g_ref[...]
    sig = jax.nn.sigmoid(gate)
    silu = gate * sig
    act_ref[...] = (silu * up).astype(BF)
    grads_ref[:, :cut] = (back * up * (sig * (1.0 + gate * (1.0 - sig)))).astype(BF)
    grads_ref[:, cut:] = (back * silu).astype(BF)


def feed_call(z_two, g_act, w_gu, part, rows):
    total, width = z_two.shape
    cut = w_gu.shape[1] // 2
    row = lambda i: (i, 0)
    whole = lambda i: (0, 0)
    return pl.pallas_call(
        feed_kernel,
        grid=(total // rows,),
        in_specs=[
            pl.BlockSpec((rows, width), row),
            pl.BlockSpec((rows, cut), lambda i: (i, part)),
            pl.BlockSpec((width, 2 * cut), whole),
        ],
        out_specs=[pl.BlockSpec((rows, cut), row), pl.BlockSpec((rows, 2 * cut), row)],
        out_shape=[
            jax.ShapeDtypeStruct((total, cut), BF),
            jax.ShapeDtypeStruct((total, 2 * cut), BF),
        ],
        compiler_params=params(("arbitrary",)),
        cost_estimate=cost(4 * total * width * cut, 2 * total * width + 4 * cut * width + 10 * total * cut),
        name="feed",
    )(z_two, g_act, w_gu)


def sum_kernel(*refs, dims):
    *ins, low_ref, high_ref = refs
    acc = None
    for a_ref, b_ref in zip(ins[0::2], ins[1::2]):
        term = mm(a_ref[...], b_ref[...], dims)
        acc = term if acc is None else acc + term
    acc = acc.astype(BF)
    half = pl.num_programs(0) // 2

    @pl.when(pl.program_id(0) < half)
    def _():
        high_ref[...] = acc

    @pl.when(pl.program_id(0) >= half)
    def _():
        low_ref[...] = acc


def sum_call(pairs, dims, rows, name):
    total = pairs[0][0].shape[0]
    cols = pairs[0][1].shape[1 if dims is NN else 0]
    steps = total // rows
    half = steps // 2
    row = lambda i: ((i + half) % steps, 0)
    low = lambda i: (jnp.maximum(i - half, 0), 0)
    high = lambda i: (jnp.minimum(i, half - 1), 0)
    whole = lambda i: (0, 0)
    specs, flat, depth = [], [], 0
    for a, b in pairs:
        specs += [pl.BlockSpec((rows, a.shape[1]), row), pl.BlockSpec(b.shape, whole)]
        flat += [a, b]
        depth += a.shape[1]
    return pl.pallas_call(
        functools.partial(sum_kernel, dims=dims),
        grid=(total // rows,),
        in_specs=specs,
        out_specs=[pl.BlockSpec((rows, cols), low), pl.BlockSpec((rows, cols), high)],
        out_shape=[jax.ShapeDtypeStruct((total // 2, cols), BF)] * 2,
        compiler_params=params(("arbitrary",)),
        cost_estimate=cost(2 * total * cols * depth, 2 * (total * depth + depth * cols + total * cols)),
        name=name,
    )(*flat)


def split_rows(count):
    half = count // 2
    row = lambda i: (i + half) % count
    low = lambda i: jnp.maximum(i - half, 0)
    high = lambda i: jnp.minimum(i, half - 1)
    return half, row, low, high


def hidden_kernel(me_ref, a_ref, w_ref, x_ref, hid_ref, z_ref, rms_ref):
    p = pl.program_id(0)

    @pl.when(p == 0)
    def _():
        hid_ref[...] = x_ref[...].astype(F32)

    hid_ref[...] += mm(a_ref[0], w_ref[...], NN)

    @pl.when(p == pl.num_programs(0) - 1)
    def _():
        hid = hid_ref[...]
        rms = rms_of(hid)
        rms_ref[...] = rms
        z_ref[...] = (hid * rms).astype(BF)


def hidden_call(me, attn, wo, x, count):
    _, rows, feat = attn.shape
    width = wo.shape[1]
    true3 = lambda p, me_ref: (offset_of(p, count) ^ me_ref[0], 0, 0)
    block = lambda p, me_ref: (p, 0)
    whole = lambda p, me_ref: (0, 0)
    return pl.pallas_call(
        hidden_kernel,
        grid_spec=pltpu.PrefetchScalarGridSpec(
            num_scalar_prefetch=1,
            grid=(count,),
            in_specs=[
                pl.BlockSpec((1, rows, feat), true3),
                pl.BlockSpec((feat, width), block),
                pl.BlockSpec((rows, width), whole),
            ],
            out_specs=[
                pl.BlockSpec((rows, width), whole),
                pl.BlockSpec((rows, width), whole),
                pl.BlockSpec((rows, 1), whole),
            ],
        ),
        out_shape=[
            jax.ShapeDtypeStruct((rows, width), F32),
            jax.ShapeDtypeStruct((rows, width), BF),
            jax.ShapeDtypeStruct((rows, 1), F32),
        ],
        compiler_params=params(("arbitrary",)),
        cost_estimate=cost(2 * rows * feat * count * width, 2 * feat * count * width + 10 * rows * width),
        name="hidden",
    )(me, attn, wo, x)


def back_attn_kernel(me_ref, g_ref, w_ref, out_ref):
    out_ref[0] = mm(g_ref[...], w_ref[...], NT).astype(BF)


def back_attn_call(me, g, wo, count):
    rows, width = g.shape
    feat = wo.shape[0] // count
    true3 = lambda p, me_ref: (offset_of(p, count) ^ me_ref[0], 0, 0)
    block = lambda p, me_ref: (p, 0)
    whole = lambda p, me_ref: (0, 0)
    return pl.pallas_call(
        back_attn_kernel,
        grid_spec=pltpu.PrefetchScalarGridSpec(
            num_scalar_prefetch=1,
            grid=(count,),
            in_specs=[pl.BlockSpec((rows, width), whole), pl.BlockSpec((feat, width), block)],
            out_specs=pl.BlockSpec((1, rows, feat), true3),
        ),
        out_shape=jax.ShapeDtypeStruct((count, rows, feat), BF),
        compiler_params=params(("arbitrary",)),
        cost_estimate=cost(2 * rows * feat * count * width, 2 * feat * count * width + 4 * rows * width),
        name="back_attn",
    )(me, g, wo)


def grad_wo_kernel(me_ref, a_ref, g_ref, low_ref, high_ref):
    out = mm(a_ref[0], g_ref[...], TN).astype(BF)
    half = pl.num_programs(0) // 2

    @pl.when(pl.program_id(0) < half)
    def _():
        high_ref[...] = out

    @pl.when(pl.program_id(0) >= half)
    def _():
        low_ref[...] = out


def grad_wo_call(me, attn, g, count):
    _, rows, feat = attn.shape
    width = g.shape[1]
    half, row, low, high = split_rows(count)
    return pl.pallas_call(
        grad_wo_kernel,
        grid_spec=pltpu.PrefetchScalarGridSpec(
            num_scalar_prefetch=1,
            grid=(count,),
            in_specs=[
                pl.BlockSpec(
                    (1, rows, feat), lambda p, me_ref: (offset_of(row(p), count) ^ me_ref[0], 0, 0)
                ),
                pl.BlockSpec((rows, width), lambda p, me_ref: (0, 0)),
            ],
            out_specs=[
                pl.BlockSpec((feat, width), lambda p, me_ref: (low(p), 0)),
                pl.BlockSpec((feat, width), lambda p, me_ref: (high(p), 0)),
            ],
        ),
        out_shape=[jax.ShapeDtypeStruct((half * feat, width), BF)] * 2,
        compiler_params=params(("arbitrary",)),
        cost_estimate=cost(2 * rows * feat * count * width, 2 * feat * count * width + 4 * rows * width),
        name="grad_wo",
    )(me, attn, g)


def finish_feed_kernel(*refs, halves, per_half, unit, count):
    gots, (wg_ref, wu_ref, gain_ref, g_ref, u_ref, sum_ref) = refs[:halves], refs[halves:]
    gain = gain_ref[...]
    total = None
    for h, got_ref in enumerate(gots):
        for kind, (w_ref, out_ref) in enumerate(((wg_ref, g_ref), (wu_ref, u_ref))):
            for i in range(per_half):
                frm = (kind * per_half + i) * unit
                for t in range(count):
                    at = ((h * per_half + i) * count + t) * unit
                    raw = got_ref[t, :, frm : frm + unit].astype(F32)
                    out_ref[:, at : at + unit] = raw * gain
                    term = raw * w_ref[:, at : at + unit].astype(F32)
                    total = term if total is None else total + term
    sum_ref[...] = jnp.sum(total, 1, keepdims=True)


def finish_feed_call(gots, w_gate, w_up, gain, per_half, unit):
    own, hidden = w_gate.shape
    return pl.pallas_call(
        functools.partial(
            finish_feed_kernel,
            halves=len(gots),
            per_half=per_half,
            unit=unit,
            count=gots[0].shape[0],
        ),
        out_shape=[
            jax.ShapeDtypeStruct((own, hidden), F32),
            jax.ShapeDtypeStruct((own, hidden), F32),
            jax.ShapeDtypeStruct((own, 1), F32),
        ],
        compiler_params=pltpu.CompilerParams(vmem_limit_bytes=VMEM_LIMIT),
        cost_estimate=cost(8 * own * hidden, 16 * own * hidden),
        name="finish_feed",
    )(*gots, w_gate, w_up, gain)


def finish_qkv_kernel(
    got_ref, wq_ref, wk_ref, wv_ref, gain_ref, q_ref, k_ref, v_ref, sum_ref, *, heads, reps
):
    gain = gain_ref[...]
    total = None
    feat = heads * HD
    for t in range(got_ref.shape[0]):
        raw = got_ref[t, :, :feat].astype(F32)
        at = slice(t * feat, (t + 1) * feat)
        q_ref[:, at] = raw * gain
        term = jnp.sum(raw * wq_ref[:, at].astype(F32), 1, keepdims=True)
        total = term if total is None else total + term
    for kind, (w_ref, out_ref) in enumerate(((wk_ref, k_ref), (wv_ref, v_ref))):
        frm = slice(feat + kind * HD, feat + (kind + 1) * HD)
        for t in range(got_ref.shape[0] // reps):
            raw = got_ref[t * reps, :, frm].astype(F32)
            for r in range(1, reps):
                raw = raw + got_ref[t * reps + r, :, frm].astype(F32)
            at = slice(t * HD, (t + 1) * HD)
            out_ref[:, at] = raw * gain
            total = total + jnp.sum(raw * w_ref[:, at].astype(F32), 1, keepdims=True)
    sum_ref[...] = total


def finish_qkv_call(got, w_query, w_key, w_value, gain, heads, reps):
    own = w_query.shape[0]
    like = lambda w: jax.ShapeDtypeStruct(w.shape, F32)
    return pl.pallas_call(
        functools.partial(finish_qkv_kernel, heads=heads, reps=reps),
        out_shape=[like(w_query), like(w_key), like(w_value), jax.ShapeDtypeStruct((own, 1), F32)],
        compiler_params=pltpu.CompilerParams(vmem_limit_bytes=VMEM_LIMIT),
        cost_estimate=cost(8 * own * w_query.shape[1], 16 * own * w_query.shape[1]),
        name="finish_qkv",
    )(got, w_query, w_key, w_value, gain)


def rms_of(values):
    return lax.rsqrt(jnp.mean(values * values, -1, keepdims=True) + EPS)


def shards(
    inputs, attn_gain, w_query, w_key, w_value, w_output, ffn_gain, w_gate, w_up, w_down, cotangent
):
    _, rows, width = inputs.shape
    n_cp = lax.axis_size("cp")
    n_dp = lax.axis_size("dp")
    me = lax.axis_index("cp")
    heads = H // n_cp
    reps = n_cp // KVH
    total = rows * n_cp
    own = w_query.shape[0]
    hidden = w_gate.shape[1]
    unit = hidden // (n_dp * n_cp)
    halves = 2
    per_half = n_dp // halves
    me_arr = jnp.reshape(me, (1,)).astype(jnp.int32)
    gain_one = attn_gain.astype(F32)[:, None]
    gain_two = ffn_gain.astype(F32)[:, None]

    def gather_z(value):
        return lax.all_gather(value, "dp", axis=0, tiled=True)

    def scatter_z(value):
        return lax.psum_scatter(value, "dp", scatter_dimension=0, tiled=True)

    def give(value):
        return lax.all_to_all(value, "cp", 0, 0)

    scaled_q = (w_query.astype(F32) * gain_one).astype(BF).reshape(own, n_cp, heads * HD)
    scaled_k = (w_key.astype(F32) * gain_one).astype(BF).reshape(own, KVH, 1, HD)
    scaled_v = (w_value.astype(F32) * gain_one).astype(BF).reshape(own, KVH, 1, HD)
    spread = lambda v: jnp.broadcast_to(v, (own, KVH, reps, HD)).reshape(own, n_cp, HD)
    qkv_own = jnp.concatenate([scaled_q, spread(scaled_k), spread(scaled_v)], 2).transpose(1, 0, 2)
    qkv_cols = (heads + 2) * HD
    qkv_rows = give(qkv_own).reshape(n_cp * own, qkv_cols)
    wo_own = lax.ppermute(w_output, ("dp", "cp"), deal(n_dp, n_cp, 0))
    depth = n_cp * own
    if own * width % qkv_cols == 0:
        joint = jnp.concatenate([qkv_rows, wo_own.reshape(-1, qkv_cols)], 0)
        joint = gather_z(joint).reshape(n_dp, -1, qkv_cols)
        wo_rows = joint[:, depth:].reshape(n_dp * own, width)
    else:
        joint = gather_z(qkv_rows).reshape(n_dp, -1, qkv_cols)
        wo_rows = gather_z(wo_own)

    w_down_full = gather_z(w_down)
    scaled_g = (w_gate.astype(F32) * gain_two).astype(BF).reshape(own, n_dp, n_cp, unit)
    scaled_u = (w_up.astype(F32) * gain_two).astype(BF).reshape(own, n_dp, n_cp, unit)
    cut = per_half * unit
    w_gu, w_dn, last, given = [], [], qkv_rows, []
    for h in range(halves):
        at = slice(h * per_half, (h + 1) * per_half)
        both = jnp.concatenate([scaled_g[:, at], scaled_u[:, at]], 1)
        both = both.transpose(2, 0, 1, 3).reshape(n_cp, own, 2 * cut)
        last = give(after(both, last))
        given.append(last)
        w_gu.append(gather_z(last.reshape(n_cp * own, 2 * cut)))
        w_dn.append(w_down_full[h * cut : (h + 1) * cut])

    shard_at = jnp.array([offset_of(p, n_cp) for p in range(n_cp)], jnp.int32) ^ me
    positions = (shard_at[:, None] * rows + jnp.arange(rows, dtype=jnp.int32)[None, :]).reshape(-1)
    half_dim = HD // 2
    inv_freq = THETA ** (-(jnp.arange(half_dim, dtype=F32) * 2.0 / HD))
    angles = positions.astype(F32)[:, None] * inv_freq[None, :]
    cos_half, sin_half = jnp.cos(angles), jnp.sin(angles)
    cos = jnp.concatenate([cos_half, cos_half], -1)
    sin = jnp.concatenate([-sin_half, sin_half], -1)

    xb = inputs.reshape(rows, width)
    x = xb.astype(F32)
    rms_one = rms_of(x)
    z_one = x * rms_one
    z_one_all = gather_rows(z_one.astype(BF), n_cp, [cos, sin] + given)
    wo_rel = gather_rows(wo_rows, n_cp)
    g_outb = cotangent.reshape(rows, width)
    g_out = g_outb.astype(F32)
    g_out_all = gather_rows(after(g_outb, z_one_all), n_cp)

    q, k, v, kt, vt = qkv_call(z_one_all, joint, cos, sin, rows, heads)
    mixed, lse = attend_call(me_arr, q, k, vt, rows, heads, n_cp)
    feat = heads * HD
    attn = give(mixed.reshape(n_cp, rows, feat))
    hid, z_two_b, rms_two = hidden_call(me_arr, attn, wo_rel, xb, n_cp)
    g_act = back_act_call(after(g_out_all, z_two_b), w_down_full, rows)
    z_two_all = gather_rows(z_two_b, n_cp)

    acts, gus, red_gu = [], [], []
    for h in range(halves):
        z_in = after(z_two_all, part_gu) if h else z_two_all
        act, gu = feed_call(z_in, g_act, w_gu[h], h, rows)
        acts.append(act)
        gus.append(gu)
        if h == 0:
            part_gu = mm(z_two_all, gu, TN).astype(BF)
            red_gu.append(scatter_z(part_gu))
    part = sum_call([(gus[h], w_gu[h]) for h in range(halves)], NT, rows, "g_two")
    part_gu = mm(z_two_all, after(gus[1], *part), TN).astype(BF)
    red_gu.append(scatter_z(part_gu))
    acc = scatter_first(*part, n_cp, part_gu)
    out_part = sum_call([(after(acts[h], acc), w_dn[h]) for h in range(halves)], NN, rows, "out")
    state = scatter_mid(acc, n_cp, *out_part)
    downs = [mm(after(act, *state), g_out_all, TN).astype(BF) for act in acts]
    grad_down = scatter_z(after(jnp.concatenate(downs, 0), red_gu[0]))
    out_acc = scatter_first(*out_part, n_cp, *downs)
    u = scatter_last(state, n_cp, out_acc)

    z_two = hid * rms_two
    g_hidden = g_out + rms_two * (u - z_two * jnp.mean(u * z_two, -1, keepdims=True))
    g_hidb = g_hidden.astype(BF)
    g_heads = back_attn_call(me_arr, g_hidb, wo_rel, n_cp)
    g_mixed = give(g_heads).reshape(total, feat)
    wo_part = grad_wo_call(me_arr, attn, after(g_hidb, g_heads), n_cp)
    back_gu = [give(after(red_gu[0].reshape(n_cp, own, 2 * cut), g_mixed))]
    lse = after(lse, *wo_part)
    g_qkv = attend_back_call(me_arr, q, g_mixed, mixed, lse, k, kt, v, cos, sin, rows, heads, n_cp)
    out_state = scatter_mid(after(out_acc, g_mixed), n_cp, g_qkv)
    wo_acc = scatter_first(*wo_part, n_cp, g_qkv)
    part_qkv = mm(z_one_all, after(g_qkv, wo_acc, red_gu[1], *out_state), TN).astype(BF)
    red_qkv = scatter_z(part_qkv)
    back_gu.append(give(after(red_gu[1].reshape(n_cp, own, 2 * cut), g_qkv)))
    wo_state = scatter_mid(wo_acc, n_cp, part_qkv)
    w_qkv = joint[:, :depth].reshape(width, qkv_cols)
    part = sum_call([(after(g_qkv, back_gu[0], *wo_state), w_qkv)], NT, rows, "g_one")
    out_sum = scatter_last(out_state, n_cp)
    output = hid + out_sum
    w_acc = scatter_first(*part, n_cp, back_gu[1], out_sum)
    wo_sum = scatter_last(wo_state, n_cp, w_acc).astype(BF)
    w_state = scatter_mid(w_acc, n_cp)

    wo_sum = scatter_z(after(wo_sum, grad_down))
    got = give(red_qkv.reshape(n_cp, own, qkv_cols))
    back_pairs = [(b, a) for a, b in deal(n_dp, n_cp, 0)]
    grad_output = lax.ppermute(wo_sum, ("dp", "cp"), back_pairs).astype(F32)
    w_one = scatter_last(w_state, n_cp, got)
    grad_in = g_hidden + rms_one * (w_one - z_one * jnp.mean(w_one * z_one, -1, keepdims=True))

    grad_g, grad_u, gain_two_sum = finish_feed_call(back_gu, w_gate, w_up, gain_two, per_half, unit)
    grad_q, grad_k, grad_v, gain_one_sum = finish_qkv_call(
        got, w_query, w_key, w_value, gain_one, heads, reps
    )

    return (
        output[None],
        grad_in[None],
        gain_one_sum[:, 0],
        grad_q,
        grad_k,
        grad_v,
        grad_output,
        gain_two_sum[:, 0],
        grad_g,
        grad_u,
        grad_down.astype(F32),
    )


def solution(mesh):
    both = ("dp", "cp")
    rows = P("dp", "cp", None)
    mat = P(both, None)
    vec = P(both)
    return jax.shard_map(
        shards,
        mesh=mesh,
        in_specs=(rows, vec, mat, mat, mat, mat, vec, mat, mat, mat, rows),
        out_specs=(rows, rows, vec, mat, mat, mat, mat, vec, mat, mat, mat),
        check_vma=False,
    )
```

```python
import functools
import math

import jax
import jax.numpy as jnp
from jax import lax
from jax.experimental import pallas as pl
from jax.experimental.pallas import tpu as pltpu
from jax.sharding import PartitionSpec as P

H = 16
KVH = 8
HD = 128
EPS = 1e-05
THETA = 1000000.0
SCALE = HD ** (-0.5)
LOG2E = math.log2(math.e)
BF = jnp.bfloat16
F32 = jnp.float32
VMEM_LIMIT = 56 * 1024 * 1024
SHARE = 0.05

NN = (((1,), (0,)), ((), ()))
NT = (((1,), (1,)), ((), ()))
TN = (((0,), (0,)), ((), ()))


def mm(left, right, dims):
    return lax.dot_general(left, right, dims, preferred_element_type=F32)


def offset_of(position, count):
    half = count // 2
    return ((position % half) << 1) | (position // half)


def position_of(offset, count):
    return (offset >> 1) + (offset & 1) * (count // 2)


def after(value, *deps):
    return lax.optimization_barrier((value, *deps))[0]


def swap(value, count, offset):
    return lax.ppermute(value, "cp", [(i, i ^ offset) for i in range(count)])


def gather_rows(part, count, dep=None):
    half = part.shape[0] // 2
    if count == 8:
        by_x = swap(part, count, 2)
        by_y = swap(part, count, 4)
        if dep is not None:
            by_y = after(by_y, *dep)
        near = jnp.concatenate([part, by_x, by_y], 0)
        near_other = swap(near, count, 1)
        far = jnp.concatenate([swap(by_y[:half], count, 2), swap(by_x[half:], count, 4)], 0)
        return jnp.concatenate([near, far, near_other, swap(far, count, 1)], 0)
    inner, bit = part, 2
    while bit < count:
        inner = jnp.concatenate([inner, swap(inner, count, bit)], 0)
        bit *= 2
    return jnp.concatenate([inner, swap(inner, count, 1)], 0)


def plus(left, right):
    return (left.astype(F32) + right.astype(F32)).astype(BF)


def scatter_first(low, high, count, *deps):
    got = swap(high, count, 1)
    return plus(low, after(got, *deps) if deps else got)


def scatter_mid(acc, count, *deps):
    rows = 2 * acc.shape[0] // count
    half = rows // 2
    parts = [acc[i * rows : (i + 1) * rows] for i in range(count // 2)]
    if count == 8:
        own, to_x, to_y, far = parts
        from_x = swap(far[:half], count, 2)
        from_y = swap(far[half:], count, 4)
        if deps:
            from_x, from_y = lax.optimization_barrier((from_x, from_y, *deps))[:2]
        send_x = jnp.concatenate([to_x[:half], plus(to_x[half:], from_y)], 0)
        send_y = jnp.concatenate([plus(to_y[:half], from_x), to_y[half:]], 0)
        return own, send_x, send_y
    bit = count // 2
    while bit > 2:
        keep, give = parts[: len(parts) // 2], parts[len(parts) // 2 :]
        parts = [plus(a, swap(b, count, bit)) for a, b in zip(keep, give)]
        bit //= 2
    return tuple(parts)


def scatter_last(state, count, *deps):
    got = [swap(part, count, offset) for offset, part in zip((2, 4), state[1:])]
    if deps:
        got = lax.optimization_barrier((*got, *deps))[: len(got)]
    total = state[0].astype(F32)
    for part in got:
        total = total + part.astype(F32)
    return total


def deal(count, n_cp, shift):
    return [
        (b, ((b % count + shift) % count) * n_cp + b // count) for b in range(count * n_cp)
    ]


def params(semantics):
    return pltpu.CompilerParams(dimension_semantics=semantics, vmem_limit_bytes=VMEM_LIMIT)


def cost(flops, nbytes, trans=0):
    return pl.CostEstimate(
        flops=int(flops * SHARE), bytes_accessed=int(nbytes * SHARE), transcendentals=int(trans * SHARE)
    )


def turn(value, cos, sin):
    return value * cos + pltpu.roll(value, HD // 2, 1) * sin


def qkv_kernel(z_ref, w_ref, cos_ref, sin_ref, q_ref, k_ref, v_ref, kt_ref, vt_ref, *, heads):
    cos, sin = cos_ref[...], sin_ref[...]
    flat = None
    depth = z_ref.shape[1] // w_ref.shape[0]
    for d in range(w_ref.shape[0]):
        term = mm(z_ref[:, d * depth : (d + 1) * depth], w_ref[d, :depth, :], NN)
        flat = term if flat is None else flat + term
    for h in range(heads):
        at = slice(h * HD, (h + 1) * HD)
        q_ref[:, at] = turn(flat[:, at], cos, sin).astype(BF)
    key = turn(flat[:, heads * HD : (heads + 1) * HD], cos, sin)
    value = flat[:, (heads + 1) * HD :]
    k_ref[...] = key.astype(BF)
    v_ref[...] = value.astype(BF)
    kt_ref[...] = key.T.astype(BF)
    vt_ref[...] = value.T.astype(BF)


def qkv_call(z_one, w_qkv, cos, sin, rows, heads):
    total, width = z_one.shape
    cols = w_qkv.shape[2]
    row = lambda i: (i, 0)
    col = lambda i: (0, i)
    whole = lambda i: (0, 0)
    return pl.pallas_call(
        functools.partial(qkv_kernel, heads=heads),
        grid=(total // rows,),
        in_specs=[
            pl.BlockSpec((rows, width), row),
            pl.BlockSpec(w_qkv.shape, lambda i: (0, 0, 0)),
            pl.BlockSpec((rows, HD), row),
            pl.BlockSpec((rows, HD), row),
        ],
        out_specs=[
            pl.BlockSpec((rows, heads * HD), row),
            pl.BlockSpec((rows, HD), row),
            pl.BlockSpec((rows, HD), row),
            pl.BlockSpec((HD, rows), col),
            pl.BlockSpec((HD, rows), col),
        ],
        out_shape=[
            jax.ShapeDtypeStruct((total, heads * HD), BF),
            jax.ShapeDtypeStruct((total, HD), BF),
            jax.ShapeDtypeStruct((total, HD), BF),
            jax.ShapeDtypeStruct((HD, total), BF),
            jax.ShapeDtypeStruct((HD, total), BF),
        ],
        compiler_params=params(("arbitrary",)),
        cost_estimate=cost(2 * total * width * cols, 2 * (total * width + width * cols)),
        name="qkv",
    )(z_one, w_qkv, cos, sin)


def stack_heads(block, heads):
    if heads == 1:
        return block
    return jnp.concatenate([block[:, h * HD : (h + 1) * HD] for h in range(heads)], 0)


def diagonal_mask(rows, heads):
    key_at = lax.broadcasted_iota(jnp.int32, (rows, rows), 0)
    query_at = lax.broadcasted_iota(jnp.int32, (rows, rows), 1)
    one = key_at <= query_at
    return one if heads == 1 else jnp.concatenate([one] * heads, 1)


def attend_kernel(me_ref, q_ref, k_ref, vt_ref, o_ref, lse_ref, *, heads, rows, count):
    i = pl.program_id(0)
    me = me_ref[0]
    wide = heads * rows
    queries = stack_heads(q_ref[...], heads)

    def step(j, carry, masked):
        top, total, acc = carry
        at = pl.multiple_of(position_of(j ^ me, count) * rows, rows)
        s = mm(k_ref[pl.ds(at, rows), :], queries, NT) * (SCALE * LOG2E)
        if masked:
            s = jnp.where(diagonal_mask(rows, heads), s, -1e30)
        new_top = jnp.maximum(top, jnp.max(s, 0, keepdims=True))
        fade = jnp.exp2(top - new_top)
        p = jnp.exp2(s - new_top)
        total = total * fade + jnp.sum(p, 0, keepdims=True)
        acc = acc * fade + mm(vt_ref[:, pl.ds(at, rows)], p.astype(BF), NN)
        return new_top, total, acc

    carry = (
        jnp.full((1, wide), -1e30, F32),
        jnp.zeros((1, wide), F32),
        jnp.zeros((HD, wide), F32),
    )
    carry = step(i, carry, True)
    top, total, acc = lax.fori_loop(0, i, lambda j, c: step(j, c, False), carry)
    out = (acc / total).T
    for h in range(heads):
        o_ref[:, h * HD : (h + 1) * HD] = out[h * rows : (h + 1) * rows, :].astype(BF)
    lse_ref[0] = top + jnp.log2(total)


def attend_call(me, q, k, vt, rows, heads, count):
    total = q.shape[0]
    slot = lambda i, me_ref: (position_of(i ^ me_ref[0], count), 0)
    true = lambda i, me_ref: (i, 0)
    true3 = lambda i, me_ref: (i, 0, 0)
    whole = lambda i, me_ref: (0, 0)
    return pl.pallas_call(
        functools.partial(attend_kernel, heads=heads, rows=rows, count=count),
        grid_spec=pltpu.PrefetchScalarGridSpec(
            num_scalar_prefetch=1,
            grid=(count,),
            in_specs=[
                pl.BlockSpec((rows, heads * HD), slot),
                pl.BlockSpec((total, HD), whole),
                pl.BlockSpec((HD, total), whole),
            ],
            out_specs=[
                pl.BlockSpec((rows, heads * HD), true),
                pl.BlockSpec((1, 1, heads * rows), true3),
            ],
        ),
        out_shape=[
            jax.ShapeDtypeStruct((total, heads * HD), BF),
            jax.ShapeDtypeStruct((count, 1, heads * rows), F32),
        ],
        compiler_params=params(("arbitrary",)),
        cost_estimate=cost(4 * total * total * heads * HD, 8 * total * HD, heads * total * total // 2),
        name="attend",
    )(me, q, k, vt)


def attend_back_kernel(
    me_ref,
    q_ref,
    g_ref,
    o_ref,
    lse_ref,
    k_ref,
    kt_ref,
    v_ref,
    cos_ref,
    sin_ref,
    out_ref,
    dk_ref,
    dv_ref,
    *,
    heads,
    rows,
    count,
):
    i = pl.program_id(0)
    me = me_ref[0]
    wide = heads * rows

    @pl.when(i == 0)
    def _():
        dk_ref[...] = jnp.zeros_like(dk_ref)
        dv_ref[...] = jnp.zeros_like(dv_ref)

    queries = stack_heads(q_ref[...], heads)
    grads = stack_heads(g_ref[...], heads)
    outs = stack_heads(o_ref[...], heads)
    lse = lse_ref[0]
    mixed = jnp.sum((outs.astype(F32) * grads.astype(F32)).T, 0, keepdims=True)

    def step(j, dqt, masked):
        at = pl.multiple_of(position_of(j ^ me, count) * rows, rows)
        here = pl.ds(at, rows)
        s = mm(k_ref[here, :], queries, NT) * (SCALE * LOG2E)
        p = jnp.exp2(s - lse)
        if masked:
            p = jnp.where(diagonal_mask(rows, heads), p, 0.0)
        gp = mm(v_ref[here, :], grads, NT)
        gs = (p * (gp - mixed) * SCALE).astype(BF)
        dv_ref[here, :] += mm(p.astype(BF), grads, NN)
        dk_ref[here, :] += mm(gs, queries, NN)
        return dqt + mm(kt_ref[:, here], gs, NN)

    dqt = step(i, jnp.zeros((HD, wide), F32), True)
    dqt = lax.fori_loop(0, i, lambda j, c: step(j, c, False), dqt)
    dq = dqt.T
    mine = pl.ds(pl.multiple_of(position_of(i ^ me, count) * rows, rows), rows)
    cos, sin = cos_ref[mine, :], sin_ref[mine, :]
    for h in range(heads):
        one = turn(dq[h * rows : (h + 1) * rows, :], cos, -sin)
        out_ref[mine, h * HD : (h + 1) * HD] = one.astype(BF)

    @pl.when(i == count - 1)
    def _():
        out_ref[:, heads * HD : (heads + 1) * HD] = turn(
            dk_ref[...], cos_ref[...], -sin_ref[...]
        ).astype(BF)
        out_ref[:, (heads + 1) * HD :] = dv_ref[...].astype(BF)


def attend_back_call(me, q, g, o, lse, k, kt, v, cos, sin, rows, heads, count):
    total = q.shape[0]
    slot = lambda i, me_ref: (position_of(i ^ me_ref[0], count), 0)
    true = lambda i, me_ref: (i, 0)
    true3 = lambda i, me_ref: (i, 0, 0)
    whole = lambda i, me_ref: (0, 0)
    cols = (heads + 2) * HD
    return pl.pallas_call(
        functools.partial(attend_back_kernel, heads=heads, rows=rows, count=count),
        grid_spec=pltpu.PrefetchScalarGridSpec(
            num_scalar_prefetch=1,
            grid=(count,),
            in_specs=[
                pl.BlockSpec((rows, heads * HD), slot),
                pl.BlockSpec((rows, heads * HD), true),
                pl.BlockSpec((rows, heads * HD), true),
                pl.BlockSpec((1, 1, heads * rows), true3),
                pl.BlockSpec((total, HD), whole),
                pl.BlockSpec((HD, total), whole),
                pl.BlockSpec((total, HD), whole),
                pl.BlockSpec((total, HD), whole),
                pl.BlockSpec((total, HD), whole),
            ],
            out_specs=pl.BlockSpec((total, cols), whole),
            scratch_shapes=[pltpu.VMEM((total, HD), F32), pltpu.VMEM((total, HD), F32)],
        ),
        out_shape=jax.ShapeDtypeStruct((total, cols), BF),
        compiler_params=params(("arbitrary",)),
        cost_estimate=cost(10 * total * total * heads * HD, 16 * total * HD, heads * total * total // 2),
        name="attend_back",
    )(me, q, g, o, lse, k, kt, v, cos, sin)


def back_act_kernel(g_ref, d_ref, out_ref):
    out_ref[...] = mm(g_ref[...], d_ref[...], NT)


def back_act_call(g_out, w_down, rows):
    total, width = g_out.shape
    cols = w_down.shape[0]
    return pl.pallas_call(
        back_act_kernel,
        grid=(total // rows,),
        in_specs=[
            pl.BlockSpec((rows, width), lambda i: (i, 0)),
            pl.BlockSpec((cols, width), lambda i: (0, 0)),
        ],
        out_specs=pl.BlockSpec((rows, cols), lambda i: (i, 0)),
        out_shape=jax.ShapeDtypeStruct((total, cols), F32),
        compiler_params=params(("arbitrary",)),
        cost_estimate=cost(2 * total * width * cols, 2 * total * width + 2 * cols * width + 4 * total * cols),
        name="back_act",
    )(g_out, w_down)


def feed_kernel(z_ref, g_ref, w_ref, act_ref, grads_ref):
    cut = g_ref.shape[1]
    z = z_ref[...]
    gate = mm(z, w_ref[:, :cut], NN)
    up = mm(z, w_ref[:, cut:], NN)
    back = g_ref[...]
    sig = jax.nn.sigmoid(gate)
    silu = gate * sig
    act_ref[...] = (silu * up).astype(BF)
    grads_ref[:, :cut] = (back * up * (sig * (1.0 + gate * (1.0 - sig)))).astype(BF)
    grads_ref[:, cut:] = (back * silu).astype(BF)


def feed_call(z_two, g_act, w_gu, part, rows):
    total, width = z_two.shape
    cut = w_gu.shape[1] // 2
    row = lambda i: (i, 0)
    whole = lambda i: (0, 0)
    return pl.pallas_call(
        feed_kernel,
        grid=(total // rows,),
        in_specs=[
            pl.BlockSpec((rows, width), row),
            pl.BlockSpec((rows, cut), lambda i: (i, part)),
            pl.BlockSpec((width, 2 * cut), whole),
        ],
        out_specs=[pl.BlockSpec((rows, cut), row), pl.BlockSpec((rows, 2 * cut), row)],
        out_shape=[
            jax.ShapeDtypeStruct((total, cut), BF),
            jax.ShapeDtypeStruct((total, 2 * cut), BF),
        ],
        compiler_params=params(("arbitrary",)),
        cost_estimate=cost(4 * total * width * cut, 2 * total * width + 4 * cut * width + 10 * total * cut),
        name="feed",
    )(z_two, g_act, w_gu)


def sum_kernel(*refs, dims):
    *ins, low_ref, high_ref = refs
    acc = None
    for a_ref, b_ref in zip(ins[0::2], ins[1::2]):
        term = mm(a_ref[...], b_ref[...], dims)
        acc = term if acc is None else acc + term
    acc = acc.astype(BF)
    half = pl.num_programs(0) // 2

    @pl.when(pl.program_id(0) < half)
    def _():
        high_ref[...] = acc

    @pl.when(pl.program_id(0) >= half)
    def _():
        low_ref[...] = acc


def sum_call(pairs, dims, rows, name):
    total = pairs[0][0].shape[0]
    cols = pairs[0][1].shape[1 if dims is NN else 0]
    steps = total // rows
    half = steps // 2
    row = lambda i: ((i + half) % steps, 0)
    low = lambda i: (jnp.maximum(i - half, 0), 0)
    high = lambda i: (jnp.minimum(i, half - 1), 0)
    whole = lambda i: (0, 0)
    specs, flat, depth = [], [], 0
    for a, b in pairs:
        specs += [pl.BlockSpec((rows, a.shape[1]), row), pl.BlockSpec(b.shape, whole)]
        flat += [a, b]
        depth += a.shape[1]
    return pl.pallas_call(
        functools.partial(sum_kernel, dims=dims),
        grid=(total // rows,),
        in_specs=specs,
        out_specs=[pl.BlockSpec((rows, cols), low), pl.BlockSpec((rows, cols), high)],
        out_shape=[jax.ShapeDtypeStruct((total // 2, cols), BF)] * 2,
        compiler_params=params(("arbitrary",)),
        cost_estimate=cost(2 * total * cols * depth, 2 * (total * depth + depth * cols + total * cols)),
        name=name,
    )(*flat)


def split_rows(count):
    half = count // 2
    row = lambda i: (i + half) % count
    low = lambda i: jnp.maximum(i - half, 0)
    high = lambda i: jnp.minimum(i, half - 1)
    return half, row, low, high


def hidden_kernel(me_ref, a_ref, w_ref, x_ref, hid_ref, z_ref, rms_ref):
    p = pl.program_id(0)

    @pl.when(p == 0)
    def _():
        hid_ref[...] = x_ref[...].astype(F32)

    hid_ref[...] += mm(a_ref[0], w_ref[...], NN)

    @pl.when(p == pl.num_programs(0) - 1)
    def _():
        hid = hid_ref[...]
        rms = rms_of(hid)
        rms_ref[...] = rms
        z_ref[...] = (hid * rms).astype(BF)


def hidden_call(me, attn, wo, x, count):
    _, rows, feat = attn.shape
    width = wo.shape[1]
    true3 = lambda p, me_ref: (offset_of(p, count) ^ me_ref[0], 0, 0)
    block = lambda p, me_ref: (p, 0)
    whole = lambda p, me_ref: (0, 0)
    return pl.pallas_call(
        hidden_kernel,
        grid_spec=pltpu.PrefetchScalarGridSpec(
            num_scalar_prefetch=1,
            grid=(count,),
            in_specs=[
                pl.BlockSpec((1, rows, feat), true3),
                pl.BlockSpec((feat, width), block),
                pl.BlockSpec((rows, width), whole),
            ],
            out_specs=[
                pl.BlockSpec((rows, width), whole),
                pl.BlockSpec((rows, width), whole),
                pl.BlockSpec((rows, 1), whole),
            ],
        ),
        out_shape=[
            jax.ShapeDtypeStruct((rows, width), F32),
            jax.ShapeDtypeStruct((rows, width), BF),
            jax.ShapeDtypeStruct((rows, 1), F32),
        ],
        compiler_params=params(("arbitrary",)),
        cost_estimate=cost(2 * rows * feat * count * width, 2 * feat * count * width + 10 * rows * width),
        name="hidden",
    )(me, attn, wo, x)


def back_attn_kernel(me_ref, g_ref, w_ref, out_ref):
    out_ref[0] = mm(g_ref[...], w_ref[...], NT).astype(BF)


def back_attn_call(me, g, wo, count):
    rows, width = g.shape
    feat = wo.shape[0] // count
    true3 = lambda p, me_ref: (offset_of(p, count) ^ me_ref[0], 0, 0)
    block = lambda p, me_ref: (p, 0)
    whole = lambda p, me_ref: (0, 0)
    return pl.pallas_call(
        back_attn_kernel,
        grid_spec=pltpu.PrefetchScalarGridSpec(
            num_scalar_prefetch=1,
            grid=(count,),
            in_specs=[pl.BlockSpec((rows, width), whole), pl.BlockSpec((feat, width), block)],
            out_specs=pl.BlockSpec((1, rows, feat), true3),
        ),
        out_shape=jax.ShapeDtypeStruct((count, rows, feat), BF),
        compiler_params=params(("arbitrary",)),
        cost_estimate=cost(2 * rows * feat * count * width, 2 * feat * count * width + 4 * rows * width),
        name="back_attn",
    )(me, g, wo)


def grad_wo_kernel(me_ref, a_ref, g_ref, low_ref, high_ref):
    out = mm(a_ref[0], g_ref[...], TN).astype(BF)
    half = pl.num_programs(0) // 2

    @pl.when(pl.program_id(0) < half)
    def _():
        high_ref[...] = out

    @pl.when(pl.program_id(0) >= half)
    def _():
        low_ref[...] = out


def grad_wo_call(me, attn, g, count):
    _, rows, feat = attn.shape
    width = g.shape[1]
    half, row, low, high = split_rows(count)
    return pl.pallas_call(
        grad_wo_kernel,
        grid_spec=pltpu.PrefetchScalarGridSpec(
            num_scalar_prefetch=1,
            grid=(count,),
            in_specs=[
                pl.BlockSpec(
                    (1, rows, feat), lambda p, me_ref: (offset_of(row(p), count) ^ me_ref[0], 0, 0)
                ),
                pl.BlockSpec((rows, width), lambda p, me_ref: (0, 0)),
            ],
            out_specs=[
                pl.BlockSpec((feat, width), lambda p, me_ref: (low(p), 0)),
                pl.BlockSpec((feat, width), lambda p, me_ref: (high(p), 0)),
            ],
        ),
        out_shape=[jax.ShapeDtypeStruct((half * feat, width), BF)] * 2,
        compiler_params=params(("arbitrary",)),
        cost_estimate=cost(2 * rows * feat * count * width, 2 * feat * count * width + 4 * rows * width),
        name="grad_wo",
    )(me, attn, g)


def finish_feed_kernel(*refs, halves, per_half, unit, count):
    gots, (wg_ref, wu_ref, gain_ref, g_ref, u_ref, sum_ref) = refs[:halves], refs[halves:]
    gain = gain_ref[...]
    total = None
    for h, got_ref in enumerate(gots):
        for kind, (w_ref, out_ref) in enumerate(((wg_ref, g_ref), (wu_ref, u_ref))):
            for i in range(per_half):
                frm = (kind * per_half + i) * unit
                for t in range(count):
                    at = ((h * per_half + i) * count + t) * unit
                    raw = got_ref[t, :, frm : frm + unit].astype(F32)
                    out_ref[:, at : at + unit] = raw * gain
                    term = raw * w_ref[:, at : at + unit].astype(F32)
                    total = term if total is None else total + term
    sum_ref[...] = jnp.sum(total, 1, keepdims=True)


def finish_feed_call(gots, w_gate, w_up, gain, per_half, unit):
    own, hidden = w_gate.shape
    return pl.pallas_call(
        functools.partial(
            finish_feed_kernel,
            halves=len(gots),
            per_half=per_half,
            unit=unit,
            count=gots[0].shape[0],
        ),
        out_shape=[
            jax.ShapeDtypeStruct((own, hidden), F32),
            jax.ShapeDtypeStruct((own, hidden), F32),
            jax.ShapeDtypeStruct((own, 1), F32),
        ],
        compiler_params=pltpu.CompilerParams(vmem_limit_bytes=VMEM_LIMIT),
        cost_estimate=cost(8 * own * hidden, 16 * own * hidden),
        name="finish_feed",
    )(*gots, w_gate, w_up, gain)


def finish_qkv_kernel(
    got_ref, wq_ref, wk_ref, wv_ref, gain_ref, q_ref, k_ref, v_ref, sum_ref, *, heads, reps
):
    gain = gain_ref[...]
    total = None
    feat = heads * HD
    for t in range(got_ref.shape[0]):
        raw = got_ref[t, :, :feat].astype(F32)
        at = slice(t * feat, (t + 1) * feat)
        q_ref[:, at] = raw * gain
        term = jnp.sum(raw * wq_ref[:, at].astype(F32), 1, keepdims=True)
        total = term if total is None else total + term
    for kind, (w_ref, out_ref) in enumerate(((wk_ref, k_ref), (wv_ref, v_ref))):
        frm = slice(feat + kind * HD, feat + (kind + 1) * HD)
        for t in range(got_ref.shape[0] // reps):
            raw = got_ref[t * reps, :, frm].astype(F32)
            for r in range(1, reps):
                raw = raw + got_ref[t * reps + r, :, frm].astype(F32)
            at = slice(t * HD, (t + 1) * HD)
            out_ref[:, at] = raw * gain
            total = total + jnp.sum(raw * w_ref[:, at].astype(F32), 1, keepdims=True)
    sum_ref[...] = total


def finish_qkv_call(got, w_query, w_key, w_value, gain, heads, reps):
    own = w_query.shape[0]
    like = lambda w: jax.ShapeDtypeStruct(w.shape, F32)
    return pl.pallas_call(
        functools.partial(finish_qkv_kernel, heads=heads, reps=reps),
        out_shape=[like(w_query), like(w_key), like(w_value), jax.ShapeDtypeStruct((own, 1), F32)],
        compiler_params=pltpu.CompilerParams(vmem_limit_bytes=VMEM_LIMIT),
        cost_estimate=cost(8 * own * w_query.shape[1], 16 * own * w_query.shape[1]),
        name="finish_qkv",
    )(got, w_query, w_key, w_value, gain)


def rms_of(values):
    return lax.rsqrt(jnp.mean(values * values, -1, keepdims=True) + EPS)


def shards(
    inputs, attn_gain, w_query, w_key, w_value, w_output, ffn_gain, w_gate, w_up, w_down, cotangent
):
    _, rows, width = inputs.shape
    n_cp = lax.axis_size("cp")
    n_dp = lax.axis_size("dp")
    me = lax.axis_index("cp")
    heads = H // n_cp
    reps = n_cp // KVH
    total = rows * n_cp
    own = w_query.shape[0]
    hidden = w_gate.shape[1]
    unit = hidden // (n_dp * n_cp)
    halves = 2
    per_half = n_dp // halves
    me_arr = jnp.reshape(me, (1,)).astype(jnp.int32)
    gain_one = attn_gain.astype(F32)[:, None]
    gain_two = ffn_gain.astype(F32)[:, None]

    def gather_z(value):
        return lax.all_gather(value, "dp", axis=0, tiled=True)

    def scatter_z(value):
        return lax.psum_scatter(value, "dp", scatter_dimension=0, tiled=True)

    def give(value):
        return lax.all_to_all(value, "cp", 0, 0)

    scaled_q = (w_query.astype(F32) * gain_one).astype(BF).reshape(own, n_cp, heads * HD)
    scaled_k = (w_key.astype(F32) * gain_one).astype(BF).reshape(own, KVH, 1, HD)
    scaled_v = (w_value.astype(F32) * gain_one).astype(BF).reshape(own, KVH, 1, HD)
    spread = lambda v: jnp.broadcast_to(v, (own, KVH, reps, HD)).reshape(own, n_cp, HD)
    qkv_own = jnp.concatenate([scaled_q, spread(scaled_k), spread(scaled_v)], 2).transpose(1, 0, 2)
    qkv_cols = (heads + 2) * HD
    qkv_rows = give(qkv_own).reshape(n_cp * own, qkv_cols)
    wo_own = lax.ppermute(w_output, ("dp", "cp"), deal(n_dp, n_cp, 0))
    depth = n_cp * own
    if own * width % qkv_cols == 0:
        joint = jnp.concatenate([qkv_rows, wo_own.reshape(-1, qkv_cols)], 0)
        joint = gather_z(joint).reshape(n_dp, -1, qkv_cols)
        wo_rows = joint[:, depth:].reshape(n_dp * own, width)
    else:
        joint = gather_z(qkv_rows).reshape(n_dp, -1, qkv_cols)
        wo_rows = gather_z(wo_own)

    w_down_full = gather_z(w_down)
    scaled_g = (w_gate.astype(F32) * gain_two).astype(BF).reshape(own, n_dp, n_cp, unit)
    scaled_u = (w_up.astype(F32) * gain_two).astype(BF).reshape(own, n_dp, n_cp, unit)
    cut = per_half * unit
    w_gu, w_dn, last, given = [], [], qkv_rows, []
    for h in range(halves):
        at = slice(h * per_half, (h + 1) * per_half)
        both = jnp.concatenate([scaled_g[:, at], scaled_u[:, at]], 1)
        both = both.transpose(2, 0, 1, 3).reshape(n_cp, own, 2 * cut)
        last = give(after(both, last))
        given.append(last)
        w_gu.append(gather_z(last.reshape(n_cp * own, 2 * cut)))
        w_dn.append(w_down_full[h * cut : (h + 1) * cut])

    shard_at = jnp.array([offset_of(p, n_cp) for p in range(n_cp)], jnp.int32) ^ me
    positions = (shard_at[:, None] * rows + jnp.arange(rows, dtype=jnp.int32)[None, :]).reshape(-1)
    half_dim = HD // 2
    inv_freq = THETA ** (-(jnp.arange(half_dim, dtype=F32) * 2.0 / HD))
    angles = positions.astype(F32)[:, None] * inv_freq[None, :]
    cos_half, sin_half = jnp.cos(angles), jnp.sin(angles)
    cos = jnp.concatenate([cos_half, cos_half], -1)
    sin = jnp.concatenate([-sin_half, sin_half], -1)

    xb = inputs.reshape(rows, width)
    x = xb.astype(F32)
    rms_one = rms_of(x)
    z_one = x * rms_one
    z_one_all = gather_rows(z_one.astype(BF), n_cp, [cos, sin] + given)
    wo_rel = gather_rows(wo_rows, n_cp)
    g_outb = cotangent.reshape(rows, width)
    g_out = g_outb.astype(F32)
    g_out_all = gather_rows(after(g_outb, z_one_all), n_cp)

    q, k, v, kt, vt = qkv_call(z_one_all, joint, cos, sin, rows, heads)
    mixed, lse = attend_call(me_arr, q, k, vt, rows, heads, n_cp)
    feat = heads * HD
    attn = give(mixed.reshape(n_cp, rows, feat))
    hid, z_two_b, rms_two = hidden_call(me_arr, attn, wo_rel, xb, n_cp)
    g_act = back_act_call(after(g_out_all, z_two_b), w_down_full, rows)
    z_two_all = gather_rows(z_two_b, n_cp)

    acts, gus, red_gu = [], [], []
    for h in range(halves):
        z_in = after(z_two_all, part_gu) if h else z_two_all
        act, gu = feed_call(z_in, g_act, w_gu[h], h, rows)
        acts.append(act)
        gus.append(gu)
        if h == 0:
            part_gu = mm(z_two_all, gu, TN).astype(BF)
            red_gu.append(scatter_z(part_gu))
    part = sum_call([(gus[h], w_gu[h]) for h in range(halves)], NT, rows, "g_two")
    part_gu = mm(z_two_all, after(gus[1], *part), TN).astype(BF)
    red_gu.append(scatter_z(part_gu))
    acc = scatter_first(*part, n_cp, part_gu)
    out_part = sum_call([(after(acts[h], acc), w_dn[h]) for h in range(halves)], NN, rows, "out")
    state = scatter_mid(acc, n_cp, *out_part)
    downs = [mm(after(act, *state), g_out_all, TN).astype(BF) for act in acts]
    grad_down = scatter_z(after(jnp.concatenate(downs, 0), red_gu[0]))
    out_acc = scatter_first(*out_part, n_cp, *downs)
    u = scatter_last(state, n_cp, out_acc)

    z_two = hid * rms_two
    g_hidden = g_out + rms_two * (u - z_two * jnp.mean(u * z_two, -1, keepdims=True))
    g_hidb = g_hidden.astype(BF)
    g_heads = back_attn_call(me_arr, g_hidb, wo_rel, n_cp)
    wo_part = grad_wo_call(me_arr, attn, after(g_hidb, g_heads), n_cp)
    out_state = scatter_mid(after(out_acc, g_hidb), n_cp, *wo_part)
    g_mixed = give(after(g_heads, *out_state)).reshape(total, feat)
    back_gu = [give(after(red_gu[0].reshape(n_cp, own, 2 * cut), g_mixed))]
    g_qkv = attend_back_call(me_arr, q, g_mixed, mixed, lse, k, kt, v, cos, sin, rows, heads, n_cp)
    out_sum = scatter_last(after(out_state, g_mixed), n_cp, g_qkv)
    output = hid + out_sum
    wo_acc = scatter_first(*wo_part, n_cp, g_qkv, out_sum)
    w_qkv = joint[:, :depth].reshape(width, qkv_cols)
    part = sum_call([(after(g_qkv, wo_acc), w_qkv)], NT, rows, "g_one")
    wo_state = scatter_mid(wo_acc, n_cp, *part)
    part_qkv = mm(z_one_all, after(g_qkv, red_gu[1], back_gu[0], *wo_state), TN).astype(BF)
    red_qkv = scatter_z(part_qkv)
    back_gu.append(give(after(red_gu[1].reshape(n_cp, own, 2 * cut), part_qkv)))
    w_acc = scatter_first(*part, n_cp, part_qkv)
    wo_sum = scatter_last(wo_state, n_cp, w_acc).astype(BF)
    w_state = scatter_mid(w_acc, n_cp, back_gu[1])

    wo_sum = scatter_z(after(wo_sum, grad_down))
    got = give(red_qkv.reshape(n_cp, own, qkv_cols))
    back_pairs = [(b, a) for a, b in deal(n_dp, n_cp, 0)]
    grad_output = lax.ppermute(wo_sum, ("dp", "cp"), back_pairs).astype(F32)
    w_one = scatter_last(w_state, n_cp, got)
    grad_in = g_hidden + rms_one * (w_one - z_one * jnp.mean(w_one * z_one, -1, keepdims=True))

    grad_g, grad_u, gain_two_sum = finish_feed_call(back_gu, w_gate, w_up, gain_two, per_half, unit)
    grad_q, grad_k, grad_v, gain_one_sum = finish_qkv_call(
        got, w_query, w_key, w_value, gain_one, heads, reps
    )

    return (
        output[None],
        grad_in[None],
        gain_one_sum[:, 0],
        grad_q,
        grad_k,
        grad_v,
        grad_output,
        gain_two_sum[:, 0],
        grad_g,
        grad_u,
        grad_down.astype(F32),
    )


def solution(mesh):
    both = ("dp", "cp")
    rows = P("dp", "cp", None)
    mat = P(both, None)
    vec = P(both)
    return jax.shard_map(
        shards,
        mesh=mesh,
        in_specs=(rows, vec, mat, mat, mat, mat, vec, mat, mat, mat, rows),
        out_specs=(rows, rows, vec, mat, mat, mat, mat, vec, mat, mat, mat),
        check_vma=False,
    )
```

```python
import functools
import math

import jax
import jax.numpy as jnp
from jax import lax
from jax.experimental import pallas as pl
from jax.experimental.pallas import tpu as pltpu
from jax.sharding import PartitionSpec as P

H = 16
KVH = 8
HD = 128
EPS = 1e-05
THETA = 1000000.0
SCALE = HD ** (-0.5)
LOG2E = math.log2(math.e)
BF = jnp.bfloat16
F32 = jnp.float32
VMEM_LIMIT = 56 * 1024 * 1024
SHARE = 0.05

NN = (((1,), (0,)), ((), ()))
NT = (((1,), (1,)), ((), ()))
TN = (((0,), (0,)), ((), ()))


def mm(left, right, dims):
    return lax.dot_general(left, right, dims, preferred_element_type=F32)


def offset_of(position, count):
    half = count // 2
    return ((position % half) << 1) | (position // half)


def position_of(offset, count):
    return (offset >> 1) + (offset & 1) * (count // 2)


def after(value, *deps):
    return lax.optimization_barrier((value, *deps))[0]


def swap(value, count, offset):
    return lax.ppermute(value, "cp", [(i, i ^ offset) for i in range(count)])


def gather_rows(part, count, dep=None, late=()):
    half = part.shape[0] // 2
    if count == 8:
        by_x = swap(part, count, 2)
        by_y = swap(part, count, 4)
        if dep is not None:
            by_y = after(by_y, *dep)
        near = jnp.concatenate([part, by_x, by_y], 0)
        near_other = swap(near, count, 1)
        far = [swap(by_y[:half], count, 2), swap(by_x[half:], count, 4)]
        far = jnp.concatenate(lax.optimization_barrier((*far, *late))[:2], 0)
        return jnp.concatenate([near, far, near_other, swap(far, count, 1)], 0)
    inner, bit = part, 2
    while bit < count:
        inner = jnp.concatenate([inner, swap(inner, count, bit)], 0)
        bit *= 2
    return jnp.concatenate([inner, swap(inner, count, 1)], 0)


def plus(left, right):
    return (left.astype(F32) + right.astype(F32)).astype(BF)


def scatter_first(low, high, count, *deps):
    got = swap(high, count, 1)
    return plus(low, after(got, *deps) if deps else got)


def scatter_mid(acc, count, *deps):
    rows = 2 * acc.shape[0] // count
    half = rows // 2
    parts = [acc[i * rows : (i + 1) * rows] for i in range(count // 2)]
    if count == 8:
        own, to_x, to_y, far = parts
        from_x = swap(far[:half], count, 2)
        from_y = swap(far[half:], count, 4)
        if deps:
            from_x, from_y = lax.optimization_barrier((from_x, from_y, *deps))[:2]
        send_x = jnp.concatenate([to_x[:half], plus(to_x[half:], from_y)], 0)
        send_y = jnp.concatenate([plus(to_y[:half], from_x), to_y[half:]], 0)
        return own, send_x, send_y
    bit = count // 2
    while bit > 2:
        keep, give = parts[: len(parts) // 2], parts[len(parts) // 2 :]
        parts = [plus(a, swap(b, count, bit)) for a, b in zip(keep, give)]
        bit //= 2
    return tuple(parts)


def scatter_last(state, count, *deps):
    got = [swap(part, count, offset) for offset, part in zip((2, 4), state[1:])]
    if deps:
        got = lax.optimization_barrier((*got, *deps))[: len(got)]
    total = state[0].astype(F32)
    for part in got:
        total = total + part.astype(F32)
    return total


def deal(count, n_cp, shift):
    return [
        (b, ((b % count + shift) % count) * n_cp + b // count) for b in range(count * n_cp)
    ]


def params(semantics):
    return pltpu.CompilerParams(dimension_semantics=semantics, vmem_limit_bytes=VMEM_LIMIT)


def cost(flops, nbytes, trans=0):
    return pl.CostEstimate(
        flops=int(flops * SHARE), bytes_accessed=int(nbytes * SHARE), transcendentals=int(trans * SHARE)
    )


def turn(value, cos, sin):
    return value * cos + pltpu.roll(value, HD // 2, 1) * sin


def qkv_kernel(z_ref, w_ref, cos_ref, sin_ref, q_ref, k_ref, v_ref, kt_ref, vt_ref, *, heads):
    cos, sin = cos_ref[...], sin_ref[...]
    flat = None
    depth = z_ref.shape[1] // w_ref.shape[0]
    for d in range(w_ref.shape[0]):
        term = mm(z_ref[:, d * depth : (d + 1) * depth], w_ref[d, :depth, :], NN)
        flat = term if flat is None else flat + term
    for h in range(heads):
        at = slice(h * HD, (h + 1) * HD)
        q_ref[:, at] = turn(flat[:, at], cos, sin).astype(BF)
    key = turn(flat[:, heads * HD : (heads + 1) * HD], cos, sin)
    value = flat[:, (heads + 1) * HD :]
    k_ref[...] = key.astype(BF)
    v_ref[...] = value.astype(BF)
    kt_ref[...] = key.T.astype(BF)
    vt_ref[...] = value.T.astype(BF)


def qkv_call(z_one, w_qkv, cos, sin, rows, heads):
    total, width = z_one.shape
    cols = w_qkv.shape[2]
    row = lambda i: (i, 0)
    col = lambda i: (0, i)
    whole = lambda i: (0, 0)
    return pl.pallas_call(
        functools.partial(qkv_kernel, heads=heads),
        grid=(total // rows,),
        in_specs=[
            pl.BlockSpec((rows, width), row),
            pl.BlockSpec(w_qkv.shape, lambda i: (0, 0, 0)),
            pl.BlockSpec((rows, HD), row),
            pl.BlockSpec((rows, HD), row),
        ],
        out_specs=[
            pl.BlockSpec((rows, heads * HD), row),
            pl.BlockSpec((rows, HD), row),
            pl.BlockSpec((rows, HD), row),
            pl.BlockSpec((HD, rows), col),
            pl.BlockSpec((HD, rows), col),
        ],
        out_shape=[
            jax.ShapeDtypeStruct((total, heads * HD), BF),
            jax.ShapeDtypeStruct((total, HD), BF),
            jax.ShapeDtypeStruct((total, HD), BF),
            jax.ShapeDtypeStruct((HD, total), BF),
            jax.ShapeDtypeStruct((HD, total), BF),
        ],
        compiler_params=params(("arbitrary",)),
        cost_estimate=cost(2 * total * width * cols, 2 * (total * width + width * cols)),
        name="qkv",
    )(z_one, w_qkv, cos, sin)


def stack_heads(block, heads):
    if heads == 1:
        return block
    return jnp.concatenate([block[:, h * HD : (h + 1) * HD] for h in range(heads)], 0)


def diagonal_mask(rows, heads):
    key_at = lax.broadcasted_iota(jnp.int32, (rows, rows), 0)
    query_at = lax.broadcasted_iota(jnp.int32, (rows, rows), 1)
    one = key_at <= query_at
    return one if heads == 1 else jnp.concatenate([one] * heads, 1)


def attend_kernel(me_ref, q_ref, k_ref, vt_ref, o_ref, lse_ref, *, heads, rows, count):
    i = pl.program_id(0)
    me = me_ref[0]
    wide = heads * rows
    queries = stack_heads(q_ref[...], heads)

    def step(j, carry, masked):
        top, total, acc = carry
        at = pl.multiple_of(position_of(j ^ me, count) * rows, rows)
        s = mm(k_ref[pl.ds(at, rows), :], queries, NT) * (SCALE * LOG2E)
        if masked:
            s = jnp.where(diagonal_mask(rows, heads), s, -1e30)
        new_top = jnp.maximum(top, jnp.max(s, 0, keepdims=True))
        fade = jnp.exp2(top - new_top)
        p = jnp.exp2(s - new_top)
        total = total * fade + jnp.sum(p, 0, keepdims=True)
        acc = acc * fade + mm(vt_ref[:, pl.ds(at, rows)], p.astype(BF), NN)
        return new_top, total, acc

    carry = (
        jnp.full((1, wide), -1e30, F32),
        jnp.zeros((1, wide), F32),
        jnp.zeros((HD, wide), F32),
    )
    carry = step(i, carry, True)
    top, total, acc = lax.fori_loop(0, i, lambda j, c: step(j, c, False), carry)
    out = (acc / total).T
    for h in range(heads):
        o_ref[:, h * HD : (h + 1) * HD] = out[h * rows : (h + 1) * rows, :].astype(BF)
    lse_ref[0] = top + jnp.log2(total)


def attend_call(me, q, k, vt, rows, heads, count):
    total = q.shape[0]
    slot = lambda i, me_ref: (position_of(i ^ me_ref[0], count), 0)
    true = lambda i, me_ref: (i, 0)
    true3 = lambda i, me_ref: (i, 0, 0)
    whole = lambda i, me_ref: (0, 0)
    return pl.pallas_call(
        functools.partial(attend_kernel, heads=heads, rows=rows, count=count),
        grid_spec=pltpu.PrefetchScalarGridSpec(
            num_scalar_prefetch=1,
            grid=(count,),
            in_specs=[
                pl.BlockSpec((rows, heads * HD), slot),
                pl.BlockSpec((total, HD), whole),
                pl.BlockSpec((HD, total), whole),
            ],
            out_specs=[
                pl.BlockSpec((rows, heads * HD), true),
                pl.BlockSpec((1, 1, heads * rows), true3),
            ],
        ),
        out_shape=[
            jax.ShapeDtypeStruct((total, heads * HD), BF),
            jax.ShapeDtypeStruct((count, 1, heads * rows), F32),
        ],
        compiler_params=params(("arbitrary",)),
        cost_estimate=cost(4 * total * total * heads * HD, 8 * total * HD, heads * total * total // 2),
        name="attend",
    )(me, q, k, vt)


def attend_back_kernel(
    me_ref,
    q_ref,
    g_ref,
    o_ref,
    lse_ref,
    k_ref,
    kt_ref,
    v_ref,
    cos_ref,
    sin_ref,
    out_ref,
    dk_ref,
    dv_ref,
    *,
    heads,
    rows,
    count,
):
    i = pl.program_id(0)
    me = me_ref[0]
    wide = heads * rows

    @pl.when(i == 0)
    def _():
        dk_ref[...] = jnp.zeros_like(dk_ref)
        dv_ref[...] = jnp.zeros_like(dv_ref)

    queries = stack_heads(q_ref[...], heads)
    grads = stack_heads(g_ref[...], heads)
    outs = stack_heads(o_ref[...], heads)
    lse = lse_ref[0]
    mixed = jnp.sum((outs.astype(F32) * grads.astype(F32)).T, 0, keepdims=True)

    def step(j, dqt, masked):
        at = pl.multiple_of(position_of(j ^ me, count) * rows, rows)
        here = pl.ds(at, rows)
        s = mm(k_ref[here, :], queries, NT) * (SCALE * LOG2E)
        p = jnp.exp2(s - lse)
        if masked:
            p = jnp.where(diagonal_mask(rows, heads), p, 0.0)
        gp = mm(v_ref[here, :], grads, NT)
        gs = (p * (gp - mixed) * SCALE).astype(BF)
        dv_ref[here, :] += mm(p.astype(BF), grads, NN)
        dk_ref[here, :] += mm(gs, queries, NN)
        return dqt + mm(kt_ref[:, here], gs, NN)

    dqt = step(i, jnp.zeros((HD, wide), F32), True)
    dqt = lax.fori_loop(0, i, lambda j, c: step(j, c, False), dqt)
    dq = dqt.T
    mine = pl.ds(pl.multiple_of(position_of(i ^ me, count) * rows, rows), rows)
    cos, sin = cos_ref[mine, :], sin_ref[mine, :]
    for h in range(heads):
        one = turn(dq[h * rows : (h + 1) * rows, :], cos, -sin)
        out_ref[mine, h * HD : (h + 1) * HD] = one.astype(BF)

    @pl.when(i == count - 1)
    def _():
        out_ref[:, heads * HD : (heads + 1) * HD] = turn(
            dk_ref[...], cos_ref[...], -sin_ref[...]
        ).astype(BF)
        out_ref[:, (heads + 1) * HD :] = dv_ref[...].astype(BF)


def attend_back_call(me, q, g, o, lse, k, kt, v, cos, sin, rows, heads, count):
    total = q.shape[0]
    slot = lambda i, me_ref: (position_of(i ^ me_ref[0], count), 0)
    true = lambda i, me_ref: (i, 0)
    true3 = lambda i, me_ref: (i, 0, 0)
    whole = lambda i, me_ref: (0, 0)
    cols = (heads + 2) * HD
    return pl.pallas_call(
        functools.partial(attend_back_kernel, heads=heads, rows=rows, count=count),
        grid_spec=pltpu.PrefetchScalarGridSpec(
            num_scalar_prefetch=1,
            grid=(count,),
            in_specs=[
                pl.BlockSpec((rows, heads * HD), slot),
                pl.BlockSpec((rows, heads * HD), true),
                pl.BlockSpec((rows, heads * HD), true),
                pl.BlockSpec((1, 1, heads * rows), true3),
                pl.BlockSpec((total, HD), whole),
                pl.BlockSpec((HD, total), whole),
                pl.BlockSpec((total, HD), whole),
                pl.BlockSpec((total, HD), whole),
                pl.BlockSpec((total, HD), whole),
            ],
            out_specs=pl.BlockSpec((total, cols), whole),
            scratch_shapes=[pltpu.VMEM((total, HD), F32), pltpu.VMEM((total, HD), F32)],
        ),
        out_shape=jax.ShapeDtypeStruct((total, cols), BF),
        compiler_params=params(("arbitrary",)),
        cost_estimate=cost(10 * total * total * heads * HD, 16 * total * HD, heads * total * total // 2),
        name="attend_back",
    )(me, q, g, o, lse, k, kt, v, cos, sin)


def back_act_kernel(g_ref, d_ref, out_ref):
    blocks, _, wide = d_ref.shape
    unit = out_ref.shape[1] // blocks
    for b in range(blocks):
        acc = None
        for c in range(g_ref.shape[1] // wide):
            part = d_ref[b, c * unit : (c + 1) * unit, :]
            term = mm(g_ref[:, c * wide : (c + 1) * wide], part, NT)
            acc = term if acc is None else acc + term
        out_ref[:, b * unit : (b + 1) * unit] = acc


def back_act_call(g_out, packed, rows):
    total, width = g_out.shape
    blocks, depth, wide = packed.shape
    depth = depth // 2
    cols = blocks * depth * wide // width
    return pl.pallas_call(
        back_act_kernel,
        grid=(total // rows,),
        in_specs=[
            pl.BlockSpec((rows, width), lambda i: (i, 0)),
            pl.BlockSpec((blocks, depth, wide), lambda i: (0, 1, 0)),
        ],
        out_specs=pl.BlockSpec((rows, cols), lambda i: (i, 0)),
        out_shape=jax.ShapeDtypeStruct((total, cols), F32),
        compiler_params=params(("arbitrary",)),
        cost_estimate=cost(2 * total * width * cols, 2 * total * width + 2 * cols * width + 4 * total * cols),
        name="back_act",
    )(g_out, packed)


def feed_kernel(z_ref, g_ref, w_ref, act_ref, grads_ref):
    cut = g_ref.shape[1]
    blocks, depth, _ = w_ref.shape
    both = None
    for b in range(blocks):
        term = mm(z_ref[:, b * depth : (b + 1) * depth], w_ref[b], NN)
        both = term if both is None else both + term
    gate, up = both[:, :cut], both[:, cut:]
    back = g_ref[...]
    sig = jax.nn.sigmoid(gate)
    silu = gate * sig
    act_ref[...] = (silu * up).astype(BF)
    grads_ref[:, :cut] = (back * up * (sig * (1.0 + gate * (1.0 - sig)))).astype(BF)
    grads_ref[:, cut:] = (back * silu).astype(BF)


def feed_call(z_two, g_act, w_gu, part, rows):
    total, width = z_two.shape
    cut = w_gu.shape[2] // 2
    blocks = w_gu.shape[0]
    row = lambda i: (i, 0)
    return pl.pallas_call(
        feed_kernel,
        grid=(total // rows,),
        in_specs=[
            pl.BlockSpec((rows, width), row),
            pl.BlockSpec((rows, cut), lambda i: (i, part)),
            pl.BlockSpec((blocks, width // blocks, 2 * cut), lambda i: (0, 0, 0)),
        ],
        out_specs=[pl.BlockSpec((rows, cut), row), pl.BlockSpec((rows, 2 * cut), row)],
        out_shape=[
            jax.ShapeDtypeStruct((total, cut), BF),
            jax.ShapeDtypeStruct((total, 2 * cut), BF),
        ],
        compiler_params=params(("arbitrary",)),
        cost_estimate=cost(4 * total * width * cut, 2 * total * width + 4 * cut * width + 10 * total * cut),
        name="feed",
    )(z_two, g_act, w_gu)


def sum_kernel(*refs, dims):
    *ins, low_ref, high_ref = refs
    acc = None
    for a_ref, b_ref in zip(ins[0::2], ins[1::2]):
        term = mm(a_ref[...], b_ref[...], dims)
        acc = term if acc is None else acc + term
    acc = acc.astype(BF)
    half = pl.num_programs(0) // 2

    @pl.when(pl.program_id(0) < half)
    def _():
        high_ref[...] = acc

    @pl.when(pl.program_id(0) >= half)
    def _():
        low_ref[...] = acc


def sum_call(pairs, dims, rows, name):
    total = pairs[0][0].shape[0]
    cols = pairs[0][1].shape[1 if dims is NN else 0]
    steps = total // rows
    half = steps // 2
    row = lambda i: ((i + half) % steps, 0)
    low = lambda i: (jnp.maximum(i - half, 0), 0)
    high = lambda i: (jnp.minimum(i, half - 1), 0)
    whole = lambda i: (0, 0)
    specs, flat, depth = [], [], 0
    for a, b in pairs:
        specs += [pl.BlockSpec((rows, a.shape[1]), row), pl.BlockSpec(b.shape, whole)]
        flat += [a, b]
        depth += a.shape[1]
    return pl.pallas_call(
        functools.partial(sum_kernel, dims=dims),
        grid=(total // rows,),
        in_specs=specs,
        out_specs=[pl.BlockSpec((rows, cols), low), pl.BlockSpec((rows, cols), high)],
        out_shape=[jax.ShapeDtypeStruct((total // 2, cols), BF)] * 2,
        compiler_params=params(("arbitrary",)),
        cost_estimate=cost(2 * total * cols * depth, 2 * (total * depth + depth * cols + total * cols)),
        name=name,
    )(*flat)


def split_rows(count):
    half = count // 2
    row = lambda i: (i + half) % count
    low = lambda i: jnp.maximum(i - half, 0)
    high = lambda i: jnp.minimum(i, half - 1)
    return half, row, low, high


def hidden_kernel(me_ref, a_ref, w_ref, x_ref, hid_ref, z_ref, rms_ref):
    p = pl.program_id(0)

    @pl.when(p == 0)
    def _():
        hid_ref[...] = x_ref[...].astype(F32)

    hid_ref[...] += mm(a_ref[0], w_ref[...], NN)

    @pl.when(p == pl.num_programs(0) - 1)
    def _():
        hid = hid_ref[...]
        rms = rms_of(hid)
        rms_ref[...] = rms
        z_ref[...] = (hid * rms).astype(BF)


def hidden_call(me, attn, wo, x, count):
    _, rows, feat = attn.shape
    width = wo.shape[1]
    true3 = lambda p, me_ref: (offset_of(p, count) ^ me_ref[0], 0, 0)
    block = lambda p, me_ref: (p, 0)
    whole = lambda p, me_ref: (0, 0)
    return pl.pallas_call(
        hidden_kernel,
        grid_spec=pltpu.PrefetchScalarGridSpec(
            num_scalar_prefetch=1,
            grid=(count,),
            in_specs=[
                pl.BlockSpec((1, rows, feat), true3),
                pl.BlockSpec((feat, width), block),
                pl.BlockSpec((rows, width), whole),
            ],
            out_specs=[
                pl.BlockSpec((rows, width), whole),
                pl.BlockSpec((rows, width), whole),
                pl.BlockSpec((rows, 1), whole),
            ],
        ),
        out_shape=[
            jax.ShapeDtypeStruct((rows, width), F32),
            jax.ShapeDtypeStruct((rows, width), BF),
            jax.ShapeDtypeStruct((rows, 1), F32),
        ],
        compiler_params=params(("arbitrary",)),
        cost_estimate=cost(2 * rows * feat * count * width, 2 * feat * count * width + 10 * rows * width),
        name="hidden",
    )(me, attn, wo, x)


def back_attn_kernel(me_ref, g_ref, w_ref, out_ref):
    out_ref[0] = mm(g_ref[...], w_ref[...], NT).astype(BF)


def back_attn_call(me, g, wo, count):
    rows, width = g.shape
    feat = wo.shape[0] // count
    true3 = lambda p, me_ref: (offset_of(p, count) ^ me_ref[0], 0, 0)
    block = lambda p, me_ref: (p, 0)
    whole = lambda p, me_ref: (0, 0)
    return pl.pallas_call(
        back_attn_kernel,
        grid_spec=pltpu.PrefetchScalarGridSpec(
            num_scalar_prefetch=1,
            grid=(count,),
            in_specs=[pl.BlockSpec((rows, width), whole), pl.BlockSpec((feat, width), block)],
            out_specs=pl.BlockSpec((1, rows, feat), true3),
        ),
        out_shape=jax.ShapeDtypeStruct((count, rows, feat), BF),
        compiler_params=params(("arbitrary",)),
        cost_estimate=cost(2 * rows * feat * count * width, 2 * feat * count * width + 4 * rows * width),
        name="back_attn",
    )(me, g, wo)


def grad_wo_kernel(me_ref, a_ref, g_ref, low_ref, high_ref):
    out = mm(a_ref[0], g_ref[...], TN).astype(BF)
    half = pl.num_programs(0) // 2

    @pl.when(pl.program_id(0) < half)
    def _():
        high_ref[...] = out

    @pl.when(pl.program_id(0) >= half)
    def _():
        low_ref[...] = out


def grad_wo_call(me, attn, g, count):
    _, rows, feat = attn.shape
    width = g.shape[1]
    half, row, low, high = split_rows(count)
    return pl.pallas_call(
        grad_wo_kernel,
        grid_spec=pltpu.PrefetchScalarGridSpec(
            num_scalar_prefetch=1,
            grid=(count,),
            in_specs=[
                pl.BlockSpec(
                    (1, rows, feat), lambda p, me_ref: (offset_of(row(p), count) ^ me_ref[0], 0, 0)
                ),
                pl.BlockSpec((rows, width), lambda p, me_ref: (0, 0)),
            ],
            out_specs=[
                pl.BlockSpec((feat, width), lambda p, me_ref: (low(p), 0)),
                pl.BlockSpec((feat, width), lambda p, me_ref: (high(p), 0)),
            ],
        ),
        out_shape=[jax.ShapeDtypeStruct((half * feat, width), BF)] * 2,
        compiler_params=params(("arbitrary",)),
        cost_estimate=cost(2 * rows * feat * count * width, 2 * feat * count * width + 4 * rows * width),
        name="grad_wo",
    )(me, attn, g)


def packed_kernel(*refs, down):
    *ins, low_ref, high_ref = refs
    lefts, weights = ins[:2], ins[2:]
    blocks, depth, wide = weights[0].shape
    pieces = []
    if down:
        per = blocks // 2
        unit = lefts[0].shape[1] // per
        for c in range(depth // unit):
            acc = None
            for b in range(blocks):
                left = lefts[b // per][:, (b % per) * unit : (b % per + 1) * unit]
                term = mm(left, weights[0][b, c * unit : (c + 1) * unit, :], NN)
                acc = term if acc is None else acc + term
            pieces.append(acc.astype(BF))
    else:
        for b in range(blocks):
            acc = mm(lefts[0][...], weights[0][b], NT) + mm(lefts[1][...], weights[1][b], NT)
            pieces.append(acc.astype(BF))
    out = jnp.concatenate(pieces, 1)
    half = pl.num_programs(0) // 2

    @pl.when(pl.program_id(0) < half)
    def _():
        high_ref[...] = out

    @pl.when(pl.program_id(0) >= half)
    def _():
        low_ref[...] = out


def packed_call(lefts, weights, down, width, rows, name):
    total, cols = lefts[0].shape
    blocks, _, wide = weights[0].shape
    depth = width // blocks
    half, row, low, high = split_rows(total // rows)
    left = pl.BlockSpec((rows, cols), lambda i: (row(i), 0))
    weight = pl.BlockSpec((blocks, depth, wide), lambda i: (0, 1 if down else 0, 0))
    return pl.pallas_call(
        functools.partial(packed_kernel, down=down),
        grid=(total // rows,),
        in_specs=[left, left] + [weight] * len(weights),
        out_specs=[
            pl.BlockSpec((rows, width), lambda i: (low(i), 0)),
            pl.BlockSpec((rows, width), lambda i: (high(i), 0)),
        ],
        out_shape=[jax.ShapeDtypeStruct((total // 2, width), BF)] * 2,
        compiler_params=params(("arbitrary",)),
        cost_estimate=cost(4 * total * cols * width, 2 * total * (2 * cols + width) + 4 * cols * width),
        name=name,
    )(*lefts, *weights)


def finish_feed_kernel(*refs, halves, per_half, unit, count):
    gots, (wg_ref, wu_ref, gain_ref, g_ref, u_ref, sum_ref) = refs[:halves], refs[halves:]
    gain = gain_ref[...]
    total = None
    for h, got_ref in enumerate(gots):
        for kind, (w_ref, out_ref) in enumerate(((wg_ref, g_ref), (wu_ref, u_ref))):
            for i in range(per_half):
                frm = (kind * per_half + i) * unit
                for t in range(count):
                    at = ((h * per_half + i) * count + t) * unit
                    raw = got_ref[t, :, frm : frm + unit].astype(F32)
                    out_ref[:, at : at + unit] = raw * gain
                    term = raw * w_ref[:, at : at + unit].astype(F32)
                    total = term if total is None else total + term
    sum_ref[...] = jnp.sum(total, 1, keepdims=True)


def finish_feed_call(gots, w_gate, w_up, gain, per_half, unit):
    own, hidden = w_gate.shape
    return pl.pallas_call(
        functools.partial(
            finish_feed_kernel,
            halves=len(gots),
            per_half=per_half,
            unit=unit,
            count=gots[0].shape[0],
        ),
        out_shape=[
            jax.ShapeDtypeStruct((own, hidden), F32),
            jax.ShapeDtypeStruct((own, hidden), F32),
            jax.ShapeDtypeStruct((own, 1), F32),
        ],
        compiler_params=pltpu.CompilerParams(vmem_limit_bytes=VMEM_LIMIT),
        cost_estimate=cost(8 * own * hidden, 16 * own * hidden),
        name="finish_feed",
    )(*gots, w_gate, w_up, gain)


def finish_qkv_kernel(
    got_ref, wq_ref, wk_ref, wv_ref, gain_ref, q_ref, k_ref, v_ref, sum_ref, *, heads, reps
):
    gain = gain_ref[...]
    total = None
    feat = heads * HD
    for t in range(got_ref.shape[0]):
        raw = got_ref[t, :, :feat].astype(F32)
        at = slice(t * feat, (t + 1) * feat)
        q_ref[:, at] = raw * gain
        term = jnp.sum(raw * wq_ref[:, at].astype(F32), 1, keepdims=True)
        total = term if total is None else total + term
    for kind, (w_ref, out_ref) in enumerate(((wk_ref, k_ref), (wv_ref, v_ref))):
        frm = slice(feat + kind * HD, feat + (kind + 1) * HD)
        for t in range(got_ref.shape[0] // reps):
            raw = got_ref[t * reps, :, frm].astype(F32)
            for r in range(1, reps):
                raw = raw + got_ref[t * reps + r, :, frm].astype(F32)
            at = slice(t * HD, (t + 1) * HD)
            out_ref[:, at] = raw * gain
            total = total + jnp.sum(raw * w_ref[:, at].astype(F32), 1, keepdims=True)
    sum_ref[...] = total


def finish_qkv_call(got, w_query, w_key, w_value, gain, heads, reps):
    own = w_query.shape[0]
    like = lambda w: jax.ShapeDtypeStruct(w.shape, F32)
    return pl.pallas_call(
        functools.partial(finish_qkv_kernel, heads=heads, reps=reps),
        out_shape=[like(w_query), like(w_key), like(w_value), jax.ShapeDtypeStruct((own, 1), F32)],
        compiler_params=pltpu.CompilerParams(vmem_limit_bytes=VMEM_LIMIT),
        cost_estimate=cost(8 * own * w_query.shape[1], 16 * own * w_query.shape[1]),
        name="finish_qkv",
    )(got, w_query, w_key, w_value, gain)


def rms_of(values):
    return lax.rsqrt(jnp.mean(values * values, -1, keepdims=True) + EPS)


def shards(
    inputs, attn_gain, w_query, w_key, w_value, w_output, ffn_gain, w_gate, w_up, w_down, cotangent
):
    _, rows, width = inputs.shape
    n_cp = lax.axis_size("cp")
    n_dp = lax.axis_size("dp")
    me = lax.axis_index("cp")
    heads = H // n_cp
    reps = n_cp // KVH
    total = rows * n_cp
    own = w_query.shape[0]
    hidden = w_gate.shape[1]
    unit = hidden // (n_dp * n_cp)
    halves = 2
    per_half = n_dp // halves
    me_arr = jnp.reshape(me, (1,)).astype(jnp.int32)
    gain_one = attn_gain.astype(F32)[:, None]
    gain_two = ffn_gain.astype(F32)[:, None]

    def gather_z(value):
        return lax.all_gather(value, "dp", axis=0, tiled=True)

    def scatter_z(value):
        return lax.psum_scatter(value, "dp", scatter_dimension=0, tiled=True)

    def give(value):
        return lax.all_to_all(value, "cp", 0, 0)

    scaled_q = (w_query.astype(F32) * gain_one).astype(BF).reshape(own, n_cp, heads * HD)
    scaled_k = (w_key.astype(F32) * gain_one).astype(BF).reshape(own, KVH, 1, HD)
    scaled_v = (w_value.astype(F32) * gain_one).astype(BF).reshape(own, KVH, 1, HD)
    spread = lambda v: jnp.broadcast_to(v, (own, KVH, reps, HD)).reshape(own, n_cp, HD)
    qkv_own = jnp.concatenate([scaled_q, spread(scaled_k), spread(scaled_v)], 2).transpose(1, 0, 2)
    qkv_cols = (heads + 2) * HD
    qkv_rows = give(qkv_own).reshape(n_cp * own, qkv_cols)
    wo_own = lax.ppermute(w_output, ("dp", "cp"), deal(n_dp, n_cp, 0))
    depth = n_cp * own
    if own * width % qkv_cols == 0:
        joint = jnp.concatenate([qkv_rows, wo_own.reshape(-1, qkv_cols)], 0)
        joint = gather_z(joint).reshape(n_dp, -1, qkv_cols)
        wo_rows = joint[:, depth:].reshape(n_dp * own, width)
    else:
        joint = gather_z(qkv_rows).reshape(n_dp, -1, qkv_cols)
        wo_rows = gather_z(wo_own)

    scaled_g = (w_gate.astype(F32) * gain_two).astype(BF).reshape(own, n_dp, n_cp, unit)
    scaled_u = (w_up.astype(F32) * gain_two).astype(BF).reshape(own, n_dp, n_cp, unit)
    cut = per_half * unit
    w_gu, last, given = [], qkv_rows, []
    for h in range(halves):
        at = slice(h * per_half, (h + 1) * per_half)
        both = jnp.concatenate([scaled_g[:, at], scaled_u[:, at]], 1)
        both = both.transpose(2, 0, 1, 3).reshape(n_cp, own, 2 * cut)
        last = give(after(both, last))
        given.append(last)
        block = last.reshape(depth, 2 * cut)
        if h == 0:
            columns = [w_down[:, c : c + 2 * cut] for c in range(0, width, 2 * cut)]
            block = jnp.concatenate([block, *columns], 0)
        w_gu.append(gather_z(block).reshape(n_dp, -1, 2 * cut))
    packed = w_gu[0]

    shard_at = jnp.array([offset_of(p, n_cp) for p in range(n_cp)], jnp.int32) ^ me
    positions = (shard_at[:, None] * rows + jnp.arange(rows, dtype=jnp.int32)[None, :]).reshape(-1)
    half_dim = HD // 2
    inv_freq = THETA ** (-(jnp.arange(half_dim, dtype=F32) * 2.0 / HD))
    angles = positions.astype(F32)[:, None] * inv_freq[None, :]
    cos_half, sin_half = jnp.cos(angles), jnp.sin(angles)
    cos = jnp.concatenate([cos_half, cos_half], -1)
    sin = jnp.concatenate([-sin_half, sin_half], -1)

    xb = inputs.reshape(rows, width)
    x = xb.astype(F32)
    rms_one = rms_of(x)
    z_one = x * rms_one
    z_one_all = gather_rows(z_one.astype(BF), n_cp, [cos, sin] + given)
    wo_rel = gather_rows(wo_rows, n_cp)
    g_outb = cotangent.reshape(rows, width)
    g_out = g_outb.astype(F32)
    g_out_all = gather_rows(after(g_outb, z_one_all), n_cp)

    q, k, v, kt, vt = qkv_call(z_one_all, joint, cos, sin, rows, heads)
    mixed, lse = attend_call(me_arr, q, k, vt, rows, heads, n_cp)
    feat = heads * HD
    attn = give(mixed.reshape(n_cp, rows, feat))
    hid, z_two_b, rms_two = hidden_call(me_arr, attn, wo_rel, xb, n_cp)
    g_act = back_act_call(after(g_out_all, z_two_b), packed, rows)
    z_two_all = gather_rows(z_two_b, n_cp, late=(g_act,))

    acts, gus, red_gu = [], [], []
    for h in range(halves):
        z_in = after(z_two_all, part_gu) if h else z_two_all
        act, gu = feed_call(z_in, g_act, w_gu[h], h, rows)
        acts.append(act)
        gus.append(gu)
        if h == 0:
            part_gu = mm(z_two_all, gu, TN).astype(BF)
            red_gu.append(scatter_z(part_gu))
    part = packed_call(gus, w_gu, False, width, rows, "g_two")
    part_gu = mm(z_two_all, after(gus[1], *part), TN).astype(BF)
    red_gu.append(scatter_z(part_gu))
    acc = scatter_first(*part, n_cp, part_gu)
    out_part = packed_call([after(a, acc) for a in acts], [packed], True, width, rows, "out")
    state = scatter_mid(acc, n_cp, *out_part)
    downs = [mm(after(act, *state), g_out_all, TN).astype(BF) for act in acts]
    grad_down = scatter_z(after(jnp.concatenate(downs, 0), red_gu[0]))
    out_acc = scatter_first(*out_part, n_cp, *downs)
    u = scatter_last(state, n_cp, out_acc)

    z_two = hid * rms_two
    g_hidden = g_out + rms_two * (u - z_two * jnp.mean(u * z_two, -1, keepdims=True))
    g_hidb = g_hidden.astype(BF)
    g_heads = back_attn_call(me_arr, g_hidb, wo_rel, n_cp)
    wo_part = grad_wo_call(me_arr, attn, after(g_hidb, g_heads), n_cp)
    out_state = scatter_mid(after(out_acc, g_hidb), n_cp, *wo_part)
    g_mixed = give(after(g_heads, *out_state)).reshape(total, feat)
    back_gu = [give(after(red_gu[0].reshape(n_cp, own, 2 * cut), g_mixed))]
    g_qkv = attend_back_call(me_arr, q, g_mixed, mixed, lse, k, kt, v, cos, sin, rows, heads, n_cp)
    out_sum = scatter_last(after(out_state, g_mixed), n_cp, g_qkv)
    output = hid + out_sum
    wo_acc = scatter_first(*wo_part, n_cp, g_qkv, out_sum)
    w_qkv = joint[:, :depth].reshape(width, qkv_cols)
    part = sum_call([(after(g_qkv, wo_acc), w_qkv)], NT, rows, "g_one")
    wo_state = scatter_mid(wo_acc, n_cp, *part)
    part_qkv = mm(z_one_all, after(g_qkv, red_gu[1], back_gu[0], *wo_state), TN).astype(BF)
    red_qkv = scatter_z(part_qkv)
    back_gu.append(give(after(red_gu[1].reshape(n_cp, own, 2 * cut), part_qkv)))
    w_acc = scatter_first(*part, n_cp, part_qkv)
    wo_sum = scatter_last(wo_state, n_cp, w_acc).astype(BF)
    w_state = scatter_mid(w_acc, n_cp, back_gu[1])

    wo_sum = scatter_z(after(wo_sum, grad_down))
    got = give(red_qkv.reshape(n_cp, own, qkv_cols))
    back_pairs = [(b, a) for a, b in deal(n_dp, n_cp, 0)]
    grad_output = lax.ppermute(wo_sum, ("dp", "cp"), back_pairs).astype(F32)
    w_one = scatter_last(w_state, n_cp, got)
    grad_in = g_hidden + rms_one * (w_one - z_one * jnp.mean(w_one * z_one, -1, keepdims=True))

    grad_g, grad_u, gain_two_sum = finish_feed_call(back_gu, w_gate, w_up, gain_two, per_half, unit)
    grad_q, grad_k, grad_v, gain_one_sum = finish_qkv_call(
        after(got, wo_sum), w_query, w_key, w_value, gain_one, heads, reps
    )

    return (
        output[None],
        grad_in[None],
        gain_one_sum[:, 0],
        grad_q,
        grad_k,
        grad_v,
        grad_output,
        gain_two_sum[:, 0],
        grad_g,
        grad_u,
        grad_down.astype(F32),
    )


def solution(mesh):
    both = ("dp", "cp")
    rows = P("dp", "cp", None)
    mat = P(both, None)
    vec = P(both)
    return jax.shard_map(
        shards,
        mesh=mesh,
        in_specs=(rows, vec, mat, mat, mat, mat, vec, mat, mat, mat, rows),
        out_specs=(rows, rows, vec, mat, mat, mat, mat, vec, mat, mat, mat),
        check_vma=False,
    )
```

```python
import functools
import math

import jax
import jax.numpy as jnp
from jax import lax
from jax.experimental import pallas as pl
from jax.experimental.pallas import tpu as pltpu
from jax.sharding import PartitionSpec as P

H = 16
KVH = 8
HD = 128
EPS = 1e-05
THETA = 1000000.0
SCALE = HD ** (-0.5)
LOG2E = math.log2(math.e)
BF = jnp.bfloat16
F32 = jnp.float32
VMEM_LIMIT = 56 * 1024 * 1024
SHARE = 0.05

NN = (((1,), (0,)), ((), ()))
NT = (((1,), (1,)), ((), ()))
TN = (((0,), (0,)), ((), ()))


def mm(left, right, dims):
    return lax.dot_general(left, right, dims, preferred_element_type=F32)


def offset_of(position, count):
    half = count // 2
    return ((position % half) << 1) | (position // half)


def position_of(offset, count):
    return (offset >> 1) + (offset & 1) * (count // 2)


def after(value, *deps):
    return lax.optimization_barrier((value, *deps))[0]


def swap(value, count, offset):
    return lax.ppermute(value, "cp", [(i, i ^ offset) for i in range(count)])


def gather_rows(part, count, dep=None, late=()):
    half = part.shape[0] // 2
    if count == 8:
        by_x = swap(part, count, 2)
        by_y = swap(part, count, 4)
        if dep is not None:
            by_y = after(by_y, *dep)
        near = jnp.concatenate([part, by_x, by_y], 0)
        near_other = swap(near, count, 1)
        far = [swap(by_y[:half], count, 2), swap(by_x[half:], count, 4)]
        far = jnp.concatenate(lax.optimization_barrier((*far, *late))[:2], 0)
        return jnp.concatenate([near, far, near_other, swap(far, count, 1)], 0)
    inner, bit = part, 2
    while bit < count:
        inner = jnp.concatenate([inner, swap(inner, count, bit)], 0)
        bit *= 2
    return jnp.concatenate([inner, swap(inner, count, 1)], 0)


def plus(left, right):
    return (left.astype(F32) + right.astype(F32)).astype(BF)


def scatter_first(low, high, count, *deps):
    got = swap(high, count, 1)
    return plus(low, after(got, *deps) if deps else got)


def scatter_mid(acc, count, *deps):
    rows = 2 * acc.shape[0] // count
    half = rows // 2
    parts = [acc[i * rows : (i + 1) * rows] for i in range(count // 2)]
    if count == 8:
        own, to_x, to_y, far = parts
        from_x = swap(far[:half], count, 2)
        from_y = swap(far[half:], count, 4)
        if deps:
            from_x, from_y = lax.optimization_barrier((from_x, from_y, *deps))[:2]
        send_x = jnp.concatenate([to_x[:half], plus(to_x[half:], from_y)], 0)
        send_y = jnp.concatenate([plus(to_y[:half], from_x), to_y[half:]], 0)
        return own, send_x, send_y
    bit = count // 2
    while bit > 2:
        keep, give = parts[: len(parts) // 2], parts[len(parts) // 2 :]
        parts = [plus(a, swap(b, count, bit)) for a, b in zip(keep, give)]
        bit //= 2
    return tuple(parts)


def scatter_last(state, count, *deps):
    got = [swap(part, count, offset) for offset, part in zip((2, 4), state[1:])]
    if deps:
        got = lax.optimization_barrier((*got, *deps))[: len(got)]
    total = state[0].astype(F32)
    for part in got:
        total = total + part.astype(F32)
    return total


def deal(count, n_cp, shift):
    return [
        (b, ((b % count + shift) % count) * n_cp + b // count) for b in range(count * n_cp)
    ]


def params(semantics):
    return pltpu.CompilerParams(dimension_semantics=semantics, vmem_limit_bytes=VMEM_LIMIT)


def cost(flops, nbytes, trans=0):
    return pl.CostEstimate(
        flops=int(flops * SHARE), bytes_accessed=int(nbytes * SHARE), transcendentals=int(trans * SHARE)
    )


def turn(value, cos, sin):
    return value * cos + pltpu.roll(value, HD // 2, 1) * sin


def qkv_kernel(z_ref, w_ref, cos_ref, sin_ref, q_ref, k_ref, v_ref, kt_ref, vt_ref, *, heads):
    cos, sin = cos_ref[...], sin_ref[...]
    flat = None
    depth = z_ref.shape[1] // w_ref.shape[0]
    for d in range(w_ref.shape[0]):
        term = mm(z_ref[:, d * depth : (d + 1) * depth], w_ref[d, :depth, :], NN)
        flat = term if flat is None else flat + term
    for h in range(heads):
        at = slice(h * HD, (h + 1) * HD)
        q_ref[:, at] = turn(flat[:, at], cos, sin).astype(BF)
    key = turn(flat[:, heads * HD : (heads + 1) * HD], cos, sin)
    value = flat[:, (heads + 1) * HD :]
    k_ref[...] = key.astype(BF)
    v_ref[...] = value.astype(BF)
    kt_ref[...] = key.T.astype(BF)
    vt_ref[...] = value.T.astype(BF)


def qkv_call(z_one, w_qkv, cos, sin, rows, heads):
    total, width = z_one.shape
    cols = w_qkv.shape[2]
    row = lambda i: (i, 0)
    col = lambda i: (0, i)
    whole = lambda i: (0, 0)
    return pl.pallas_call(
        functools.partial(qkv_kernel, heads=heads),
        grid=(total // rows,),
        in_specs=[
            pl.BlockSpec((rows, width), row),
            pl.BlockSpec(w_qkv.shape, lambda i: (0, 0, 0)),
            pl.BlockSpec((rows, HD), row),
            pl.BlockSpec((rows, HD), row),
        ],
        out_specs=[
            pl.BlockSpec((rows, heads * HD), row),
            pl.BlockSpec((rows, HD), row),
            pl.BlockSpec((rows, HD), row),
            pl.BlockSpec((HD, rows), col),
            pl.BlockSpec((HD, rows), col),
        ],
        out_shape=[
            jax.ShapeDtypeStruct((total, heads * HD), BF),
            jax.ShapeDtypeStruct((total, HD), BF),
            jax.ShapeDtypeStruct((total, HD), BF),
            jax.ShapeDtypeStruct((HD, total), BF),
            jax.ShapeDtypeStruct((HD, total), BF),
        ],
        compiler_params=params(("arbitrary",)),
        cost_estimate=cost(2 * total * width * cols, 2 * (total * width + width * cols)),
        name="qkv",
    )(z_one, w_qkv, cos, sin)


def stack_heads(block, heads):
    if heads == 1:
        return block
    return jnp.concatenate([block[:, h * HD : (h + 1) * HD] for h in range(heads)], 0)


def diagonal_mask(rows, heads):
    key_at = lax.broadcasted_iota(jnp.int32, (rows, rows), 0)
    query_at = lax.broadcasted_iota(jnp.int32, (rows, rows), 1)
    one = key_at <= query_at
    return one if heads == 1 else jnp.concatenate([one] * heads, 1)


def attend_kernel(me_ref, q_ref, k_ref, vt_ref, o_ref, lse_ref, *, heads, rows, count):
    i = pl.program_id(0)
    me = me_ref[0]
    wide = heads * rows
    queries = stack_heads(q_ref[...], heads)

    def step(j, carry, masked):
        top, total, acc = carry
        at = pl.multiple_of(position_of(j ^ me, count) * rows, rows)
        s = mm(k_ref[pl.ds(at, rows), :], queries, NT) * (SCALE * LOG2E)
        if masked:
            s = jnp.where(diagonal_mask(rows, heads), s, -1e30)
        new_top = jnp.maximum(top, jnp.max(s, 0, keepdims=True))
        fade = jnp.exp2(top - new_top)
        p = jnp.exp2(s - new_top)
        total = total * fade + jnp.sum(p, 0, keepdims=True)
        acc = acc * fade + mm(vt_ref[:, pl.ds(at, rows)], p.astype(BF), NN)
        return new_top, total, acc

    carry = (
        jnp.full((1, wide), -1e30, F32),
        jnp.zeros((1, wide), F32),
        jnp.zeros((HD, wide), F32),
    )
    carry = step(i, carry, True)
    top, total, acc = lax.fori_loop(0, i, lambda j, c: step(j, c, False), carry)
    out = (acc / total).T
    for h in range(heads):
        o_ref[:, h * HD : (h + 1) * HD] = out[h * rows : (h + 1) * rows, :].astype(BF)
    lse_ref[0] = top + jnp.log2(total)


def attend_call(me, q, k, vt, rows, heads, count):
    total = q.shape[0]
    slot = lambda i, me_ref: (position_of(i ^ me_ref[0], count), 0)
    true = lambda i, me_ref: (i, 0)
    true3 = lambda i, me_ref: (i, 0, 0)
    whole = lambda i, me_ref: (0, 0)
    return pl.pallas_call(
        functools.partial(attend_kernel, heads=heads, rows=rows, count=count),
        grid_spec=pltpu.PrefetchScalarGridSpec(
            num_scalar_prefetch=1,
            grid=(count,),
            in_specs=[
                pl.BlockSpec((rows, heads * HD), slot),
                pl.BlockSpec((total, HD), whole),
                pl.BlockSpec((HD, total), whole),
            ],
            out_specs=[
                pl.BlockSpec((rows, heads * HD), true),
                pl.BlockSpec((1, 1, heads * rows), true3),
            ],
        ),
        out_shape=[
            jax.ShapeDtypeStruct((total, heads * HD), BF),
            jax.ShapeDtypeStruct((count, 1, heads * rows), F32),
        ],
        compiler_params=params(("arbitrary",)),
        cost_estimate=cost(4 * total * total * heads * HD, 8 * total * HD, heads * total * total // 2),
        name="attend",
    )(me, q, k, vt)


def attend_back_kernel(
    me_ref,
    q_ref,
    g_ref,
    o_ref,
    lse_ref,
    k_ref,
    kt_ref,
    v_ref,
    cos_ref,
    sin_ref,
    out_ref,
    dk_ref,
    dv_ref,
    *,
    heads,
    rows,
    count,
):
    i = pl.program_id(0)
    me = me_ref[0]
    wide = heads * rows

    @pl.when(i == 0)
    def _():
        dk_ref[...] = jnp.zeros_like(dk_ref)
        dv_ref[...] = jnp.zeros_like(dv_ref)

    queries = stack_heads(q_ref[...], heads)
    grads = stack_heads(g_ref[...], heads)
    outs = stack_heads(o_ref[...], heads)
    lse = lse_ref[0]
    mixed = jnp.sum((outs.astype(F32) * grads.astype(F32)).T, 0, keepdims=True)

    def step(j, dqt, masked):
        at = pl.multiple_of(position_of(j ^ me, count) * rows, rows)
        here = pl.ds(at, rows)
        s = mm(k_ref[here, :], queries, NT) * (SCALE * LOG2E)
        p = jnp.exp2(s - lse)
        if masked:
            p = jnp.where(diagonal_mask(rows, heads), p, 0.0)
        gp = mm(v_ref[here, :], grads, NT)
        gs = (p * (gp - mixed) * SCALE).astype(BF)
        dv_ref[here, :] += mm(p.astype(BF), grads, NN)
        dk_ref[here, :] += mm(gs, queries, NN)
        return dqt + mm(kt_ref[:, here], gs, NN)

    dqt = step(i, jnp.zeros((HD, wide), F32), True)
    dqt = lax.fori_loop(0, i, lambda j, c: step(j, c, False), dqt)
    dq = dqt.T
    mine = pl.ds(pl.multiple_of(position_of(i ^ me, count) * rows, rows), rows)
    cos, sin = cos_ref[mine, :], sin_ref[mine, :]
    for h in range(heads):
        one = turn(dq[h * rows : (h + 1) * rows, :], cos, -sin)
        out_ref[mine, h * HD : (h + 1) * HD] = one.astype(BF)

    @pl.when(i == count - 1)
    def _():
        out_ref[:, heads * HD : (heads + 1) * HD] = turn(
            dk_ref[...], cos_ref[...], -sin_ref[...]
        ).astype(BF)
        out_ref[:, (heads + 1) * HD :] = dv_ref[...].astype(BF)


def attend_back_call(me, q, g, o, lse, k, kt, v, cos, sin, rows, heads, count):
    total = q.shape[0]
    slot = lambda i, me_ref: (position_of(i ^ me_ref[0], count), 0)
    true = lambda i, me_ref: (i, 0)
    true3 = lambda i, me_ref: (i, 0, 0)
    whole = lambda i, me_ref: (0, 0)
    cols = (heads + 2) * HD
    return pl.pallas_call(
        functools.partial(attend_back_kernel, heads=heads, rows=rows, count=count),
        grid_spec=pltpu.PrefetchScalarGridSpec(
            num_scalar_prefetch=1,
            grid=(count,),
            in_specs=[
                pl.BlockSpec((rows, heads * HD), slot),
                pl.BlockSpec((rows, heads * HD), true),
                pl.BlockSpec((rows, heads * HD), true),
                pl.BlockSpec((1, 1, heads * rows), true3),
                pl.BlockSpec((total, HD), whole),
                pl.BlockSpec((HD, total), whole),
                pl.BlockSpec((total, HD), whole),
                pl.BlockSpec((total, HD), whole),
                pl.BlockSpec((total, HD), whole),
            ],
            out_specs=pl.BlockSpec((total, cols), whole),
            scratch_shapes=[pltpu.VMEM((total, HD), F32), pltpu.VMEM((total, HD), F32)],
        ),
        out_shape=jax.ShapeDtypeStruct((total, cols), BF),
        compiler_params=params(("arbitrary",)),
        cost_estimate=cost(10 * total * total * heads * HD, 16 * total * HD, heads * total * total // 2),
        name="attend_back",
    )(me, q, g, o, lse, k, kt, v, cos, sin)


def back_act_kernel(g_ref, d_ref, out_ref):
    blocks, _, wide = d_ref.shape
    unit = out_ref.shape[1] // blocks
    for b in range(blocks):
        acc = None
        for c in range(g_ref.shape[1] // wide):
            part = d_ref[b, c * unit : (c + 1) * unit, :]
            term = mm(g_ref[:, c * wide : (c + 1) * wide], part, NT)
            acc = term if acc is None else acc + term
        out_ref[:, b * unit : (b + 1) * unit] = acc


def back_act_call(g_out, packed, rows):
    total, width = g_out.shape
    blocks, depth, wide = packed.shape
    depth = depth // 2
    cols = blocks * depth * wide // width
    return pl.pallas_call(
        back_act_kernel,
        grid=(total // rows,),
        in_specs=[
            pl.BlockSpec((rows, width), lambda i: (i, 0)),
            pl.BlockSpec((blocks, depth, wide), lambda i: (0, 1, 0)),
        ],
        out_specs=pl.BlockSpec((rows, cols), lambda i: (i, 0)),
        out_shape=jax.ShapeDtypeStruct((total, cols), F32),
        compiler_params=params(("arbitrary",)),
        cost_estimate=cost(2 * total * width * cols, 2 * total * width + 2 * cols * width + 4 * total * cols),
        name="back_act",
    )(g_out, packed)


def feed_kernel(z_ref, g_ref, w_ref, act_ref, grads_ref):
    cut = g_ref.shape[1]
    blocks, depth, _ = w_ref.shape
    both = None
    for b in range(blocks):
        term = mm(z_ref[:, b * depth : (b + 1) * depth], w_ref[b], NN)
        both = term if both is None else both + term
    gate, up = both[:, :cut], both[:, cut:]
    back = g_ref[...]
    sig = jax.nn.sigmoid(gate)
    silu = gate * sig
    act_ref[...] = (silu * up).astype(BF)
    grads_ref[:, :cut] = (back * up * (sig * (1.0 + gate * (1.0 - sig)))).astype(BF)
    grads_ref[:, cut:] = (back * silu).astype(BF)


def feed_call(z_two, g_act, w_gu, part, rows):
    total, width = z_two.shape
    cut = w_gu.shape[2] // 2
    blocks = w_gu.shape[0]
    row = lambda i: (i, 0)
    return pl.pallas_call(
        feed_kernel,
        grid=(total // rows,),
        in_specs=[
            pl.BlockSpec((rows, width), row),
            pl.BlockSpec((rows, cut), lambda i: (i, part)),
            pl.BlockSpec((blocks, width // blocks, 2 * cut), lambda i: (0, 0, 0)),
        ],
        out_specs=[pl.BlockSpec((rows, cut), row), pl.BlockSpec((rows, 2 * cut), row)],
        out_shape=[
            jax.ShapeDtypeStruct((total, cut), BF),
            jax.ShapeDtypeStruct((total, 2 * cut), BF),
        ],
        compiler_params=params(("arbitrary",)),
        cost_estimate=cost(4 * total * width * cut, 2 * total * width + 4 * cut * width + 10 * total * cut),
        name="feed",
    )(z_two, g_act, w_gu)


def sum_kernel(*refs, dims):
    *ins, low_ref, high_ref = refs
    acc = None
    for a_ref, b_ref in zip(ins[0::2], ins[1::2]):
        term = mm(a_ref[...], b_ref[...], dims)
        acc = term if acc is None else acc + term
    acc = acc.astype(BF)
    half = pl.num_programs(0) // 2

    @pl.when(pl.program_id(0) < half)
    def _():
        high_ref[...] = acc

    @pl.when(pl.program_id(0) >= half)
    def _():
        low_ref[...] = acc


def sum_call(pairs, dims, rows, name):
    total = pairs[0][0].shape[0]
    cols = pairs[0][1].shape[1 if dims is NN else 0]
    steps = total // rows
    half = steps // 2
    row = lambda i: ((i + half) % steps, 0)
    low = lambda i: (jnp.maximum(i - half, 0), 0)
    high = lambda i: (jnp.minimum(i, half - 1), 0)
    whole = lambda i: (0, 0)
    specs, flat, depth = [], [], 0
    for a, b in pairs:
        specs += [pl.BlockSpec((rows, a.shape[1]), row), pl.BlockSpec(b.shape, whole)]
        flat += [a, b]
        depth += a.shape[1]
    return pl.pallas_call(
        functools.partial(sum_kernel, dims=dims),
        grid=(total // rows,),
        in_specs=specs,
        out_specs=[pl.BlockSpec((rows, cols), low), pl.BlockSpec((rows, cols), high)],
        out_shape=[jax.ShapeDtypeStruct((total // 2, cols), BF)] * 2,
        compiler_params=params(("arbitrary",)),
        cost_estimate=cost(2 * total * cols * depth, 2 * (total * depth + depth * cols + total * cols)),
        name=name,
    )(*flat)


def split_rows(count):
    half = count // 2
    row = lambda i: (i + half) % count
    low = lambda i: jnp.maximum(i - half, 0)
    high = lambda i: jnp.minimum(i, half - 1)
    return half, row, low, high


def hidden_kernel(me_ref, a_ref, w_ref, x_ref, hid_ref, z_ref, rms_ref):
    p = pl.program_id(0)

    @pl.when(p == 0)
    def _():
        hid_ref[...] = x_ref[...].astype(F32)

    hid_ref[...] += mm(a_ref[0], w_ref[...], NN)

    @pl.when(p == pl.num_programs(0) - 1)
    def _():
        hid = hid_ref[...]
        rms = rms_of(hid)
        rms_ref[...] = rms
        z_ref[...] = (hid * rms).astype(BF)


def hidden_call(me, attn, wo, x, count):
    _, rows, feat = attn.shape
    width = wo.shape[1]
    true3 = lambda p, me_ref: (offset_of(p, count) ^ me_ref[0], 0, 0)
    block = lambda p, me_ref: (p, 0)
    whole = lambda p, me_ref: (0, 0)
    return pl.pallas_call(
        hidden_kernel,
        grid_spec=pltpu.PrefetchScalarGridSpec(
            num_scalar_prefetch=1,
            grid=(count,),
            in_specs=[
                pl.BlockSpec((1, rows, feat), true3),
                pl.BlockSpec((feat, width), block),
                pl.BlockSpec((rows, width), whole),
            ],
            out_specs=[
                pl.BlockSpec((rows, width), whole),
                pl.BlockSpec((rows, width), whole),
                pl.BlockSpec((rows, 1), whole),
            ],
        ),
        out_shape=[
            jax.ShapeDtypeStruct((rows, width), F32),
            jax.ShapeDtypeStruct((rows, width), BF),
            jax.ShapeDtypeStruct((rows, 1), F32),
        ],
        compiler_params=params(("arbitrary",)),
        cost_estimate=cost(2 * rows * feat * count * width, 2 * feat * count * width + 10 * rows * width),
        name="hidden",
    )(me, attn, wo, x)


def back_attn_kernel(me_ref, g_ref, w_ref, out_ref):
    out_ref[0] = mm(g_ref[...], w_ref[...], NT).astype(BF)


def back_attn_call(me, g, wo, count):
    rows, width = g.shape
    feat = wo.shape[0] // count
    true3 = lambda p, me_ref: (offset_of(p, count) ^ me_ref[0], 0, 0)
    block = lambda p, me_ref: (p, 0)
    whole = lambda p, me_ref: (0, 0)
    return pl.pallas_call(
        back_attn_kernel,
        grid_spec=pltpu.PrefetchScalarGridSpec(
            num_scalar_prefetch=1,
            grid=(count,),
            in_specs=[pl.BlockSpec((rows, width), whole), pl.BlockSpec((feat, width), block)],
            out_specs=pl.BlockSpec((1, rows, feat), true3),
        ),
        out_shape=jax.ShapeDtypeStruct((count, rows, feat), BF),
        compiler_params=params(("arbitrary",)),
        cost_estimate=cost(2 * rows * feat * count * width, 2 * feat * count * width + 4 * rows * width),
        name="back_attn",
    )(me, g, wo)


def grad_wo_kernel(me_ref, a_ref, g_ref, low_ref, high_ref):
    out = mm(a_ref[0], g_ref[...], TN).astype(BF)
    half = pl.num_programs(0) // 2

    @pl.when(pl.program_id(0) < half)
    def _():
        high_ref[...] = out

    @pl.when(pl.program_id(0) >= half)
    def _():
        low_ref[...] = out


def grad_wo_call(me, attn, g, count):
    _, rows, feat = attn.shape
    width = g.shape[1]
    half, row, low, high = split_rows(count)
    return pl.pallas_call(
        grad_wo_kernel,
        grid_spec=pltpu.PrefetchScalarGridSpec(
            num_scalar_prefetch=1,
            grid=(count,),
            in_specs=[
                pl.BlockSpec(
                    (1, rows, feat), lambda p, me_ref: (offset_of(row(p), count) ^ me_ref[0], 0, 0)
                ),
                pl.BlockSpec((rows, width), lambda p, me_ref: (0, 0)),
            ],
            out_specs=[
                pl.BlockSpec((feat, width), lambda p, me_ref: (low(p), 0)),
                pl.BlockSpec((feat, width), lambda p, me_ref: (high(p), 0)),
            ],
        ),
        out_shape=[jax.ShapeDtypeStruct((half * feat, width), BF)] * 2,
        compiler_params=params(("arbitrary",)),
        cost_estimate=cost(2 * rows * feat * count * width, 2 * feat * count * width + 4 * rows * width),
        name="grad_wo",
    )(me, attn, g)


def packed_kernel(*refs, down):
    *ins, low_ref, high_ref = refs
    lefts, weights = ins[:2], ins[2:]
    blocks, depth, wide = weights[0].shape
    pieces = []
    if down:
        per = blocks // 2
        unit = lefts[0].shape[1] // per
        for c in range(depth // unit):
            acc = None
            for b in range(blocks):
                left = lefts[b // per][:, (b % per) * unit : (b % per + 1) * unit]
                term = mm(left, weights[0][b, c * unit : (c + 1) * unit, :], NN)
                acc = term if acc is None else acc + term
            pieces.append(acc.astype(BF))
    else:
        for b in range(blocks):
            acc = mm(lefts[0][...], weights[0][b], NT) + mm(lefts[1][...], weights[1][b], NT)
            pieces.append(acc.astype(BF))
    out = jnp.concatenate(pieces, 1)
    half = pl.num_programs(0) // 2

    @pl.when(pl.program_id(0) < half)
    def _():
        high_ref[...] = out

    @pl.when(pl.program_id(0) >= half)
    def _():
        low_ref[...] = out


def packed_call(lefts, weights, down, width, rows, name):
    total, cols = lefts[0].shape
    blocks, _, wide = weights[0].shape
    depth = width // blocks
    half, row, low, high = split_rows(total // rows)
    left = pl.BlockSpec((rows, cols), lambda i: (row(i), 0))
    weight = pl.BlockSpec((blocks, depth, wide), lambda i: (0, 1 if down else 0, 0))
    return pl.pallas_call(
        functools.partial(packed_kernel, down=down),
        grid=(total // rows,),
        in_specs=[left, left] + [weight] * len(weights),
        out_specs=[
            pl.BlockSpec((rows, width), lambda i: (low(i), 0)),
            pl.BlockSpec((rows, width), lambda i: (high(i), 0)),
        ],
        out_shape=[jax.ShapeDtypeStruct((total // 2, width), BF)] * 2,
        compiler_params=params(("arbitrary",)),
        cost_estimate=cost(4 * total * cols * width, 2 * total * (2 * cols + width) + 4 * cols * width),
        name=name,
    )(*lefts, *weights)


def finish_feed_kernel(*refs, halves, per_half, unit, count):
    gots, (wg_ref, wu_ref, gain_ref, g_ref, u_ref, sum_ref) = refs[:halves], refs[halves:]
    gain = gain_ref[...]
    total = None
    for h, got_ref in enumerate(gots):
        for kind, (w_ref, out_ref) in enumerate(((wg_ref, g_ref), (wu_ref, u_ref))):
            for i in range(per_half):
                frm = (kind * per_half + i) * unit
                for t in range(count):
                    at = ((h * per_half + i) * count + t) * unit
                    raw = got_ref[t, :, frm : frm + unit].astype(F32)
                    out_ref[:, at : at + unit] = raw * gain
                    term = raw * w_ref[:, at : at + unit].astype(F32)
                    total = term if total is None else total + term
    sum_ref[...] = jnp.sum(total, 1, keepdims=True)


def finish_feed_call(gots, w_gate, w_up, gain, per_half, unit):
    own, hidden = w_gate.shape
    return pl.pallas_call(
        functools.partial(
            finish_feed_kernel,
            halves=len(gots),
            per_half=per_half,
            unit=unit,
            count=gots[0].shape[0],
        ),
        out_shape=[
            jax.ShapeDtypeStruct((own, hidden), F32),
            jax.ShapeDtypeStruct((own, hidden), F32),
            jax.ShapeDtypeStruct((own, 1), F32),
        ],
        compiler_params=pltpu.CompilerParams(vmem_limit_bytes=VMEM_LIMIT),
        cost_estimate=cost(8 * own * hidden, 16 * own * hidden),
        name="finish_feed",
    )(*gots, w_gate, w_up, gain)


def finish_qkv_kernel(
    got_ref, wq_ref, wk_ref, wv_ref, gain_ref, q_ref, k_ref, v_ref, sum_ref, *, heads, reps
):
    gain = gain_ref[...]
    total = None
    feat = heads * HD
    for t in range(got_ref.shape[0]):
        raw = got_ref[t, :, :feat].astype(F32)
        at = slice(t * feat, (t + 1) * feat)
        q_ref[:, at] = raw * gain
        term = jnp.sum(raw * wq_ref[:, at].astype(F32), 1, keepdims=True)
        total = term if total is None else total + term
    for kind, (w_ref, out_ref) in enumerate(((wk_ref, k_ref), (wv_ref, v_ref))):
        frm = slice(feat + kind * HD, feat + (kind + 1) * HD)
        for t in range(got_ref.shape[0] // reps):
            raw = got_ref[t * reps, :, frm].astype(F32)
            for r in range(1, reps):
                raw = raw + got_ref[t * reps + r, :, frm].astype(F32)
            at = slice(t * HD, (t + 1) * HD)
            out_ref[:, at] = raw * gain
            total = total + jnp.sum(raw * w_ref[:, at].astype(F32), 1, keepdims=True)
    sum_ref[...] = total


def finish_qkv_call(got, w_query, w_key, w_value, gain, heads, reps):
    own = w_query.shape[0]
    like = lambda w: jax.ShapeDtypeStruct(w.shape, F32)
    return pl.pallas_call(
        functools.partial(finish_qkv_kernel, heads=heads, reps=reps),
        out_shape=[like(w_query), like(w_key), like(w_value), jax.ShapeDtypeStruct((own, 1), F32)],
        compiler_params=pltpu.CompilerParams(vmem_limit_bytes=VMEM_LIMIT),
        cost_estimate=cost(8 * own * w_query.shape[1], 16 * own * w_query.shape[1]),
        name="finish_qkv",
    )(got, w_query, w_key, w_value, gain)


def rms_of(values):
    return lax.rsqrt(jnp.mean(values * values, -1, keepdims=True) + EPS)


def shards(
    inputs, attn_gain, w_query, w_key, w_value, w_output, ffn_gain, w_gate, w_up, w_down, cotangent
):
    _, rows, width = inputs.shape
    n_cp = lax.axis_size("cp")
    n_dp = lax.axis_size("dp")
    me = lax.axis_index("cp")
    heads = H // n_cp
    reps = n_cp // KVH
    total = rows * n_cp
    own = w_query.shape[0]
    hidden = w_gate.shape[1]
    unit = hidden // (n_dp * n_cp)
    halves = 2
    per_half = n_dp // halves
    me_arr = jnp.reshape(me, (1,)).astype(jnp.int32)
    gain_one = attn_gain.astype(F32)[:, None]
    gain_two = ffn_gain.astype(F32)[:, None]

    def gather_z(value):
        return lax.all_gather(value, "dp", axis=0, tiled=True)

    def scatter_z(value):
        return lax.psum_scatter(value, "dp", scatter_dimension=0, tiled=True)

    def give(value):
        return lax.all_to_all(value, "cp", 0, 0)

    scaled_q = (w_query.astype(F32) * gain_one).astype(BF).reshape(own, n_cp, heads * HD)
    scaled_k = (w_key.astype(F32) * gain_one).astype(BF).reshape(own, KVH, 1, HD)
    scaled_v = (w_value.astype(F32) * gain_one).astype(BF).reshape(own, KVH, 1, HD)
    spread = lambda v: jnp.broadcast_to(v, (own, KVH, reps, HD)).reshape(own, n_cp, HD)
    qkv_own = jnp.concatenate([scaled_q, spread(scaled_k), spread(scaled_v)], 2).transpose(1, 0, 2)
    qkv_cols = (heads + 2) * HD
    qkv_rows = give(qkv_own).reshape(n_cp * own, qkv_cols)
    wo_own = lax.ppermute(w_output, ("dp", "cp"), deal(n_dp, n_cp, 0))
    depth = n_cp * own
    if own * width % qkv_cols == 0:
        joint = jnp.concatenate([qkv_rows, wo_own.reshape(-1, qkv_cols)], 0)
        joint = gather_z(joint).reshape(n_dp, -1, qkv_cols)
        wo_rows = joint[:, depth:].reshape(n_dp * own, width)
    else:
        joint = gather_z(qkv_rows).reshape(n_dp, -1, qkv_cols)
        wo_rows = gather_z(wo_own)

    scaled_g = (w_gate.astype(F32) * gain_two).astype(BF).reshape(own, n_dp, n_cp, unit)
    scaled_u = (w_up.astype(F32) * gain_two).astype(BF).reshape(own, n_dp, n_cp, unit)
    cut = per_half * unit
    w_gu, last, given = [], qkv_rows, []
    for h in range(halves):
        at = slice(h * per_half, (h + 1) * per_half)
        both = jnp.concatenate([scaled_g[:, at], scaled_u[:, at]], 1)
        both = both.transpose(2, 0, 1, 3).reshape(n_cp, own, 2 * cut)
        last = give(after(both, last))
        given.append(last)
        block = last.reshape(depth, 2 * cut)
        if h == 0:
            columns = [w_down[:, c : c + 2 * cut] for c in range(0, width, 2 * cut)]
            block = jnp.concatenate([block, *columns], 0)
        w_gu.append(gather_z(block).reshape(n_dp, -1, 2 * cut))
    packed = w_gu[0]

    shard_at = jnp.array([offset_of(p, n_cp) for p in range(n_cp)], jnp.int32) ^ me
    positions = (shard_at[:, None] * rows + jnp.arange(rows, dtype=jnp.int32)[None, :]).reshape(-1)
    half_dim = HD // 2
    inv_freq = THETA ** (-(jnp.arange(half_dim, dtype=F32) * 2.0 / HD))
    angles = positions.astype(F32)[:, None] * inv_freq[None, :]
    cos_half, sin_half = jnp.cos(angles), jnp.sin(angles)
    cos = jnp.concatenate([cos_half, cos_half], -1)
    sin = jnp.concatenate([-sin_half, sin_half], -1)

    xb = inputs.reshape(rows, width)
    x = xb.astype(F32)
    rms_one = rms_of(x)
    z_one = x * rms_one
    z_one_all = gather_rows(z_one.astype(BF), n_cp, [cos, sin] + given)
    wo_rel = gather_rows(wo_rows, n_cp)
    g_outb = cotangent.reshape(rows, width)
    g_out = g_outb.astype(F32)
    g_out_all = gather_rows(after(g_outb, z_one_all), n_cp)

    q, k, v, kt, vt = qkv_call(z_one_all, joint, cos, sin, rows, heads)
    mixed, lse = attend_call(me_arr, q, k, vt, rows, heads, n_cp)
    feat = heads * HD
    attn = give(mixed.reshape(n_cp, rows, feat))
    hid, z_two_b, rms_two = hidden_call(me_arr, attn, wo_rel, xb, n_cp)
    g_act = back_act_call(after(g_out_all, z_two_b), packed, rows)
    z_two_all = gather_rows(z_two_b, n_cp, late=(g_act,))

    acts, gus, red_gu = [], [], []
    for h in range(halves):
        z_in = after(z_two_all, part_gu) if h else z_two_all
        act, gu = feed_call(z_in, g_act, w_gu[h], h, rows)
        acts.append(act)
        gus.append(gu)
        if h == 0:
            part_gu = mm(z_two_all, gu, TN).astype(BF)
            red_gu.append(scatter_z(part_gu))
    part = packed_call(gus, w_gu, False, width, rows, "g_two")
    part_gu = mm(z_two_all, after(gus[1], *part), TN).astype(BF)
    red_gu.append(scatter_z(part_gu))
    acc = scatter_first(*part, n_cp, part_gu)
    out_part = packed_call([after(a, acc) for a in acts], [packed], True, width, rows, "out")
    state = scatter_mid(acc, n_cp, *out_part)
    downs = [mm(after(act, *state), g_out_all, TN).astype(BF) for act in acts]
    grad_down = scatter_z(after(jnp.concatenate(downs, 0), red_gu[0]))
    out_acc = scatter_first(*out_part, n_cp, *downs)
    u = scatter_last(state, n_cp, out_acc)

    z_two = hid * rms_two
    g_hidden = g_out + rms_two * (u - z_two * jnp.mean(u * z_two, -1, keepdims=True))
    g_hidb = g_hidden.astype(BF)
    g_heads = back_attn_call(me_arr, g_hidb, wo_rel, n_cp)
    wo_part = grad_wo_call(me_arr, attn, after(g_hidb, g_heads), n_cp)
    out_state = scatter_mid(after(out_acc, g_hidb), n_cp, *wo_part)
    g_mixed = give(after(g_heads, *out_state)).reshape(total, feat)
    back_gu = [give(after(red_gu[0].reshape(n_cp, own, 2 * cut), g_mixed))]
    g_qkv = attend_back_call(me_arr, q, g_mixed, mixed, lse, k, kt, v, cos, sin, rows, heads, n_cp)
    out_sum = scatter_last(after(out_state, g_mixed), n_cp, g_qkv)
    output = hid + out_sum
    wo_acc = scatter_first(*wo_part, n_cp, g_qkv, out_sum)
    w_qkv = joint[:, :depth].reshape(width, qkv_cols)
    part = sum_call([(after(g_qkv, wo_acc), w_qkv)], NT, rows, "g_one")
    wo_state = scatter_mid(wo_acc, n_cp, *part)
    part_qkv = mm(z_one_all, after(g_qkv, red_gu[1], back_gu[0], *wo_state), TN).astype(BF)
    red_qkv = scatter_z(part_qkv)
    back_gu.append(give(after(red_gu[1].reshape(n_cp, own, 2 * cut), part_qkv)))
    w_acc = scatter_first(*part, n_cp, part_qkv)
    wo_sum = scatter_last(wo_state, n_cp, w_acc).astype(BF)
    w_state = scatter_mid(w_acc, n_cp, back_gu[1])

    wo_sum = scatter_z(after(wo_sum, grad_down))
    got = give(red_qkv.reshape(n_cp, own, qkv_cols))
    back_pairs = [(b, a) for a, b in deal(n_dp, n_cp, 0)]
    grad_output = lax.ppermute(wo_sum, ("dp", "cp"), back_pairs).astype(F32)
    w_one = scatter_last(w_state, n_cp)
    grad_in = g_hidden + rms_one * (w_one - z_one * jnp.mean(w_one * z_one, -1, keepdims=True))

    grad_g, grad_u, gain_two_sum = finish_feed_call(back_gu, w_gate, w_up, gain_two, per_half, unit)
    grad_q, grad_k, grad_v, gain_one_sum = finish_qkv_call(
        after(got, wo_sum), w_query, w_key, w_value, gain_one, heads, reps
    )

    return (
        output[None],
        grad_in[None],
        gain_one_sum[:, 0],
        grad_q,
        grad_k,
        grad_v,
        grad_output,
        gain_two_sum[:, 0],
        grad_g,
        grad_u,
        grad_down.astype(F32),
    )


def solution(mesh):
    both = ("dp", "cp")
    rows = P("dp", "cp", None)
    mat = P(both, None)
    vec = P(both)
    return jax.shard_map(
        shards,
        mesh=mesh,
        in_specs=(rows, vec, mat, mat, mat, mat, vec, mat, mat, mat, rows),
        out_specs=(rows, rows, vec, mat, mat, mat, mat, vec, mat, mat, mat),
        check_vma=False,
    )
```
